32 devices in a mesh: dp: 8 (over y, x, core), feat: 4 (over z).
Axes of the slice: x: 2, y: 2, z: 4, core: 2. Of those that a mesh axis runs over, the one named last changes fastest.
Arguments:
- bins: int32 [4096, 128], P('dp', 'feat'), may hold values from 0 to 47
- fractions: float32 [4096, 128], P('dp', 'feat'), may hold values from 0 to 1
- missing: int32 [4096, 128], P('dp', 'feat'), may hold values 0 or 1
- bin_table: float32 [128, 48, 16], P('feat'), may hold values from -0.875 to 0.875
- bin_bias: float32 [128, 16], P('feat'), may hold values from -3 to 3
- miss_vector: float32 [128, 16], P('feat'), may hold values from -6 to 6
- scale_in: float32 [32, 2048], replicated, may hold values from -4 to 4
- weight: float32 [2048, 512], replicated, may hold values from -0.125 to 0.125
- scale_out: float32 [32, 512], replicated, may hold values from 0.25 to 1.75
- bias_out: float32 [32, 512], replicated, may hold values from -3 to 3
- cotangent: float32 [4096, 32, 512], P(('dp', 'feat')), may hold values from -6 to 6
Outputs:
- hidden: float32 [4096, 32, 512], P(('dp', 'feat'))
- grad_fractions: float32 [4096, 128], P('dp', 'feat')
- grad_table: float32 [128, 48, 16], P('feat')
- grad_bin_bias: float32 [128, 16], P('feat')
- grad_miss: float32 [128, 16], P('feat')
- grad_scale_in: float32 [32, 2048], P(None, 'feat')
- grad_weight: float32 [2048, 512], P('feat')
- grad_scale_out: float32 [32, 512], P(None, 'feat')
- grad_bias_out: float32 [32, 512], P(None, 'feat')
The draws below stay inside these ranges and needn't reach their ends.
All inputs are finite; a program needn't handle non-finite values. No bound on the sum of `missing` on one device may be relied on, other than what follows from the above.
Results may differ from the reference program's by a relative error of at most 0.0003.
Values sent between devices are 32-bit elements; how exact they have to be, the bound alone decides.
A program may use at most 128 MiB of HBM per device.

```python
import jax
import jax.numpy as jnp
from jax import lax

F = 128
B = 48
E = 16
K = 32
H = 512
DIN = 2048
OBJECTS = 4096


def touch_ends(drawn, key, least, high):
    longest = drawn.shape.index(max(drawn.shape))
    spots = []
    for shift in (0, 1):
        where = [jax.random.randint(jax.random.fold_in(key, axis), (), 0, length) for axis, length in enumerate(drawn.shape)]
        where[longest] = (where[longest] + shift) % drawn.shape[longest]
        spots.append(tuple(where))
    return drawn.at[spots[0]].set(least).at[spots[1]].set(high)


def block_scale(rng, shape, split, low, high):
    factor_of, own = 1.0, jax.random.fold_in(rng, 6)
    for dim, parts in split:
        draws = jnp.exp(jax.random.uniform(jax.random.fold_in(own, dim), (parts,), jnp.float32, low / len(split), high / len(split)))
        factor_of = factor_of * jnp.repeat(draws, shape[dim] // parts).reshape([-1 if axis == dim else 1 for axis in range(len(shape))])
    return factor_of


def bell_draw(rng, dims, scale, bound, split=(), held_as=jnp.bfloat16):
    gain = block_scale(rng, dims, split, -0.22, 0.18) if split else 1.0
    result = jax.random.normal(rng, dims, jnp.float32) * scale * gain
    return jnp.minimum(jnp.maximum(result, -bound), bound).astype(held_as)


def setup_inputs(seed: int = 0) -> dict:
    arg_keys = jax.random.split(jax.random.key(seed), 12)
    bins = touch_ends(jax.random.randint(arg_keys[0], (OBJECTS, F), 0, B), jax.random.fold_in(arg_keys[0], 1), 0, B - 1).astype(jnp.int32)
    fractions = jnp.clip(1.0 * jax.random.uniform(arg_keys[1], (OBJECTS, F), jnp.float32) ** block_scale(arg_keys[1], (OBJECTS, F), ((0, 8), (1, 4)), -0.2, 0.2), 0.0, 1.0)
    missing = touch_ends((jax.random.randint(arg_keys[2], (OBJECTS, F), 0, 8) < 1).astype(jnp.int32), jax.random.fold_in(arg_keys[2], 1), 0, 1)
    bin_table = bell_draw(arg_keys[3], (F, B, E), B ** -0.5, 0.875, ((0, 4),), jnp.float32)
    bin_bias = bell_draw(arg_keys[4], (F, E), 0.5, 3.0, ((0, 4),), jnp.float32)
    miss_vector = bell_draw(arg_keys[5], (F, E), 1.0, 6.0, ((0, 4),), jnp.float32)
    scale_in = bell_draw(arg_keys[6], (K, DIN), 1.0, 4.0, (), jnp.float32)
    weight = bell_draw(arg_keys[7], (DIN, H), DIN ** -0.5, 0.125, (), jnp.float32)
    scale_out = jnp.clip(1.0 + 0.15 * jax.random.normal(arg_keys[8], (K, H), jnp.float32), 0.25, 1.75)
    bias_out = bell_draw(arg_keys[9], (K, H), 0.5, 3.0, (), jnp.float32)
    cotangent = bell_draw(arg_keys[10], (OBJECTS, K, H), 1.0, 6.0, ((0, 32),), jnp.float32)
    return dict(bins=bins, fractions=fractions, missing=missing, bin_table=bin_table, bin_bias=bin_bias, miss_vector=miss_vector, scale_in=scale_in, weight=weight, scale_out=scale_out, bias_out=bias_out, cotangent=cotangent)


@jax.custom_vjp
def low(v):
    return lax.optimization_barrier(v.astype(jnp.bfloat16)).astype(jnp.float32)

@jax.custom_vjp
def low_back(v):
    return v

def low_keep(v):
    return (low(v), None)

def low_pass(kept, grad):
    return (grad,)

def back_keep(v):
    return (v, None)

def back_low(kept, grad):
    return (low(grad),)
low.defvjp(low_keep, low_pass)
low_back.defvjp(back_keep, back_low)

def encode(bins, fractions):
    levels = lax.broadcasted_iota(jnp.int32, (1, 1, B), 2)
    chosen = bins[:, :, None]
    return jnp.where(levels < chosen, jnp.float32(1.0), jnp.where(levels == chosen, fractions[:, :, None], jnp.float32(0.0)))

def reference(bins, fractions, missing, bin_table, bin_bias, miss_vector, scale_in, weight, scale_out, bias_out, cotangent):
    absent = (missing == 1)[:, :, None]

    def forward(fractions, bin_table, bin_bias, miss_vector, scale_in, weight, scale_out, bias_out):
        encoding = encode(bins, fractions)
        summed = jnp.einsum('nfb,fbe->nfe', encoding, bin_table, precision=lax.Precision.HIGHEST)
        embedded = jnp.where(absent, miss_vector[None], summed + bin_bias[None]).reshape(OBJECTS, DIN)

        def member(params):
            scale_k, out_k, bias_k = params
            pre = jnp.dot(embedded * scale_k[None], weight, precision=lax.Precision.HIGHEST)
            return jax.nn.gelu(out_k[None] * pre + bias_k[None])
        stacked = lax.map(jax.checkpoint(member), (scale_in, scale_out, bias_out))
        return jnp.transpose(stacked, (1, 0, 2))
    hidden, pullback = jax.vjp(forward, fractions, bin_table, bin_bias, miss_vector, scale_in, weight, scale_out, bias_out)
    grads = pullback(cotangent)
    return (hidden, grads[0], grads[1], grads[2], grads[3], grads[4], grads[5], grads[6], grads[7])
```

```python
import functools

import jax
import jax.numpy as jnp
from jax import lax
from jax.experimental import pallas as pl
from jax.experimental.pallas import tpu as pltpu
from jax.sharding import PartitionSpec as P

F32, BF16, F8 = jnp.float32, jnp.bfloat16, jnp.float8_e4m3fn
VMEM_LIMIT = 60 << 20
TILE = 16
CHUNK = 256
TOP = 224.0
LO = 256.0
GELU_A = 0.7978845608028654
GELU_B = GELU_A * 0.044715


def dot(a, b):
    return jnp.dot(a, b, preferred_element_type=F32)


def dot_nt(a, b):
    return lax.dot_general(a, b, (((1,), (1,)), ((), ())), preferred_element_type=F32)


def split3(x):
    hi = x.astype(BF16)
    return hi, x.astype(F8), ((x - hi.astype(F32)) * LO).astype(F8)


def split2(x):
    hi = x.astype(BF16)
    return hi, (x - hi.astype(F32)).astype(BF16)


def product(a, b, mul):
    ah, a8, al = a
    bh, b8, bl = b
    return mul(ah, bh) + (mul(a8, bl) + mul(al, b8)) * (1.0 / LO)


def encode_pair(b_ref, f_ref, m_ref, first):
    level = lax.broadcasted_iota(jnp.int32, (48, 128), 0).astype(F32)
    row = lax.broadcasted_iota(jnp.int32, (16, 128), 0)
    parts = []
    for f in (first, first + 1):
        b, fr, m = b_ref[pl.ds(f, 1), :], f_ref[pl.ds(f, 1), :], m_ref[pl.ds(f, 1), :]
        here = 1.0 - m
        parts.append(jnp.clip((b - level) + fr, 0.0, 1.0) * here)
        parts.append(jnp.where(row == 0, here, jnp.where(row == 1, m, 0.0)))
    return jnp.concatenate(parts, axis=0)


def table_pair(t_ref, p):
    blk = t_ref[pl.ds(pl.multiple_of(p * 16, 16), 16), :]
    lane = lax.broadcasted_iota(jnp.int32, (16, 128), 1)
    zero = jnp.zeros_like(blk)
    return jnp.concatenate([jnp.where(lane < 64, blk, zero), jnp.where(lane < 64, zero, blk)], axis=0)


def embed_kernel(b_ref, f_ref, m_ref, t_ref, w_ref, s_ref, sc_ref, e_ref, wh_ref, w8_ref, wl_ref, et):
    def pair(p, c):
        lh, ll = split2(table_pair(t_ref, p))
        eh, el = split2(encode_pair(b_ref, f_ref, m_ref, 2 * p))
        both = dot(jnp.concatenate([lh, ll], axis=0), eh)
        et[pl.ds(pl.multiple_of(p * 32, 32), 32), :] = both[:32] + both[32:] + dot(lh, el)
        return c

    lax.fori_loop(0, t_ref.shape[0] // 16, pair, 0)
    for j in range(et.shape[0] // 128):
        e_ref[:, j * 128:(j + 1) * 128] = et[j * 128:(j + 1) * 128, :].T
    wh_ref[...], w8_ref[...], wl_ref[...] = split3(w_ref[...] * sc_ref[1])


def forward_kernel(e_ref, s_ref, wh_ref, w8_ref, wl_ref, so_ref, bo_ref, ct_ref, sc_ref,
                   hid_ref, gh_ref, g8_ref, gl_ref, th_ref, t8_ref, tl_ref, gs_ref, gb_ref,
                   s1, so1, so2, xh0, x80, xl0, xh1, x81, xl1, pre0, pre1):
    i = pl.program_id(0)
    tiles = pl.num_programs(0) - 1
    members, width_out = so_ref.shape
    rows = TILE * members
    x = ((xh0, x80, xl0), (xh1, x81, xl1))
    pre = (pre0, pre1)
    w = (wh_ref, w8_ref, wl_ref)

    def prepare(tile, to):
        for n in range(TILE):
            v = s1[...] * e_ref[pl.ds(tile * TILE + n, 1), :]
            r = slice(n * members, (n + 1) * members)
            to[0][r, :], to[1][r, :], to[2][r, :] = split3(v)

    def multiply(a, to):
        to[...] = product([r[...] for r in a], [r[...] for r in w], dot)

    def finish(p):
        for h0 in range(0, width_out, 128):
            hs = slice(h0, h0 + 128)
            sa, sb, bo = so1[:, hs], so2[:, hs], bo_ref[:, hs]
            gs, gb = gs_ref[:, hs], gb_ref[:, hs]
            for n in range(TILE):
                r = slice(n * members, (n + 1) * members)
                q = p[r, hs]
                v = q * sa + bo
                v2 = v * v
                half = 0.5 + 0.5 * jnp.tanh(v * (GELU_B * v2 + GELU_A))
                hid = v * half
                hid_ref[n, :, hs] = hid
                g = half + hid * (1.0 - half) * ((6.0 * GELU_B) * v2 + 2.0 * GELU_A)
                ga = ct_ref[n, :, hs] * g
                gs = gs + ga * q
                gb = gb + ga
                gh_ref[r, hs], g8_ref[r, hs], gl_ref[r, hs] = split3(ga * sb)
            gs_ref[:, hs], gb_ref[:, hs] = gs, gb
        th_ref[...] = gh_ref[...].T
        t8_ref[...] = g8_ref[...].T
        tl_ref[...] = gl_ref[...].T

    @pl.when(i == 0)
    def _():
        s1[...] = s_ref[...] * sc_ref[0]
        so1[...] = so_ref[...] * sc_ref[3]
        so2[...] = so_ref[...] * sc_ref[2]
        gs_ref[...] = jnp.zeros_like(gs_ref)
        gb_ref[...] = jnp.zeros_like(gb_ref)
        prepare(0, x[0])
        multiply(x[0], pre[0])
        prepare(1, x[1])

    for par in (0, 1):
        @pl.when((i > 0) & (i < tiles) & (i % 2 == par))
        def _():
            multiply(x[par], pre[par])
            prepare(jnp.minimum(i + 1, tiles - 1), x[1 - par])
            finish(pre[1 - par])

    @pl.when(i == tiles)
    def _():
        finish(pre[1])
        gs_ref[...] = gs_ref[...] * sc_ref[4]


def backward_kernel(e_ref, s_ref, wh_ref, w8_ref, wl_ref, gh_ref, g8_ref, gl_ref, th_ref, t8_ref, tl_ref,
                    sc_ref, gw_ref, ge_ref, gsin_ref, s1, s2, xh0, x80, xl0, xh1, x81, xl1, g0, g1):
    members, width_in = s_ref.shape
    rows = gh_ref.shape[0]
    count = e_ref.shape[0]
    chunks = width_in // CHUNK
    x = ((xh0, x80, xl0), (xh1, x81, xl1))
    gt = (th_ref, t8_ref, tl_ref)
    s1[...] = s_ref[...] * sc_ref[0]
    s2[...] = s_ref[...] * sc_ref[6]

    def cols(c):
        return pl.ds(pl.multiple_of(c * CHUNK, CHUNK), CHUNK)

    def prepare(c, to):
        v = (e_ref[:, cols(c)][:, None, :] * s1[:, cols(c)][None]).reshape(rows, CHUNK)
        to[0][...], to[1][...], to[2][...] = split3(v)

    prepare(0, x[0])

    def weights(j, carry):
        for par in (0, 1):
            c = 2 * j + par
            r = product([t[...] for t in gt], [t[...] for t in x[par]], dot)
            gw_ref[cols(c), :] = r.T * sc_ref[5]
            prepare(jnp.minimum(c + 1, chunks - 1), x[1 - par])
        return carry

    lax.fori_loop(0, chunks // 2, weights, 0)

    gsin_ref[...] = jnp.zeros_like(gsin_ref)
    g1[...] = jnp.zeros_like(g1)
    step = g0.shape[0]
    objs = step // members
    parts = rows // step

    def finish(c, t, g):
        g3 = g[...].reshape(objs, members, CHUNK)
        ns = slice(t * objs, (t + 1) * objs)
        ge_ref[ns, cols(c)] = jnp.sum(g3 * s2[:, cols(c)][None], axis=1)
        gsin_ref[:, cols(c)] += jnp.sum(g3 * e_ref[ns, cols(c)][:, None, :], axis=0)

    def inputs(c, carry):
        wc = [t[cols(c), :] for t in (wh_ref, w8_ref, wl_ref)]
        for t in range(parts):
            to, fro = (g0, g1) if t % 2 == 0 else (g1, g0)
            rs = slice(t * step, (t + 1) * step)
            to[...] = product([r[rs, :] for r in (gh_ref, g8_ref, gl_ref)], wc, dot_nt)
            if t == 0:
                finish(jnp.maximum(c - 1, 0), parts - 1, fro)
            else:
                finish(c, t - 1, fro)
        return carry

    lax.fori_loop(0, chunks, inputs, 0)
    finish(chunks - 1, parts - 1, g1)
    gsin_ref[...] = gsin_ref[...] * sc_ref[7]


def table_kernel(b_ref, f_ref, m_ref, t_ref, ge_ref, gt_ref, gf_ref, et):
    for j in range(et.shape[0] // 128):
        et[j * 128:(j + 1) * 128, :] = ge_ref[:, j * 128:(j + 1) * 128].T

    def pair(p, c):
        lh, ll = split2(table_pair(t_ref, p))
        enc = encode_pair(b_ref, f_ref, m_ref, 2 * p)
        g = et[pl.ds(pl.multiple_of(p * 32, 32), 32), :]
        gh, gl = split2(g)
        eh, el = split2(enc)
        both = dot_nt(jnp.concatenate([gh, gl], axis=0), eh)
        full = both[:32] + both[32:] + dot_nt(gh, el)
        lane = lax.broadcasted_iota(jnp.int32, (16, 128), 1)
        gt_ref[pl.ds(pl.multiple_of(p * 16, 16), 16), :] = jnp.where(lane < 64, full[:16], full[16:])
        level = lax.broadcasted_iota(jnp.int32, (64, 128), 0).astype(F32)
        hot = []
        for f in (2 * p, 2 * p + 1):
            here = 1.0 - m_ref[pl.ds(f, 1), :]
            hot.append(jnp.where(level == b_ref[pl.ds(f, 1), :], here, 0.0))
        one = jnp.concatenate(hot, axis=0).astype(BF16)
        both = dot(jnp.concatenate([lh, ll], axis=0), one)
        picked = (both[:32] + both[32:]) * g
        gf_ref[pl.ds(2 * p, 1), :] = jnp.sum(picked[:16], axis=0, keepdims=True)
        gf_ref[pl.ds(2 * p + 1, 1), :] = jnp.sum(picked[16:], axis=0, keepdims=True)
        return c

    lax.fori_loop(0, t_ref.shape[0] // 16, pair, 0)


def params(**kw):
    return pltpu.CompilerParams(vmem_limit_bytes=VMEM_LIMIT, **kw)


SMEM = pl.BlockSpec(memory_space=pltpu.SMEM)


def whole(shape):
    return pl.BlockSpec(shape, lambda *_: (0,) * len(shape))


def pack(table, bias, miss):
    feats, bins, width = table.shape
    t = jnp.concatenate([jnp.transpose(table, (0, 2, 1)), bias[:, :, None], miss[:, :, None],
                         jnp.zeros((feats, width, 64 - bins - 2), F32)], axis=2)
    return jnp.transpose(t.reshape(feats // 2, 2, width, 64), (0, 2, 1, 3)).reshape(feats // 2 * width, 128)


def unpack(packed, bins, width):
    half = packed.shape[0] // width
    t = jnp.transpose(packed.reshape(half, width, 2, 64), (0, 2, 1, 3)).reshape(half * 2, width, 64)
    return jnp.transpose(t[:, :, :bins], (0, 2, 1)), t[:, :, bins], t[:, :, bins + 1]


def embed(b, f, m, t, w, s, sc):
    count, din = b.shape[1], w.shape[0]
    vm = [whole(x.shape) for x in (b, f, m, t, w, s)]
    shapes = [jax.ShapeDtypeStruct((count, din), F32)] + [jax.ShapeDtypeStruct(w.shape, d) for d in (BF16, F8, F8)]
    return pl.pallas_call(embed_kernel, out_shape=shapes, in_specs=vm + [SMEM], out_specs=[whole(x.shape) for x in shapes],
                          scratch_shapes=[pltpu.VMEM((din, count), F32)], compiler_params=params())(b, f, m, t, w, s, sc)


def forward(e, s, wp, so, bo, ct, sc):
    count, din = e.shape
    members, dout = so.shape
    rows, tiles, block = count * members, count // TILE, TILE * members
    lag = lambda i: jnp.maximum(i - 1, 0)
    big = pl.BlockSpec((TILE, members, dout), lambda i: (lag(i), 0, 0))
    nat = pl.BlockSpec((block, dout), lambda i: (lag(i), 0))
    tra = pl.BlockSpec((dout, block), lambda i: (0, lag(i)))
    return pl.pallas_call(
        forward_kernel,
        out_shape=[jax.ShapeDtypeStruct((count, members, dout), F32)]
        + [jax.ShapeDtypeStruct((rows, dout), d) for d in (BF16, F8, F8)]
        + [jax.ShapeDtypeStruct((dout, rows), d) for d in (BF16, F8, F8)]
        + [jax.ShapeDtypeStruct((members, dout), F32)] * 2,
        grid=(tiles + 1,),
        in_specs=[whole(e.shape), whole(s.shape)] + [whole(w.shape) for w in wp] + [whole(so.shape), whole(bo.shape), big, SMEM],
        out_specs=[big, nat, nat, nat, tra, tra, tra, whole(so.shape), whole(so.shape)],
        scratch_shapes=[pltpu.VMEM(s.shape, F32), pltpu.VMEM(so.shape, F32), pltpu.VMEM(so.shape, F32)]
        + [pltpu.VMEM((block, din), d) for d in (BF16, F8, F8)] * 2
        + [pltpu.VMEM((block, dout), F32)] * 2,
        compiler_params=params(),
    )(e, s, *wp, so, bo, ct, sc)


def backward(e, s, wp, gp, gt, sc):
    count, din = e.shape
    members = s.shape[0]
    rows, dout = gp[0].shape
    step = rows // 4
    shapes = [jax.ShapeDtypeStruct(x, F32) for x in ((din, dout), (count, din), (members, din))]
    ins = (e, s, *wp, *gp, *gt)
    return pl.pallas_call(
        backward_kernel,
        out_shape=shapes,
        in_specs=[whole(x.shape) for x in ins] + [SMEM],
        out_specs=[whole(x.shape) for x in shapes],
        scratch_shapes=[pltpu.VMEM(s.shape, F32)] * 2
        + [pltpu.VMEM((rows, CHUNK), d) for d in (BF16, F8, F8)] * 2
        + [pltpu.VMEM((step, CHUNK), F32)] * 2,
        compiler_params=params(),
    )(*ins, sc)


def tables(b, f, m, t, ge):
    shapes = [jax.ShapeDtypeStruct(t.shape, F32), jax.ShapeDtypeStruct(b.shape, F32)]
    ins = (b, f, m, t, ge)
    return pl.pallas_call(table_kernel, out_shape=shapes, in_specs=[whole(x.shape) for x in ins],
                          out_specs=[whole(x.shape) for x in shapes],
                          scratch_shapes=[pltpu.VMEM(ge.shape[::-1], F32)], compiler_params=params())(*ins)


def scales(e_top, s, w, so, ct):
    top = lambda v: jnp.maximum(jnp.max(jnp.abs(v)), 1e-30)
    sx = TOP / (jnp.maximum(e_top, 1e-30) * top(s))
    sw = TOP / top(w)
    sg = TOP / (1.2 * top(ct) * top(so))
    return jnp.stack([sx, sw, sg, 1.0 / (sx * sw), 1.0 / (sx * sw), 1.0 / (sg * sx), 1.0 / (sg * sw), 1.0 / (sg * sw)])


def shards(bins, fractions, missing, bin_table, bin_bias, miss_vector, scale_in, weight, scale_out, bias_out, cotangent):
    levels, width = bin_table.shape[1:]
    raw = jnp.stack([bins.astype(F32), fractions, missing.astype(F32)]).transpose(0, 2, 1)
    rows = lax.all_to_all(raw, "feat", split_axis=2, concat_axis=1, tiled=True)
    b, f, m = rows[0], rows[1], rows[2]
    packed = lax.all_gather(pack(bin_table, bin_bias, miss_vector), "feat", axis=0, tiled=True)
    tops = jnp.max(jnp.abs(packed))
    sc = scales(tops * (levels + 1), scale_in, weight, scale_out, cotangent)
    e, *wp = embed(b, f, m, packed, weight, scale_in, sc)
    hidden, *rest = forward(e, scale_in, wp, scale_out, bias_out, cotangent, sc)
    gp, gt, (gs, gb) = rest[:3], rest[3:6], rest[6:]
    gw, ge, gsin = backward(e, scale_in, wp, gp, gt, sc)
    gtab, gfrac = tables(b, f, m, packed, ge)
    grad_frac = lax.all_to_all(gfrac, "feat", split_axis=0, concat_axis=1, tiled=True).T
    part = [lax.psum_scatter(gw, "feat", scatter_dimension=0, tiled=True),
            lax.psum_scatter(gsin, "feat", scatter_dimension=1, tiled=True),
            lax.psum_scatter(gs, "feat", scatter_dimension=1, tiled=True),
            lax.psum_scatter(gb, "feat", scatter_dimension=1, tiled=True),
            lax.psum_scatter(gtab, "feat", scatter_dimension=0, tiled=True)]
    gw, gsin, gs, gb, gtab = lax.psum(part, "dp")
    g_table, g_bias, g_miss = unpack(gtab, levels, width)
    return hidden, grad_frac, g_table, g_bias, g_miss, gsin, gw, gs, gb


def solution(mesh):
    placed = (P("dp", "feat"), P("dp", "feat"), P("dp", "feat"), P("feat", None, None), P("feat", None), P("feat", None),
              P(), P(), P(), P(), P(("dp", "feat"), None, None))
    return jax.shard_map(
        shards,
        mesh=mesh,
        in_specs=placed,
        out_specs=(P(("dp", "feat"), None, None), P("dp", "feat"), P("feat", None, None), P("feat", None), P("feat", None),
                   P(None, "feat"), P("feat", None), P(None, "feat"), P(None, "feat")),
        check_vma=False,
    )
```

```python
import functools

import jax
import jax.numpy as jnp
from jax import lax
from jax.experimental import pallas as pl
from jax.experimental.pallas import tpu as pltpu
from jax.sharding import PartitionSpec as P

F32, BF16, F8 = jnp.float32, jnp.bfloat16, jnp.float8_e4m3fn
VMEM_LIMIT = 63 << 20
TILE = 16
CHUNK = 256
TOP = 224.0
LO = 256.0
GELU_A = 0.7978845608028654
GELU_B = GELU_A * 0.044715


def dot(a, b):
    return jnp.dot(a, b, preferred_element_type=F32)


def dot_nt(a, b):
    return lax.dot_general(a, b, (((1,), (1,)), ((), ())), preferred_element_type=F32)


def split3(x):
    hi = x.astype(BF16)
    return hi, x.astype(F8), ((x - hi.astype(F32)) * LO).astype(F8)


def split2(x):
    hi = x.astype(BF16)
    return hi, (x - hi.astype(F32)).astype(BF16)


def product(a, b, mul):
    ah, a8, al = a
    bh, b8, bl = b
    return mul(ah, bh) + (mul(a8, bl) + mul(al, b8)) * (1.0 / LO)


def encode_pair(raw_ref, flocal, first):
    level = lax.broadcasted_iota(jnp.int32, (48, 128), 0).astype(F32)
    row = lax.broadcasted_iota(jnp.int32, (16, 128), 0)
    parts = []
    for f in (first, first + 1):
        b, fr, m = [raw_ref[pl.ds(f + k * flocal, 1), :] for k in range(3)]
        here = 1.0 - m
        parts.append(jnp.clip((b - level) + fr, 0.0, 1.0) * here)
        parts.append(jnp.where(row == 0, here, jnp.where(row == 1, m, 0.0)))
    return jnp.concatenate(parts, axis=0)


def table_pair(t_ref, p):
    blk = t_ref[pl.ds(pl.multiple_of(p * 16, 16), 16), :]
    lane = lax.broadcasted_iota(jnp.int32, (16, 128), 1)
    zero = jnp.zeros_like(blk)
    return jnp.concatenate([jnp.where(lane < 64, blk, zero), jnp.where(lane < 64, zero, blk)], axis=0)


def embed_kernel(nf, raw_ref, t_ref, w_ref, sc_ref, e_ref, wh_ref, w8_ref, wl_ref, et):
    flocal = raw_ref.shape[0] // (3 * nf)
    at_once = 8

    def pairs(j, c):
        for k in range(at_once):
            p = j * at_once + k
            first = 2 * p
            lh, ll = split2(table_pair(t_ref, p))
            eh, el = split2(encode_pair(raw_ref, flocal, (first // flocal) * (3 * flocal) + lax.rem(first, flocal)))
            both = dot(jnp.concatenate([lh, ll], axis=0), eh)
            et[pl.ds(pl.multiple_of(p * 32, 32), 32), :] = both[:32] + both[32:] + dot(lh, el)
        return c

    lax.fori_loop(0, t_ref.shape[0] // (16 * at_once), pairs, 0)
    for j in range(et.shape[0] // 128):
        e_ref[:, j * 128:(j + 1) * 128] = et[j * 128:(j + 1) * 128, :].T
    wh_ref[...], w8_ref[...], wl_ref[...] = split3(w_ref[...] * sc_ref[1])


def forward_kernel(nf, e_ref, s_ref, wh_ref, w8_ref, wl_ref, so_ref, bo_ref, ct_ref, sc_ref,
                   hid_ref, gh_ref, g8_ref, gl_ref, th_ref, t8_ref, tl_ref, z_ref,
                   gs_ref, gb_ref, s1, so1, so2, xh0, x80, xl0, xh1, x81, xl1, pre0, pre1):
    i = pl.program_id(0)
    tiles = pl.num_programs(0) - 1
    members, width_out = so_ref.shape
    rows = TILE * members
    x = ((xh0, x80, xl0), (xh1, x81, xl1))
    pre = (pre0, pre1)
    w = (wh_ref, w8_ref, wl_ref)

    def prepare(tile, to):
        for n in range(TILE):
            v = s1[...] * e_ref[pl.ds(tile * TILE + n, 1), :]
            r = slice(n * members, (n + 1) * members)
            to[0][r, :], to[1][r, :], to[2][r, :] = split3(v)

    def multiply(a, to):
        to[...] = product([r[...] for r in a], [r[...] for r in w], dot)

    def finish(p):
        for h0 in range(0, width_out, 128):
            hs = slice(h0, h0 + 128)
            sa, sb, bo = so1[:, hs], so2[:, hs], bo_ref[:, hs]
            gs, gb = gs_ref[:, hs], gb_ref[:, hs]
            for n in range(TILE):
                r = slice(n * members, (n + 1) * members)
                q = p[r, hs]
                v = q * sa + bo
                v2 = v * v
                half = 0.5 + 0.5 * jnp.tanh(v * (GELU_B * v2 + GELU_A))
                hid = v * half
                hid_ref[n, :, hs] = hid
                g = half + hid * (1.0 - half) * ((6.0 * GELU_B) * v2 + 2.0 * GELU_A)
                ga = ct_ref[n, :, hs] * g
                gs = gs + ga * q
                gb = gb + ga
                gh_ref[r, hs], g8_ref[r, hs], gl_ref[r, hs] = split3(ga * sb)
            gs_ref[:, hs], gb_ref[:, hs] = gs, gb
        th_ref[...] = gh_ref[...].T
        t8_ref[...] = g8_ref[...].T
        tl_ref[...] = gl_ref[...].T

    @pl.when(i == 0)
    def _():
        s1[...] = s_ref[...] * sc_ref[0]
        so1[...] = so_ref[...] * sc_ref[3]
        so2[...] = so_ref[...] * sc_ref[2]
        gs_ref[...] = jnp.zeros_like(gs_ref)
        gb_ref[...] = jnp.zeros_like(gb_ref)
        prepare(0, x[0])
        multiply(x[0], pre[0])
        prepare(1, x[1])

    for par in (0, 1):
        @pl.when((i > 0) & (i < tiles) & (i % 2 == par))
        def _():
            multiply(x[par], pre[par])
            prepare(jnp.minimum(i + 1, tiles - 1), x[1 - par])
            finish(pre[1 - par])

    @pl.when(i == tiles)
    def _():
        finish(pre[1])
        part = width_out // nf
        for o in range(nf):
            z_ref[:, 2 * o * part:(2 * o + 1) * part] = gs_ref[:, o * part:(o + 1) * part] * sc_ref[4]
            z_ref[:, (2 * o + 1) * part:(2 * o + 2) * part] = gb_ref[:, o * part:(o + 1) * part]


def send(src, dst, ssem, rsem, **where):
    return pltpu.make_async_remote_copy(src_ref=src, dst_ref=dst, send_sem=ssem, recv_sem=rsem, device_id=where,
                                        device_id_type=pl.DeviceIdType.MESH)


def greet(partners):
    barrier = pltpu.get_barrier_semaphore()
    for where in partners:
        pl.semaphore_signal(barrier, inc=1, device_id=where, device_id_type=pl.DeviceIdType.MESH)
    pl.semaphore_wait(barrier, len(partners))


def backward_kernel(nd, nf, e_ref, s_ref, z_ref, raw_ref, t_ref, sc_ref, wh_in, w8_in, wl_in, gh_in, g8_in, gl_in,
                    th_in, t8_in, tl_in, gw_out, sm_out, fr_out,
                    wh, w8, wl, gh, g8, gl, th, t8, tl, s1, s2, xh0, x80, xl0, xh1, x81, xl1, g0, g1, ge, gsin, et,
                    gw, sm, gf, ra, rb, rc, r1, r2,
                    load, a_s, a_r, b_s, b_r, c_s, c_r, d_s, d_r, e_s, e_r, f_s, f_r, u_s, u_r, v_s, v_r, y_s, y_r):
    members, width_in = s_ref.shape
    rows = gh.shape[0]
    count = e_ref.shape[0]
    chunks = width_in // CHUNK
    per = chunks // nf
    nchip = nd // 2
    half, blk, sblk = CHUNK // 2, CHUNK // nd, sm.shape[1] // nd
    feats = CHUNK // 16
    flocal = fr_out.shape[1]
    me, z = lax.axis_index("dp"), lax.axis_index("feat")
    core, chip = lax.rem(me, 2), me // 2
    partner = me + 1 - 2 * core

    loads = [pltpu.make_async_copy(i, o, load.at[k]) for k, (i, o) in enumerate(
        ((th_in, th), (t8_in, t8), (tl_in, tl), (wh_in, wh), (w8_in, w8), (wl_in, wl), (gh_in, gh), (g8_in, g8), (gl_in, gl)))]
    for copy in loads:
        copy.start()

    greet([{"dp": lax.rem(me + o, nd)} for o in range(1, nd)] + [{"feat": lax.rem(z + o, nf)} for o in range(1, nf)])

    def aligned(i, n):
        return pl.ds(pl.multiple_of(i, n), n)

    def place(i):
        return lax.rem(i, nf) * per + i // nf

    def owner(i):
        return lax.rem(i, nf)

    def send_a(i):
        return send(gw.at[aligned(place(i) * CHUNK + (1 - core) * half, half)], ra.at[i], a_s.at[i], a_r.at[i], dp=partner)

    def send_b(i, o):
        to = lax.rem(chip + o, nchip)
        return send(gw.at[aligned(place(i) * CHUNK + core * half + to * blk, blk)], rb.at[i, o - 1], b_s.at[i, o - 1],
                    b_r.at[i, o - 1], dp=2 * to + core)

    def mine(i):
        return aligned(place(i) * CHUNK + core * half + chip * blk, blk)

    def send_c(i, k):
        j = i // nf
        return send(gw.at[mine(i)], rc.at[j, k - 1], c_s.at[i], c_r.at[j, k - 1], feat=owner(i))

    def home(i, q):
        return aligned((i // nf) * CHUNK + core * half + q * blk, blk)

    def send_d(i, o, q):
        j = i // nf
        return send(gw.at[mine(i)], gw_out.at[home(i, q)], d_s.at[j, o - 1], d_r.at[j, o - 1],
                    dp=2 * lax.rem(chip + o, nchip) + core)

    def send_e(i, side):
        j = i // nf
        r = aligned(j * CHUNK + side * half, half)
        return send(gw_out.at[r], gw_out.at[r], e_s.at[j], e_r.at[j], dp=partner)

    def far(i):
        return lax.rem(owner(i) - z + nf, nf)

    def step_b(i):
        send_a(i).wait_recv()
        gw[aligned(place(i) * CHUNK + core * half, half), :] += ra[i]
        for o in range(1, nchip):
            send_b(i, o).start()

    def step_c(i):
        for o in range(1, nchip):
            send_b(i, o).wait_recv()
        total = gw[mine(i), :]
        for o in range(1, nchip):
            total = total + rb[i, o - 1]
        gw[mine(i), :] = total

        @pl.when(owner(i) != z)
        def _():
            send_c(i, far(i)).start()

    def step_d(i):
        @pl.when(owner(i) == z)
        def _():
            total = gw[mine(i), :]
            for k in range(1, nf):
                send_c(i, k).wait_recv()
                total = total + rc[i // nf, k - 1]
            gw[mine(i), :] = total
            gw_out[home(i, chip), :] = total
            for o in range(1, nchip):
                send_d(i, o, chip).start()

    def step_e(i):
        @pl.when(owner(i) == z)
        def _():
            for o in range(1, nchip):
                send_d(i, o, lax.rem(chip - o + nchip, nchip)).wait_recv()
            send_e(i, core).start()

    def step_f(i):
        @pl.when(owner(i) == z)
        def _():
            send_e(i, 1 - core).wait_recv()

    def drain(i):
        send_a(i).wait_send()
        for o in range(1, nchip):
            send_b(i, o).wait_send()

        @pl.when(owner(i) != z)
        def _():
            send_c(i, far(i)).wait_send()

        @pl.when(owner(i) == z)
        def _():
            for o in range(1, nchip):
                send_d(i, o, chip).wait_send()
            send_e(i, core).wait_send()

    def send_u(i, o):
        to = lax.rem(me + o, nd)
        return send(sm.at[i, aligned(to * sblk, sblk)], r1.at[i, o - 1], u_s.at[i, o - 1], u_r.at[i, o - 1], dp=to)

    def send_v(i, k):
        j = i // nf
        return send(sm.at[i, aligned(me * sblk, sblk)], r2.at[j, k - 1], v_s.at[i], v_r.at[j, k - 1], feat=owner(i))

    def send_y(i, o, q):
        j = i // nf
        return send(sm.at[i, aligned(me * sblk, sblk)], sm_out.at[j, aligned(q * sblk, sblk)], y_s.at[j, o - 1], y_r.at[j, o - 1],
                    dp=lax.rem(me + o, nd))

    def send_f(i, k, src):
        j = i // nf
        return send(gf.at[i], fr_out.at[src, aligned(j * feats, feats)], f_s.at[i], f_r.at[j, k - 1], feat=owner(i))

    def start_u(i):
        for o in range(1, nd):
            send_u(i, o).start()

        @pl.when(owner(i) != z)
        def _():
            send_f(i, far(i), z).start()

        @pl.when(owner(i) == z)
        def _():
            fr_out[z, aligned((i // nf) * feats, feats), :] = gf[i]

    def step_v(i):
        r = aligned(me * sblk, sblk)
        for o in range(1, nd):
            send_u(i, o).wait_recv()
        total = sm[i, r, :]
        for o in range(1, nd):
            total = total + r1[i, o - 1]
        sm[i, r, :] = total

        @pl.when(owner(i) != z)
        def _():
            send_v(i, far(i)).start()

    def step_y(i):
        @pl.when(owner(i) == z)
        def _():
            r = aligned(me * sblk, sblk)
            total = sm[i, r, :]
            for k in range(1, nf):
                send_v(i, k).wait_recv()
                total = total + r2[i // nf, k - 1]
            sm[i, r, :] = total
            sm_out[i // nf, r, :] = total
            for o in range(1, nd):
                send_y(i, o, me).start()

    def step_w(i):
        @pl.when(owner(i) == z)
        def _():
            for o in range(1, nd):
                send_y(i, o, lax.rem(me - o + nd, nd)).wait_recv()
            for k in range(1, nf):
                send_f(i, k, lax.rem(z - k + nf, nf)).wait_recv()

    def drain_small(i):
        for o in range(1, nd):
            send_u(i, o).wait_send()

        @pl.when(owner(i) != z)
        def _():
            send_v(i, far(i)).wait_send()
            send_f(i, far(i), z).wait_send()

        @pl.when(owner(i) == z)
        def _():
            for o in range(1, nd):
                send_y(i, o, me).wait_send()

    def when_chunk(i, f):
        @pl.when((i >= 0) & (i < chunks))
        def _():
            f(i)

    def events(k):
        when_chunk(k, lambda i: send_a(i).start())
        when_chunk(k - 1, step_b)
        when_chunk(k - 5, step_c)
        when_chunk(k - 7, step_d)
        when_chunk(k - 8, step_e)
        when_chunk(k - 9, step_f)

    x = ((xh0, x80, xl0), (xh1, x81, xl1))
    gt = (th, t8, tl)
    s1[...] = s_ref[...] * sc_ref[0]
    s2[...] = s_ref[...] * sc_ref[6]

    def cols(i):
        return aligned(place(i) * CHUNK, CHUNK)

    def prepare(i, to):
        for n in range(0, count, TILE):
            v = (e_ref[n:n + TILE, cols(i)][:, None, :] * s1[:, cols(i)][None]).reshape(TILE * members, CHUNK)
            r = slice(n * members, (n + TILE) * members)
            to[0][r, :], to[1][r, :], to[2][r, :] = split3(v)

    prepare(0, x[0])
    for copy in loads[:3]:
        copy.wait()

    def weights(j, carry):
        for par in (0, 1):
            i = 2 * j + par
            r = product([t[...] for t in gt], [t[...] for t in x[par]], dot)
            gw[cols(i), :] = r.T * sc_ref[5]
            prepare(jnp.minimum(i + 1, chunks - 1), x[1 - par])
            events(i)
        return carry

    lax.fori_loop(0, chunks // 2, weights, 0)

    for copy in loads[3:]:
        copy.wait()
    gsin[...] = jnp.zeros_like(gsin)
    g1[...] = jnp.zeros_like(g1)
    step = g0.shape[0]
    objs = step // members
    parts = rows // step

    def finish(i, t, g):
        g3 = g[...].reshape(objs, members, CHUNK)
        ns = slice(t * objs, (t + 1) * objs)
        ge[ns, :] = jnp.sum(g3 * s2[:, cols(i)][None], axis=1)
        gsin[...] += jnp.sum(g3 * e_ref[ns, cols(i)][:, None, :], axis=0)

    def table(i):
        c = place(i)
        first = c * feats
        base = (first // flocal) * (3 * flocal) + lax.rem(first, flocal)
        for j in range(CHUNK // 128):
            et[j * 128:(j + 1) * 128, :] = ge[:, j * 128:(j + 1) * 128].T
        lane = lax.broadcasted_iota(jnp.int32, (16, 128), 1)
        level = lax.broadcasted_iota(jnp.int32, (64, 128), 0).astype(F32)
        for p in range(feats // 2):
            row = base + 2 * p
            lh, ll = split2(table_pair(t_ref, c * (feats // 2) + p))
            enc = encode_pair(raw_ref, flocal, row)
            g = et[p * 32:(p + 1) * 32, :]
            gh_, gl_ = split2(g)
            eh, el = split2(enc)
            both = dot_nt(jnp.concatenate([gh_, gl_], axis=0), eh)
            full = both[:32] + both[32:] + dot_nt(gh_, el)
            sm[i, p * 16:(p + 1) * 16, :] = jnp.where(lane < 64, full[:16], full[16:])
            hot = []
            for f in (row, row + 1):
                here = 1.0 - raw_ref[pl.ds(f + 2 * flocal, 1), :]
                hot.append(jnp.where(level == raw_ref[pl.ds(f, 1), :], here, 0.0))
            one = jnp.concatenate(hot, axis=0).astype(BF16)
            both = dot(jnp.concatenate([lh, ll], axis=0), one)
            picked = (both[:32] + both[32:]) * g
            gf[i, 2 * p:2 * p + 1, :] = jnp.sum(picked[:16], axis=0, keepdims=True)
            gf[i, 2 * p + 1:2 * p + 2, :] = jnp.sum(picked[16:], axis=0, keepdims=True)
        at = feats * 8
        for j in range(CHUNK // 128):
            sm[i, at:at + members, :] = gsin[:, j * 128:(j + 1) * 128] * sc_ref[7]
            at += members
        sm[i, at:at + members, :] = z_ref[:, aligned(c * 128, 128)]
        at += members
        sm[i, at:, :] = jnp.zeros_like(sm[i, at:, :])
        gsin[...] = jnp.zeros_like(gsin)

    def inputs(i, carry):
        wc = [t[cols(i), :] for t in (wh, w8, wl)]
        for t in range(parts):
            to, fro = (g0, g1) if t % 2 == 0 else (g1, g0)
            rs = slice(t * step, (t + 1) * step)
            to[...] = product([r[rs, :] for r in (gh, g8, gl)], wc, dot_nt)
            if t == 0:
                @pl.when(i > 0)
                def _():
                    finish(i - 1, parts - 1, fro)
                    table(i - 1)
                    start_u(i - 1)
            else:
                finish(i, t - 1, fro)
        events(i + chunks)
        when_chunk(i - 2, step_v)
        when_chunk(i - 3, step_y)
        when_chunk(i - 4, step_w)
        return carry

    lax.fori_loop(0, chunks, inputs, 0)
    last = chunks - 1
    finish(last, parts - 1, g1)
    table(last)
    start_u(last)
    step_v(last - 1)
    step_y(last - 2)
    step_v(last)
    step_y(last - 1)
    step_w(last - 3)
    step_f(last)
    step_y(last)

    def close(i, carry):
        drain(i)
        drain_small(i)
        return carry

    lax.fori_loop(0, chunks, close, 0)
    for i in range(3):
        step_w(last - 2 + i)


def final_kernel(nf, bins, gw_ref, sm_ref, fr_ref, frac_ref, tab_ref, bias_ref, miss_ref, sin_ref, gw_out, so_ref, bo_ref):
    gw_out[...] = gw_ref[...]
    flocal = fr_ref.shape[1]
    for o in range(nf):
        frac_ref[o * 128:(o + 1) * 128, :] = fr_ref[o].T
    members = sin_ref.shape[0]
    feats = CHUNK // 16
    width = so_ref.shape[1]
    small = []
    for j in range(sm_ref.shape[0]):
        t = sm_ref[j, :feats * 8, :].T
        for p in range(feats // 2):
            for odd in (0, 1):
                f = j * feats + 2 * p + odd
                col = t[odd * 64:(odd + 1) * 64, p * 16:(p + 1) * 16]
                tab_ref[f] = col[:bins]
                bias_ref[f:f + 1, :] = col[bins:bins + 1]
                miss_ref[f:f + 1, :] = col[bins + 1:bins + 2]
        at = feats * 8
        for q in range(CHUNK // 128):
            sin_ref[:, j * CHUNK + q * 128:j * CHUNK + (q + 1) * 128] = sm_ref[j, at:at + members, :]
            at += members
        small.append(sm_ref[j, at:at + members, :])
    small = small[0] if len(small) == 1 else jnp.concatenate(small, axis=1)
    so_ref[...] = small[:, :width]
    bo_ref[...] = small[:, width:]


def params(**kw):
    return pltpu.CompilerParams(vmem_limit_bytes=VMEM_LIMIT, **kw)


SMEM = pl.BlockSpec(memory_space=pltpu.SMEM)


def whole(shape):
    return pl.BlockSpec(shape, lambda *_: (0,) * len(shape))


def pack(table, bias, miss):
    feats, bins, width = table.shape
    t = jnp.concatenate([jnp.transpose(table, (0, 2, 1)), bias[:, :, None], miss[:, :, None],
                         jnp.zeros((feats, width, 64 - bins - 2), F32)], axis=2)
    return jnp.transpose(t.reshape(feats // 2, 2, width, 64), (0, 2, 1, 3)).reshape(feats // 2 * width, 128)


def embed(nf, raw, t, w, sc):
    count, din = raw.shape[1], w.shape[0]
    vm = [whole(x.shape) for x in (raw, t, w)]
    shapes = [jax.ShapeDtypeStruct((count, din), F32)] + [jax.ShapeDtypeStruct(w.shape, d) for d in (BF16, F8, F8)]
    return pl.pallas_call(functools.partial(embed_kernel, nf), out_shape=shapes, in_specs=vm + [SMEM], out_specs=[whole(x.shape) for x in shapes],
                          scratch_shapes=[pltpu.VMEM((din, count), F32)], compiler_params=params())(raw, t, w, sc)


def forward(nf, e, s, wp, so, bo, ct, sc):
    count, din = e.shape
    members, dout = so.shape
    rows, tiles, block = count * members, count // TILE, TILE * members
    lag = lambda i: jnp.maximum(i - 1, 0)
    big = pl.BlockSpec((TILE, members, dout), lambda i: (lag(i), 0, 0))
    nat = pl.BlockSpec((block, dout), lambda i: (lag(i), 0))
    tra = pl.BlockSpec((dout, block), lambda i: (0, lag(i)))
    return pl.pallas_call(
        functools.partial(forward_kernel, nf),
        out_shape=[jax.ShapeDtypeStruct((count, members, dout), F32)]
        + [jax.ShapeDtypeStruct((rows, dout), d) for d in (BF16, F8, F8)]
        + [jax.ShapeDtypeStruct((dout, rows), d) for d in (BF16, F8, F8)]
        + [jax.ShapeDtypeStruct((members, 2 * dout), F32)],
        grid=(tiles + 1,),
        in_specs=[whole(e.shape), whole(s.shape)] + [whole(w.shape) for w in wp] + [whole(so.shape), whole(bo.shape), big, SMEM],
        out_specs=[big, nat, nat, nat, tra, tra, tra, whole((members, 2 * dout))],
        scratch_shapes=[pltpu.VMEM(so.shape, F32)] * 2 + [pltpu.VMEM(s.shape, F32), pltpu.VMEM(so.shape, F32), pltpu.VMEM(so.shape, F32)]
        + [pltpu.VMEM((block, din), d) for d in (BF16, F8, F8)] * 2
        + [pltpu.VMEM((block, dout), F32)] * 2,
        compiler_params=params(),
    )(e, s, *wp, so, bo, ct, sc)


def backward(nd, nf, e, s, zs, raw, t, wp, gp, gt, sc):
    count, din = e.shape
    members = s.shape[0]
    rows, dout = gp[0].shape
    step = rows // 4
    chunks, nchip = din // CHUNK, nd // 2
    per = chunks // nf
    half, blk, sblk = CHUNK // 2, CHUNK // nd, 256 // nd
    feats, flocal = CHUNK // 16, raw.shape[0] // (3 * nf)
    shapes = [jax.ShapeDtypeStruct(x, F32) for x in ((din // nf, dout), (per, 256, 128), (nf, flocal, 128))]
    ins = (e, s, zs, raw, t)
    far = (*wp, *gp, *gt)
    dma = pltpu.SemaphoreType.DMA
    f32 = lambda *shape: pltpu.VMEM(shape, F32)
    return pl.pallas_call(
        functools.partial(backward_kernel, nd, nf),
        out_shape=shapes,
        in_specs=[whole(x.shape) for x in ins] + [SMEM] + [pl.BlockSpec(memory_space=pl.ANY)] * len(far),
        out_specs=[whole(x.shape) for x in shapes],
        scratch_shapes=[pltpu.VMEM(x.shape, x.dtype) for x in far]
        + [f32(*s.shape)] * 2
        + [pltpu.VMEM((rows, CHUNK), d) for d in (BF16, F8, F8)] * 2
        + [f32(step, CHUNK)] * 2
        + [f32(count, CHUNK), f32(members, CHUNK), f32(CHUNK, count)]
        + [f32(din, dout), f32(chunks, 256, 128), f32(chunks, feats, count)]
        + [f32(chunks, half, dout), f32(chunks, nchip - 1, blk, dout), f32(per, nf - 1, blk, dout)]
        + [f32(chunks, nd - 1, sblk, 128), f32(per, nf - 1, sblk, 128)]
        + [dma((9,))]
        + [dma((chunks,))] * 2 + [dma((chunks, nchip - 1))] * 2 + [dma((chunks,)), dma((per, nf - 1))]
        + [dma((per, nchip - 1))] * 2 + [dma((per,))] * 2 + [dma((chunks,)), dma((per, nf - 1))]
        + [dma((chunks, nd - 1))] * 2 + [dma((chunks,)), dma((per, nf - 1))] + [dma((per, nd - 1))] * 2,
        compiler_params=params(collective_id=1, has_side_effects=True),
    )(*ins, sc, *far)


def final(nf, bins, gw, sm, fr):
    per, flocal = sm.shape[0], fr.shape[1]
    members, width = 32, gw.shape[1] // nf
    shapes = [jax.ShapeDtypeStruct(x, F32) for x in (
        (nf * 128, flocal), (flocal, bins, 16), (flocal, 16), (flocal, 16), (members, per * CHUNK), gw.shape, (members, width), (members, width))]
    ins = (gw, sm, fr)
    return pl.pallas_call(functools.partial(final_kernel, nf, bins), out_shape=shapes, in_specs=[whole(x.shape) for x in ins],
                          out_specs=[whole(x.shape) for x in shapes], compiler_params=params())(*ins)


def scales(e_top, s, w, so, ct):
    top = lambda v: jnp.maximum(jnp.max(jnp.abs(v)), 1e-30)
    sx = TOP / (jnp.maximum(e_top, 1e-30) * top(s))
    sw = TOP / top(w)
    sg = TOP / (1.2 * top(ct) * top(so))
    return jnp.stack([sx, sw, sg, 1.0 / (sx * sw), 1.0 / (sx * sw), 1.0 / (sg * sx), 1.0 / (sg * sw), 1.0 / (sg * sw)])


def shards(nd, nf, bins, fractions, missing, bin_table, bin_bias, miss_vector, scale_in, weight, scale_out, bias_out, cotangent):
    levels, width = bin_table.shape[1:]
    flocal = bins.shape[1]
    raw = jnp.stack([bins.astype(F32), fractions, missing.astype(F32)]).transpose(0, 2, 1)
    raw = lax.all_to_all(raw.reshape(3 * flocal, -1), "feat", split_axis=1, concat_axis=0, tiled=True)
    packed = lax.all_gather(pack(bin_table, bin_bias, miss_vector), "feat", axis=0, tiled=True)
    tops = jnp.max(jnp.abs(packed))
    sc = scales(tops * (levels + 1), scale_in, weight, scale_out, cotangent)
    e, *wp = embed(nf, raw, packed, weight, sc)
    hidden, *rest = forward(nf, e, scale_in, wp, scale_out, bias_out, cotangent, sc)
    gw, sm, fr = backward(nd, nf, e, scale_in, rest[6], raw, packed, wp, rest[:3], rest[3:6], sc)
    frac, table, bias, miss, sin, gw, so, bo = final(nf, levels, gw, sm, fr)
    return hidden, frac, table, bias, miss, sin, gw, so, bo


def solution(mesh):
    placed = (P("dp", "feat"), P("dp", "feat"), P("dp", "feat"), P("feat", None, None), P("feat", None), P("feat", None),
              P(), P(), P(), P(), P(("dp", "feat"), None, None))
    return jax.shard_map(
        functools.partial(shards, mesh.shape["dp"], mesh.shape["feat"]),
        mesh=mesh,
        in_specs=placed,
        out_specs=(P(("dp", "feat"), None, None), P("dp", "feat"), P("feat", None, None), P("feat", None), P("feat", None),
                   P(None, "feat"), P("feat", None), P(None, "feat"), P(None, "feat")),
        check_vma=False,
    )
```

```python
import functools

import jax
import jax.numpy as jnp
from jax import lax
from jax.experimental import pallas as pl
from jax.experimental.pallas import tpu as pltpu
from jax.sharding import PartitionSpec as P

F32, BF16, F8 = jnp.float32, jnp.bfloat16, jnp.float8_e4m3fn
VMEM_LIMIT = 63 << 20
TILE = 16
CHUNK = 256
TOP = 224.0
LO = 256.0
GELU_A = 0.7978845608028654
GELU_B = GELU_A * 0.044715


def dot(a, b):
    return jnp.dot(a, b, preferred_element_type=F32)


def dot_nt(a, b):
    return lax.dot_general(a, b, (((1,), (1,)), ((), ())), preferred_element_type=F32)


def split3(x):
    hi = x.astype(BF16)
    return hi, x.astype(F8), ((x - hi.astype(F32)) * LO).astype(F8)


def split2(x):
    hi = x.astype(BF16)
    return hi, (x - hi.astype(F32)).astype(BF16)


def product(a, b, mul):
    ah, a8, al = a
    bh, b8, bl = b
    return mul(ah, bh) + (mul(a8, bl) + mul(al, b8)) * (1.0 / LO)


def encode_pair(raw_ref, flocal, first):
    level = lax.broadcasted_iota(jnp.int32, (48, 128), 0).astype(F32)
    row = lax.broadcasted_iota(jnp.int32, (16, 128), 0)
    parts = []
    for f in (first, first + 1):
        b, fr, m = [raw_ref[pl.ds(f + k * flocal, 1), :] for k in range(3)]
        here = 1.0 - m
        parts.append(jnp.clip((b - level) + fr, 0.0, 1.0) * here)
        parts.append(jnp.where(row == 0, here, jnp.where(row == 1, m, 0.0)))
    return jnp.concatenate(parts, axis=0)


def table_pair(t_ref, p):
    blk = t_ref[pl.ds(pl.multiple_of(p * 16, 16), 16), :]
    lane = lax.broadcasted_iota(jnp.int32, (16, 128), 1)
    zero = jnp.zeros_like(blk)
    return jnp.concatenate([jnp.where(lane < 64, blk, zero), jnp.where(lane < 64, zero, blk)], axis=0)


def send(src, dst, ssem, rsem, **where):
    return pltpu.make_async_remote_copy(src_ref=src, dst_ref=dst, send_sem=ssem, recv_sem=rsem, device_id=where,
                                        device_id_type=pl.DeviceIdType.MESH)


def greet(partners):
    barrier = pltpu.get_barrier_semaphore()
    for where in partners:
        pl.semaphore_signal(barrier, inc=1, device_id=where, device_id_type=pl.DeviceIdType.MESH)
    pl.semaphore_wait(barrier, len(partners))


def exchange_kernel(nf, bins_ref, fr_ref, ms_ref, tab_ref, bias_ref, miss_ref, s_ref, so_ref, w_in, ct_in,
                    raw_ref, t_ref, e_ref, sc_ref, wh_out, w8_out, wl_out,
                    mine, et, w, ct, wh, w8, wl, load, store, r_s, r_r, t_s, t_r):
    flocal, total = bins_ref.shape
    count = total // nf
    bins, width = tab_ref.shape[2], tab_ref.shape[1]
    z = lax.axis_index("feat")
    parts = ct.shape[0]
    step = ct_in.shape[0] // parts

    loads = [pltpu.make_async_copy(w_in, w, load.at[0])] + [
        pltpu.make_async_copy(ct_in.at[pl.ds(i * step, step)], ct.at[i], load.at[i + 1]) for i in range(parts)]
    for copy in loads:
        copy.start()

    def rows(q):
        return pl.ds(pl.multiple_of(q * (3 * flocal), 3 * flocal), 3 * flocal)

    def entries(q):
        n = flocal // 2 * width
        return pl.ds(pl.multiple_of(q * n, n), n)

    mine[0:flocal, :] = bins_ref[...].astype(F32)
    mine[flocal:2 * flocal, :] = fr_ref[...]
    mine[2 * flocal:, :] = ms_ref[...].astype(F32)
    raw_ref[rows(z), :] = mine[:, pl.ds(pl.multiple_of(z * count, count), count)]
    blank = jnp.zeros((width, 64 - bins - 2), F32)
    for p in range(flocal // 2):
        block = []
        for f in (2 * p, 2 * p + 1):
            block += [tab_ref[f], bias_ref[:, f:f + 1], miss_ref[:, f:f + 1], blank]
        t_ref[pl.ds(pl.multiple_of(z * (flocal // 2 * width) + p * width, width), width), :] = jnp.concatenate(block, axis=1)

    greet([{"feat": lax.rem(z + o, nf)} for o in range(1, nf)])

    def send_raw(o, q):
        to = lax.rem(z + o, nf)
        return send(mine.at[:, pl.ds(pl.multiple_of(to * count, count), count)], raw_ref.at[rows(q)],
                    r_s.at[o - 1], r_r.at[o - 1], feat=to)

    def send_table(o, q):
        return send(t_ref.at[entries(q)], t_ref.at[entries(q)], t_s.at[o - 1], t_r.at[o - 1], feat=lax.rem(z + o, nf))

    for o in range(1, nf):
        send_raw(o, z).start()
    for o in range(1, nf):
        send_table(o, z).start()

    def top(v):
        return jnp.maximum(jnp.max(jnp.max(jnp.abs(v), axis=0, keepdims=True), axis=1, keepdims=True), 1e-30)

    loads[0].wait()
    sw = TOP / top(w[...])
    for i in range(0, w.shape[0], 256):
        r = slice(i, i + 256)
        wh[r, :], w8[r, :], wl[r, :] = split3(w[r, :] * sw)
    stores = [pltpu.make_async_copy(i, o, store.at[k]) for k, (i, o) in enumerate(((wh, wh_out), (w8, w8_out), (wl, wl_out)))]
    for copy in stores:
        copy.start()

    at_once = 8
    pairs = flocal // 2

    def embed(q):
        def body(j, c):
            for k in range(at_once):
                p = q * pairs + j * at_once + k
                first = q * (3 * flocal) + 2 * (j * at_once + k)
                lh, ll = split2(table_pair(t_ref, p))
                eh, el = split2(encode_pair(raw_ref, flocal, first))
                both = dot(jnp.concatenate([lh, ll], axis=0), eh)
                et[pl.ds(pl.multiple_of(p * 32, 32), 32), :] = both[:32] + both[32:] + dot(lh, el)
            return c

        lax.fori_loop(0, pairs // at_once, body, 0)

    embed(z)
    tc = jnp.full((1, 1), 1e-30, F32)
    for i in range(parts):
        loads[i + 1].wait()
        tc = jnp.maximum(tc, top(ct[i].reshape(-1, ct.shape[-1])))
    for o in range(1, nf):
        q = lax.rem(z - o + nf, nf)
        send_raw(o, q).wait_recv()
        send_table(o, q).wait_recv()
        embed(q)
    for j in range(et.shape[0] // 128):
        e_ref[:, j * 128:(j + 1) * 128] = et[j * 128:(j + 1) * 128, :].T
    sx = TOP / (top(et[...]) * top(s_ref[...]))
    sg = TOP / (1.2 * tc * top(so_ref[...]))
    for k, v in enumerate((sx, sw, sg, 1.0 / (sx * sw), 1.0 / (sx * sw), 1.0 / (sg * sx), 1.0 / (sg * sw), 1.0 / (sg * sw))):
        sc_ref[k:k + 1, :] = jnp.broadcast_to(v, (1, 128))
    for copy in stores:
        copy.wait()
    for o in range(1, nf):
        send_raw(o, z).wait_send()
        send_table(o, z).wait_send()


def forward_kernel(nf, e_ref, s_ref, wh_ref, w8_ref, wl_ref, so_ref, bo_ref, ct_ref, sc_ref,
                   hid_ref, gh_ref, g8_ref, gl_ref, th_ref, t8_ref, tl_ref, z_ref,
                   gs_ref, gb_ref, s1, so1, so2, xh0, x80, xl0, xh1, x81, xl1, pre0, pre1):
    i = pl.program_id(0)
    tiles = pl.num_programs(0) - 1
    members, width_out = so_ref.shape
    rows = TILE * members
    x = ((xh0, x80, xl0), (xh1, x81, xl1))
    pre = (pre0, pre1)
    w = (wh_ref, w8_ref, wl_ref)

    def prepare(tile, to):
        for n in range(TILE):
            v = s1[...] * e_ref[pl.ds(tile * TILE + n, 1), :]
            r = slice(n * members, (n + 1) * members)
            to[0][r, :], to[1][r, :], to[2][r, :] = split3(v)

    def multiply(a, to):
        to[...] = product([r[...] for r in a], [r[...] for r in w], dot)

    def finish(p):
        for h0 in range(0, width_out, 128):
            hs = slice(h0, h0 + 128)
            sa, sb, bo = so1[:, hs], so2[:, hs], bo_ref[:, hs]
            gs, gb = gs_ref[:, hs], gb_ref[:, hs]
            for n in range(TILE):
                r = slice(n * members, (n + 1) * members)
                q = p[r, hs]
                v = q * sa + bo
                v2 = v * v
                half = 0.5 + 0.5 * jnp.tanh(v * (GELU_B * v2 + GELU_A))
                hid = v * half
                hid_ref[n, :, hs] = hid
                g = half + hid * (1.0 - half) * ((6.0 * GELU_B) * v2 + 2.0 * GELU_A)
                ga = ct_ref[n, :, hs] * g
                gs = gs + ga * q
                gb = gb + ga
                gh_ref[r, hs], g8_ref[r, hs], gl_ref[r, hs] = split3(ga * sb)
            gs_ref[:, hs], gb_ref[:, hs] = gs, gb
        th_ref[...] = gh_ref[...].T
        t8_ref[...] = g8_ref[...].T
        tl_ref[...] = gl_ref[...].T

    @pl.when(i == 0)
    def _():
        s1[...] = s_ref[...] * sc_ref[0:0 + 1, 0:1]
        so1[...] = so_ref[...] * sc_ref[3:3 + 1, 0:1]
        so2[...] = so_ref[...] * sc_ref[2:2 + 1, 0:1]
        gs_ref[...] = jnp.zeros_like(gs_ref)
        gb_ref[...] = jnp.zeros_like(gb_ref)
        prepare(0, x[0])
        multiply(x[0], pre[0])
        prepare(1, x[1])

    for par in (0, 1):
        @pl.when((i > 0) & (i < tiles) & (i % 2 == par))
        def _():
            finish(pre[1 - par])
            prepare(jnp.minimum(i + 1, tiles - 1), x[1 - par])
            multiply(x[par], pre[par])

    @pl.when(i == tiles)
    def _():
        finish(pre[1])
        part = width_out // nf
        for o in range(nf):
            z_ref[:, 2 * o * part:(2 * o + 1) * part] = gs_ref[:, o * part:(o + 1) * part] * sc_ref[4:4 + 1, 0:1]
            z_ref[:, (2 * o + 1) * part:(2 * o + 2) * part] = gb_ref[:, o * part:(o + 1) * part]


def backward_kernel(nd, nf, e_ref, s_ref, z_ref, raw_ref, t_ref, sc_ref, wh_in, w8_in, wl_in, gh_in, g8_in, gl_in,
                    th_in, t8_in, tl_in, gw_out, sm_out, fr_out,
                    wh, w8, wl, gh, g8, gl, th, t8, tl, s1, s2, xh0, x80, xl0, xh1, x81, xl1, g0, g1, ge, gsin, et,
                    gw, sm, gf, ra, rb, rc, r1, r2,
                    load, a_s, a_r, b_s, b_r, c_s, c_r, d_s, d_r, e_s, e_r, f_s, f_r, u_s, u_r, v_s, v_r, y_s, y_r):
    members, width_in = s_ref.shape
    rows = gh.shape[0]
    count = e_ref.shape[0]
    chunks = width_in // CHUNK
    per = chunks // nf
    nchip = nd // 2
    half, blk, sblk = CHUNK // 2, CHUNK // nd, sm.shape[1] // nd
    feats = CHUNK // 16
    flocal = fr_out.shape[1]
    me, z = lax.axis_index("dp"), lax.axis_index("feat")
    core, chip = lax.rem(me, 2), me // 2
    partner = me + 1 - 2 * core

    loads = [pltpu.make_async_copy(i, o, load.at[k]) for k, (i, o) in enumerate(
        ((th_in, th), (t8_in, t8), (tl_in, tl), (wh_in, wh), (w8_in, w8), (wl_in, wl), (gh_in, gh), (g8_in, g8), (gl_in, gl)))]
    for copy in loads:
        copy.start()

    greet([{"dp": lax.rem(me + o, nd)} for o in range(1, nd)] + [{"feat": lax.rem(z + o, nf)} for o in range(1, nf)])

    def aligned(i, n):
        return pl.ds(pl.multiple_of(i, n), n)

    def place(i):
        return lax.rem(i, nf) * per + i // nf

    def owner(i):
        return lax.rem(i, nf)

    def send_a(i):
        return send(gw.at[aligned(place(i) * CHUNK + (1 - core) * half, half)], ra.at[i], a_s.at[i], a_r.at[i], dp=partner)

    def send_b(i, o):
        to = lax.rem(chip + o, nchip)
        return send(gw.at[aligned(place(i) * CHUNK + core * half + to * blk, blk)], rb.at[i, o - 1], b_s.at[i, o - 1],
                    b_r.at[i, o - 1], dp=2 * to + core)

    def mine(i):
        return aligned(place(i) * CHUNK + core * half + chip * blk, blk)

    def send_c(i, k):
        j = i // nf
        return send(gw.at[mine(i)], rc.at[j, k - 1], c_s.at[i], c_r.at[j, k - 1], feat=owner(i))

    def home(i, q):
        return aligned((i // nf) * CHUNK + core * half + q * blk, blk)

    def send_d(i, o, q):
        j = i // nf
        return send(gw.at[mine(i)], gw_out.at[home(i, q)], d_s.at[j, o - 1], d_r.at[j, o - 1],
                    dp=2 * lax.rem(chip + o, nchip) + core)

    def send_e(i, side):
        j = i // nf
        r = aligned(j * CHUNK + side * half, half)
        return send(gw_out.at[r], gw_out.at[r], e_s.at[j], e_r.at[j], dp=partner)

    def far(i):
        return lax.rem(owner(i) - z + nf, nf)

    def step_b(i):
        send_a(i).wait_recv()
        gw[aligned(place(i) * CHUNK + core * half, half), :] += ra[i]
        for o in range(1, nchip):
            send_b(i, o).start()

    def step_c(i):
        for o in range(1, nchip):
            send_b(i, o).wait_recv()
        total = gw[mine(i), :]
        for o in range(1, nchip):
            total = total + rb[i, o - 1]
        gw[mine(i), :] = total

        @pl.when(owner(i) != z)
        def _():
            send_c(i, far(i)).start()

    def step_d(i):
        @pl.when(owner(i) == z)
        def _():
            total = gw[mine(i), :]
            for k in range(1, nf):
                send_c(i, k).wait_recv()
                total = total + rc[i // nf, k - 1]
            gw[mine(i), :] = total
            gw_out[home(i, chip), :] = total
            for o in range(1, nchip):
                send_d(i, o, chip).start()

    def step_e(i):
        @pl.when(owner(i) == z)
        def _():
            for o in range(1, nchip):
                send_d(i, o, lax.rem(chip - o + nchip, nchip)).wait_recv()
            send_e(i, core).start()

    def step_f(i):
        @pl.when(owner(i) == z)
        def _():
            send_e(i, 1 - core).wait_recv()

    def drain(i):
        send_a(i).wait_send()
        for o in range(1, nchip):
            send_b(i, o).wait_send()

        @pl.when(owner(i) != z)
        def _():
            send_c(i, far(i)).wait_send()

        @pl.when(owner(i) == z)
        def _():
            for o in range(1, nchip):
                send_d(i, o, chip).wait_send()
            send_e(i, core).wait_send()

    def send_u(i, o):
        to = lax.rem(me + o, nd)
        return send(sm.at[i, aligned(to * sblk, sblk)], r1.at[i, o - 1], u_s.at[i, o - 1], u_r.at[i, o - 1], dp=to)

    def send_v(i, k):
        j = i // nf
        return send(sm.at[i, aligned(me * sblk, sblk)], r2.at[j, k - 1], v_s.at[i], v_r.at[j, k - 1], feat=owner(i))

    def send_y(i, o, q):
        j = i // nf
        return send(sm.at[i, aligned(me * sblk, sblk)], sm_out.at[j, aligned(q * sblk, sblk)], y_s.at[j, o - 1], y_r.at[j, o - 1],
                    dp=lax.rem(me + o, nd))

    def send_f(i, k, src):
        j = i // nf
        return send(gf.at[i], fr_out.at[src, aligned(j * feats, feats)], f_s.at[i], f_r.at[j, k - 1], feat=owner(i))

    def start_u(i):
        for o in range(1, nd):
            send_u(i, o).start()

        @pl.when(owner(i) != z)
        def _():
            send_f(i, far(i), z).start()

        @pl.when(owner(i) == z)
        def _():
            fr_out[z, aligned((i // nf) * feats, feats), :] = gf[i]

    def step_v(i):
        r = aligned(me * sblk, sblk)
        for o in range(1, nd):
            send_u(i, o).wait_recv()
        total = sm[i, r, :]
        for o in range(1, nd):
            total = total + r1[i, o - 1]
        sm[i, r, :] = total

        @pl.when(owner(i) != z)
        def _():
            send_v(i, far(i)).start()

    def step_y(i):
        @pl.when(owner(i) == z)
        def _():
            r = aligned(me * sblk, sblk)
            total = sm[i, r, :]
            for k in range(1, nf):
                send_v(i, k).wait_recv()
                total = total + r2[i // nf, k - 1]
            sm[i, r, :] = total
            sm_out[i // nf, r, :] = total
            for o in range(1, nd):
                send_y(i, o, me).start()

    def step_w(i):
        @pl.when(owner(i) == z)
        def _():
            for o in range(1, nd):
                send_y(i, o, lax.rem(me - o + nd, nd)).wait_recv()
            for k in range(1, nf):
                send_f(i, k, lax.rem(z - k + nf, nf)).wait_recv()

    def drain_small(i):
        for o in range(1, nd):
            send_u(i, o).wait_send()

        @pl.when(owner(i) != z)
        def _():
            send_v(i, far(i)).wait_send()
            send_f(i, far(i), z).wait_send()

        @pl.when(owner(i) == z)
        def _():
            for o in range(1, nd):
                send_y(i, o, me).wait_send()

    def when_chunk(i, f):
        @pl.when((i >= 0) & (i < chunks))
        def _():
            f(i)

    def early(j):
        for i in (2 * j, 2 * j + 1):
            send_a(i).start()
        for i in (2 * j - 2, 2 * j - 1):
            when_chunk(i, step_b)
        for i in (2 * j - 6, 2 * j - 5):
            when_chunk(i, step_c)

    def late(t):
        @pl.when(t == 0)
        def _():
            for i in range(chunks - 2, chunks):
                step_b(i)

        @pl.when((t >= 1) & (t < chunks - 1))
        def _():
            step_c(t + 1)

        when_chunk(t - 1, step_d)
        when_chunk(t - 2, step_e)
        when_chunk(t - 3, step_f)
        when_chunk(t - 1, start_u)
        when_chunk(t - 2, step_v)
        when_chunk(t - 3, step_y)
        when_chunk(t - 4, step_w)

    x = ((xh0, x80, xl0), (xh1, x81, xl1))
    gt = (th, t8, tl)
    s1[...] = s_ref[...] * sc_ref[0:0 + 1, 0:1]
    s2[...] = s_ref[...] * sc_ref[6:6 + 1, 0:1]

    def cols(i):
        return aligned(place(i) * CHUNK, CHUNK)

    def prepare(i, to):
        for n in range(0, count, TILE):
            v = (e_ref[n:n + TILE, cols(i)][:, None, :] * s1[:, cols(i)][None]).reshape(TILE * members, CHUNK)
            r = slice(n * members, (n + TILE) * members)
            to[0][r, :], to[1][r, :], to[2][r, :] = split3(v)

    prepare(0, x[0])
    for copy in loads[:3]:
        copy.wait()

    def weights(j, carry):
        for par in (0, 1):
            i = 2 * j + par
            r = product([t[...] for t in gt], [t[...] for t in x[par]], dot)
            gw[cols(i), :] = r.T * sc_ref[5:5 + 1, 0:1]
            prepare(jnp.minimum(i + 1, chunks - 1), x[1 - par])
        early(j)
        return carry

    lax.fori_loop(0, chunks // 2, weights, 0)

    for copy in loads[3:]:
        copy.wait()
    gsin[...] = jnp.zeros_like(gsin)
    g1[...] = jnp.zeros_like(g1)
    step = g0.shape[0]
    objs = step // members
    parts = rows // step

    def finish(i, t, g):
        g3 = g[...].reshape(objs, members, CHUNK)
        ns = slice(t * objs, (t + 1) * objs)
        ge[ns, :] = jnp.sum(g3 * s2[:, cols(i)][None], axis=1)
        gsin[...] += jnp.sum(g3 * e_ref[ns, cols(i)][:, None, :], axis=0)

    def table(i):
        c = place(i)
        first = c * feats
        base = (first // flocal) * (3 * flocal) + lax.rem(first, flocal)
        for j in range(CHUNK // 128):
            et[j * 128:(j + 1) * 128, :] = ge[:, j * 128:(j + 1) * 128].T
        lane = lax.broadcasted_iota(jnp.int32, (16, 128), 1)
        level = lax.broadcasted_iota(jnp.int32, (64, 128), 0).astype(F32)
        for p in range(feats // 2):
            row = base + 2 * p
            lh, ll = split2(table_pair(t_ref, c * (feats // 2) + p))
            enc = encode_pair(raw_ref, flocal, row)
            g = et[p * 32:(p + 1) * 32, :]
            gh_, gl_ = split2(g)
            eh, el = split2(enc)
            both = dot_nt(jnp.concatenate([gh_, gl_], axis=0), eh)
            full = both[:32] + both[32:] + dot_nt(gh_, el)
            sm[i, p * 16:(p + 1) * 16, :] = jnp.where(lane < 64, full[:16], full[16:])
            hot = []
            for f in (row, row + 1):
                here = 1.0 - raw_ref[pl.ds(f + 2 * flocal, 1), :]
                hot.append(jnp.where(level == raw_ref[pl.ds(f, 1), :], here, 0.0))
            one = jnp.concatenate(hot, axis=0).astype(BF16)
            both = dot(jnp.concatenate([lh, ll], axis=0), one)
            picked = (both[:32] + both[32:]) * g
            gf[i, 2 * p:2 * p + 1, :] = jnp.sum(picked[:16], axis=0, keepdims=True)
            gf[i, 2 * p + 1:2 * p + 2, :] = jnp.sum(picked[16:], axis=0, keepdims=True)
        at = feats * 8
        for j in range(CHUNK // 128):
            sm[i, at:at + members, :] = gsin[:, j * 128:(j + 1) * 128] * sc_ref[7:7 + 1, 0:1]
            at += members
        sm[i, at:at + members, :] = z_ref[:, aligned(c * 128, 128)]
        at += members
        sm[i, at:, :] = jnp.zeros_like(sm[i, at:, :])
        gsin[...] = jnp.zeros_like(gsin)

    def inputs(i, carry):
        before = jnp.maximum(i - 1, 0)
        wc = [t[cols(i), :] for t in (wh, w8, wl)]
        finish(before, parts - 1, g1)
        table(before)
        for t in range(parts):
            to, fro = (g0, g1) if t % 2 == 0 else (g1, g0)
            rs = slice(t * step, (t + 1) * step)
            to[...] = product([r[rs, :] for r in (gh, g8, gl)], wc, dot_nt)
            if t > 0:
                finish(i, t - 1, fro)
        late(i)
        return carry

    lax.fori_loop(0, chunks, inputs, 0)
    last = chunks - 1
    finish(last, parts - 1, g1)
    table(last)
    start_u(last)
    step_v(last - 1)
    step_y(last - 2)
    step_w(last - 3)
    step_d(last)
    step_e(last - 1)
    step_f(last - 2)
    step_v(last)
    step_y(last - 1)
    step_w(last - 2)
    step_e(last)
    step_f(last - 1)
    step_y(last)
    step_w(last - 1)
    step_f(last)

    def close(i, carry):
        drain(i)
        drain_small(i)
        return carry

    lax.fori_loop(0, chunks, close, 0)
    step_w(last)


def final_kernel(nf, bins, gw_ref, sm_ref, fr_ref, frac_ref, tab_ref, bias_ref, miss_ref, sin_ref, gw_out, so_ref, bo_ref):
    gw_out[...] = gw_ref[...]
    flocal = fr_ref.shape[1]
    for o in range(nf):
        frac_ref[:, o * 128:(o + 1) * 128] = fr_ref[o]
    members = sin_ref.shape[0]
    feats = CHUNK // 16
    width = so_ref.shape[1]
    small = []
    for j in range(sm_ref.shape[0]):
        for p in range(feats // 2):
            block = sm_ref[j, p * 16:(p + 1) * 16, :]
            for odd in (0, 1):
                f = j * feats + 2 * p + odd
                tab_ref[f] = block[:, odd * 64:odd * 64 + bins]
                bias_ref[:, f:f + 1] = block[:, odd * 64 + bins:odd * 64 + bins + 1]
                miss_ref[:, f:f + 1] = block[:, odd * 64 + bins + 1:odd * 64 + bins + 2]
        at = feats * 8
        for q in range(CHUNK // 128):
            sin_ref[:, j * CHUNK + q * 128:j * CHUNK + (q + 1) * 128] = sm_ref[j, at:at + members, :]
            at += members
        small.append(sm_ref[j, at:at + members, :])
    small = small[0] if len(small) == 1 else jnp.concatenate(small, axis=1)
    so_ref[...] = small[:, :width]
    bo_ref[...] = small[:, width:]


def params(**kw):
    return pltpu.CompilerParams(vmem_limit_bytes=VMEM_LIMIT, **kw)


def whole(shape):
    return pl.BlockSpec(shape, lambda *_: (0,) * len(shape))


def exchange(nf, bins, fr, ms, tab, bias, miss, s, so, w, ct):
    flocal, total = bins.shape
    width = tab.shape[1]
    count, (din, dout) = total // nf, w.shape
    parts = 8
    ins = (bins, fr, ms, tab, bias, miss, s, so)
    shapes = [jax.ShapeDtypeStruct(x, F32) for x in ((nf * 3 * flocal, count), (nf * flocal // 2 * width, 128), (count, din), (8, 128))]
    far = [jax.ShapeDtypeStruct(w.shape, d) for d in (BF16, F8, F8)]
    dma = pltpu.SemaphoreType.DMA
    anywhere = pl.BlockSpec(memory_space=pl.ANY)
    return pl.pallas_call(
        functools.partial(exchange_kernel, nf),
        out_shape=shapes + far,
        in_specs=[whole(x.shape) for x in ins] + [anywhere] * 2,
        out_specs=[whole(x.shape) for x in shapes] + [anywhere] * 3,
        scratch_shapes=[pltpu.VMEM((3 * flocal, total), F32), pltpu.VMEM((din, count), F32), pltpu.VMEM(w.shape, F32),
                        pltpu.VMEM((parts, ct.shape[0] // parts) + ct.shape[1:], F32)]
        + [pltpu.VMEM(x.shape, x.dtype) for x in far]
        + [dma((parts + 1,)), dma((3,))] + [dma((nf - 1,))] * 4,
        compiler_params=params(collective_id=0, has_side_effects=True),
    )(*ins, w, ct)


def forward(nf, e, s, wp, so, bo, ct, sc):
    count, din = e.shape
    members, dout = so.shape
    rows, tiles, block = count * members, count // TILE, TILE * members
    lag = lambda i: jnp.maximum(i - 1, 0)
    big = pl.BlockSpec((TILE, members, dout), lambda i: (lag(i), 0, 0))
    nat = pl.BlockSpec((block, dout), lambda i: (lag(i), 0))
    tra = pl.BlockSpec((dout, block), lambda i: (0, lag(i)))
    return pl.pallas_call(
        functools.partial(forward_kernel, nf),
        out_shape=[jax.ShapeDtypeStruct((count, members, dout), F32)]
        + [jax.ShapeDtypeStruct((rows, dout), d) for d in (BF16, F8, F8)]
        + [jax.ShapeDtypeStruct((dout, rows), d) for d in (BF16, F8, F8)]
        + [jax.ShapeDtypeStruct((members, 2 * dout), F32)],
        grid=(tiles + 1,),
        in_specs=[whole(e.shape), whole(s.shape)] + [whole(w.shape) for w in wp] + [whole(so.shape), whole(bo.shape), big, whole(sc.shape)],
        out_specs=[big, nat, nat, nat, tra, tra, tra, whole((members, 2 * dout))],
        scratch_shapes=[pltpu.VMEM(so.shape, F32)] * 2 + [pltpu.VMEM(s.shape, F32), pltpu.VMEM(so.shape, F32), pltpu.VMEM(so.shape, F32)]
        + [pltpu.VMEM((block, din), d) for d in (BF16, F8, F8)] * 2
        + [pltpu.VMEM((block, dout), F32)] * 2,
        compiler_params=params(),
    )(e, s, *wp, so, bo, ct, sc)


def backward(nd, nf, e, s, zs, raw, t, wp, gp, gt, sc):
    count, din = e.shape
    members = s.shape[0]
    rows, dout = gp[0].shape
    step = rows // 4
    chunks, nchip = din // CHUNK, nd // 2
    per = chunks // nf
    half, blk, sblk = CHUNK // 2, CHUNK // nd, 256 // nd
    feats, flocal = CHUNK // 16, raw.shape[0] // (3 * nf)
    shapes = [jax.ShapeDtypeStruct(x, F32) for x in ((din // nf, dout), (per, 256, 128), (nf, flocal, 128))]
    ins = (e, s, zs, raw, t)
    far = (*wp, *gp, *gt)
    dma = pltpu.SemaphoreType.DMA
    f32 = lambda *shape: pltpu.VMEM(shape, F32)
    return pl.pallas_call(
        functools.partial(backward_kernel, nd, nf),
        out_shape=shapes,
        in_specs=[whole(x.shape) for x in ins] + [whole(sc.shape)] + [pl.BlockSpec(memory_space=pl.ANY)] * len(far),
        out_specs=[whole(x.shape) for x in shapes],
        scratch_shapes=[pltpu.VMEM(x.shape, x.dtype) for x in far]
        + [f32(*s.shape)] * 2
        + [pltpu.VMEM((rows, CHUNK), d) for d in (BF16, F8, F8)] * 2
        + [f32(step, CHUNK)] * 2
        + [f32(count, CHUNK), f32(members, CHUNK), f32(CHUNK, count)]
        + [f32(din, dout), f32(chunks, 256, 128), f32(chunks, feats, count)]
        + [f32(chunks, half, dout), f32(chunks, nchip - 1, blk, dout), f32(per, nf - 1, blk, dout)]
        + [f32(chunks, nd - 1, sblk, 128), f32(per, nf - 1, sblk, 128)]
        + [dma((9,))]
        + [dma((chunks,))] * 2 + [dma((chunks, nchip - 1))] * 2 + [dma((chunks,)), dma((per, nf - 1))]
        + [dma((per, nchip - 1))] * 2 + [dma((per,))] * 2 + [dma((chunks,)), dma((per, nf - 1))]
        + [dma((chunks, nd - 1))] * 2 + [dma((chunks,)), dma((per, nf - 1))] + [dma((per, nd - 1))] * 2,
        compiler_params=params(collective_id=1, has_side_effects=True),
    )(*ins, sc, *far)


def final(nf, bins, gw, sm, fr):
    per, flocal = sm.shape[0], fr.shape[1]
    members, width = 32, gw.shape[1] // nf
    shapes = [jax.ShapeDtypeStruct(x, F32) for x in (
        (flocal, nf * 128), (flocal, 16, bins), (16, flocal), (16, flocal), (members, per * CHUNK), gw.shape, (members, width), (members, width))]
    ins = (gw, sm, fr)
    return pl.pallas_call(functools.partial(final_kernel, nf, bins), out_shape=shapes, in_specs=[whole(x.shape) for x in ins],
                          out_specs=[whole(x.shape) for x in shapes], compiler_params=params())(*ins)


def shards(nd, nf, bins, fractions, missing, bin_table, bin_bias, miss_vector, scale_in, weight, scale_out, bias_out, cotangent):
    raw, packed, e, sc, *wp = exchange(nf, bins.T, fractions.T, missing.T, jnp.transpose(bin_table, (0, 2, 1)), bin_bias.T,
                                       miss_vector.T, scale_in, scale_out, weight, cotangent)
    hidden, *rest = forward(nf, e, scale_in, wp, scale_out, bias_out, cotangent, sc)
    gw, sm, fr = backward(nd, nf, e, scale_in, rest[6], raw, packed, wp, rest[:3], rest[3:6], sc)
    frac, table, bias, miss, sin, gw, so, bo = final(nf, bin_table.shape[1], gw, sm, fr)
    return hidden, frac.T, jnp.transpose(table, (0, 2, 1)), bias.T, miss.T, sin, gw, so, bo


def solution(mesh):
    placed = (P("dp", "feat"), P("dp", "feat"), P("dp", "feat"), P("feat", None, None), P("feat", None), P("feat", None),
              P(), P(), P(), P(), P(("dp", "feat"), None, None))
    return jax.shard_map(
        functools.partial(shards, mesh.shape["dp"], mesh.shape["feat"]),
        mesh=mesh,
        in_specs=placed,
        out_specs=(P(("dp", "feat"), None, None), P("dp", "feat"), P("feat", None, None), P("feat", None), P("feat", None),
                   P(None, "feat"), P("feat", None), P(None, "feat"), P(None, "feat")),
        check_vma=False,
    )
```

```python
import functools

import jax
import jax.numpy as jnp
from jax import lax
from jax.experimental import pallas as pl
from jax.experimental.pallas import tpu as pltpu
from jax.sharding import PartitionSpec as P

F32, BF16, F8 = jnp.float32, jnp.bfloat16, jnp.float8_e4m3fn
VMEM_LIMIT = 63 << 20
TILE = 16
DIRECT = 2
CHUNK = 256
TOP = 224.0
LO = 256.0
GELU_A = 0.7978845608028654
GELU_B = GELU_A * 0.044715


def dot(a, b):
    return jnp.dot(a, b, preferred_element_type=F32)


def dot_nt(a, b):
    return lax.dot_general(a, b, (((1,), (1,)), ((), ())), preferred_element_type=F32)


def split3(x):
    hi = x.astype(BF16)
    return hi, x.astype(F8), ((x - hi.astype(F32)) * LO).astype(F8)


def split2(x):
    hi = x.astype(BF16)
    return hi, (x - hi.astype(F32)).astype(BF16)


def product(a, b, mul):
    ah, a8, al = a
    bh, b8, bl = b
    return mul(ah, bh) + (mul(a8, bl) + mul(al, b8)) * (1.0 / LO)


def encode_pair(raw_ref, flocal, first):
    level = lax.broadcasted_iota(jnp.int32, (48, 128), 0).astype(F32)
    row = lax.broadcasted_iota(jnp.int32, (16, 128), 0)
    parts = []
    for f in (first, first + 1):
        b, fr, m = [raw_ref[pl.ds(f + k * flocal, 1), :] for k in range(3)]
        here = 1.0 - m
        parts.append(jnp.clip((b - level) + fr, 0.0, 1.0) * here)
        parts.append(jnp.where(row == 0, here, jnp.where(row == 1, m, 0.0)))
    return jnp.concatenate(parts, axis=0)


def table_pair(t_ref, p):
    blk = t_ref[pl.ds(pl.multiple_of(p * 16, 16), 16), :]
    lane = lax.broadcasted_iota(jnp.int32, (16, 128), 1)
    zero = jnp.zeros_like(blk)
    return jnp.concatenate([jnp.where(lane < 64, blk, zero), jnp.where(lane < 64, zero, blk)], axis=0)


def send(src, dst, ssem, rsem, **where):
    return pltpu.make_async_remote_copy(src_ref=src, dst_ref=dst, send_sem=ssem, recv_sem=rsem, device_id=where,
                                        device_id_type=pl.DeviceIdType.MESH)


def greet(partners):
    barrier = pltpu.get_barrier_semaphore()
    for where in partners:
        pl.semaphore_signal(barrier, inc=1, device_id=where, device_id_type=pl.DeviceIdType.MESH)
    return lambda: pl.semaphore_wait(barrier, len(partners))


def exchange_kernel(nd, nf, bins_ref, fr_ref, ms_ref, tab_ref, bias_ref, miss_ref, s_ref, so_ref, w_in, ct_in,
                    raw_ref, t_ref, e_ref, sc_ref, wh_out, w8_out, wl_out,
                    mine, et, w, ct, wh, w8, wl, load, store, r_s, r_r, x_s, x_r, y_s, y_r, z_s, z_r):
    flocal, total = bins_ref.shape
    count = total // nf
    bins, width = tab_ref.shape[2], tab_ref.shape[1]
    me, z = lax.axis_index("dp"), lax.axis_index("feat")
    nchip = nd // 2
    core, chip = lax.rem(me, 2), me // 2
    partner = me + 1 - 2 * core
    parts = ct.shape[0]
    step = ct_in.shape[0] // parts

    ready = greet([{"feat": lax.rem(z + o, nf)} for o in range(1, nf)]
                  + [{"dp": 2 * lax.rem(chip + o, nchip) + core} for o in range(1, nchip)] + [{"dp": partner}])
    loads = [pltpu.make_async_copy(w_in, w, load.at[0])] + [
        pltpu.make_async_copy(ct_in.at[pl.ds(i * step, step)], ct.at[i], load.at[i + 1]) for i in range(parts)]
    for copy in loads:
        copy.start()

    def rows(q):
        return pl.ds(pl.multiple_of(q * (3 * flocal), 3 * flocal), 3 * flocal)

    size = flocal // 2 * width // nd

    def entries(q, piece, n):
        return t_ref.at[pl.ds(pl.multiple_of(q * (nd * size) + piece * size, 8), n * size)]

    mine[0:flocal, :] = bins_ref[...].astype(F32)
    mine[flocal:2 * flocal, :] = fr_ref[...]
    mine[2 * flocal:, :] = ms_ref[...].astype(F32)
    raw_ref[rows(z), :] = mine[:, pl.ds(pl.multiple_of(z * count, count), count)]
    blank = jnp.zeros((width, 64 - bins - 2), F32)
    for p in range(flocal // 2):
        block = []
        for f in (2 * p, 2 * p + 1):
            block += [tab_ref[f], bias_ref[:, f:f + 1], miss_ref[:, f:f + 1], blank]
        t_ref[pl.ds(pl.multiple_of(z * (flocal // 2 * width) + p * width, width), width), :] = jnp.concatenate(block, axis=1)

    def send_raw(o, q):
        to = lax.rem(z + o, nf)
        return send(mine.at[:, pl.ds(pl.multiple_of(to * count, count), count)], raw_ref.at[rows(q)],
                    r_s.at[o - 1], r_r.at[o - 1], feat=to)

    def send_x(o, q):
        r = entries(q, core * nchip + chip, 1)
        return send(r, r, x_s.at[o - 1], x_r.at[o - 1], feat=lax.rem(z + o, nf))

    def send_y(o, k, c):
        r = entries(lax.rem(z - o + nf, nf), core * nchip + c, 1)
        return send(r, r, y_s.at[o - 1, k - 1], y_r.at[o - 1, k - 1], dp=2 * lax.rem(chip + k, nchip) + core)

    def send_z(o, side):
        r = entries(lax.rem(z - o + nf, nf), side * nchip, nchip)
        return send(r, r, z_s.at[o - 1], z_r.at[o - 1], dp=partner)

    others = range(1, nf)
    ready()
    for o in others:
        send_x(o, z).start()
    for o in others:
        send_raw(o, z).start()

    def top(v):
        return jnp.maximum(jnp.max(jnp.max(jnp.abs(v), axis=0, keepdims=True), axis=1, keepdims=True), 1e-30)

    at_once = 8
    pairs = flocal // 2
    entries_local = flocal * width

    def embed(q):
        def body(j, c):
            for k in range(at_once):
                p = q * pairs + j * at_once + k
                first = q * (3 * flocal) + 2 * (j * at_once + k)
                lh, ll = split2(table_pair(t_ref, p))
                eh, el = split2(encode_pair(raw_ref, flocal, first))
                both = dot(jnp.concatenate([lh, ll], axis=0), eh)
                et[pl.ds(pl.multiple_of(p * 32, 32), 32), :] = both[:32] + both[32:] + dot(lh, el)
            return c

        lax.fori_loop(0, pairs // at_once, body, 0)
        for j in range(entries_local // 128):
            at = pl.ds(pl.multiple_of(q * entries_local + j * 128, 128), 128)
            e_ref[:, at] = et[at, :].T

    embed(z)
    for o in others:
        send_x(o, lax.rem(z - o + nf, nf)).wait_recv()
        for k in range(1, nchip):
            send_y(o, k, chip).start()

    loads[0].wait()
    sw = TOP / top(w[...])
    for i in range(0, w.shape[0], 256):
        r = slice(i, i + 256)
        wh[r, :], w8[r, :], wl[r, :] = split3(w[r, :] * sw)
    stores = [pltpu.make_async_copy(i, o, store.at[k]) for k, (i, o) in enumerate(((wh, wh_out), (w8, w8_out), (wl, wl_out)))]
    for copy in stores:
        copy.start()

    for o in others:
        for k in range(1, nchip):
            send_y(o, k, lax.rem(chip - k + nchip, nchip)).wait_recv()
        send_z(o, core).start()
    tc = jnp.full((1, 1), 1e-30, F32)
    for i in range(parts):
        loads[i + 1].wait()
        tc = jnp.maximum(tc, top(ct[i].reshape(-1, ct.shape[-1])))
    for o in others:
        q = lax.rem(z - o + nf, nf)
        send_z(o, 1 - core).wait_recv()
        send_raw(o, q).wait_recv()
        embed(q)
    sx = TOP / (top(et[...]) * top(s_ref[...]))
    sg = TOP / (1.2 * tc * top(so_ref[...]))
    for k, v in enumerate((sx, sw, sg, 1.0 / (sx * sw), 1.0 / (sx * sw), 1.0 / (sg * sx), 1.0 / (sg * sw), 1.0 / (sg * sw))):
        sc_ref[k:k + 1, :] = jnp.broadcast_to(v, (1, 128))
    for copy in stores:
        copy.wait()
    for o in others:
        send_raw(o, z).wait_send()
        send_x(o, z).wait_send()
        for k in range(1, nchip):
            send_y(o, k, chip).wait_send()
        send_z(o, core).wait_send()


def forward_kernel(nf, e_ref, s_ref, wh_ref, w8_ref, wl_ref, so_ref, bo_ref, ct_ref, sc_ref,
                   hid_ref, gh_ref, g8_ref, gl_ref, th_ref, t8_ref, tl_ref, z_ref,
                   gs_ref, gb_ref, s1, so1, so2, xh0, x80, xl0, xh1, x81, xl1, pre0, pre1):
    i = pl.program_id(0)
    tiles = pl.num_programs(0) - 1
    members, width_out = so_ref.shape
    rows = TILE * members
    x = ((xh0, x80, xl0), (xh1, x81, xl1))
    pre = (pre0, pre1)
    w = (wh_ref, w8_ref, wl_ref)

    def prepare(tile, to):
        for n in range(TILE):
            v = s1[...] * e_ref[pl.ds(tile * TILE + n, 1), :]
            r = slice(n * members, (n + 1) * members)
            to[0][r, :], to[1][r, :], to[2][r, :] = split3(v)

    def multiply(a, to):
        to[...] = product([r[...] for r in a], [r[...] for r in w], dot)

    def finish(p):
        for h0 in range(0, width_out, 128):
            hs = slice(h0, h0 + 128)
            sa, sb, bo = so1[:, hs], so2[:, hs], bo_ref[:, hs]
            gs, gb = gs_ref[:, hs], gb_ref[:, hs]
            for n in range(TILE):
                r = slice(n * members, (n + 1) * members)
                q = p[r, hs]
                v = q * sa + bo
                v2 = v * v
                half = 0.5 + 0.5 * jnp.tanh(v * (GELU_B * v2 + GELU_A))
                hid = v * half
                hid_ref[n, :, hs] = hid
                g = half + hid * (1.0 - half) * ((6.0 * GELU_B) * v2 + 2.0 * GELU_A)
                ga = ct_ref[n, :, hs] * g
                gs = gs + ga * q
                gb = gb + ga
                gh_ref[r, hs], g8_ref[r, hs], gl_ref[r, hs] = split3(ga * sb)
            gs_ref[:, hs], gb_ref[:, hs] = gs, gb
        th_ref[...] = gh_ref[...].T
        t8_ref[...] = g8_ref[...].T
        tl_ref[...] = gl_ref[...].T

    @pl.when(i == 0)
    def _():
        s1[...] = s_ref[...] * sc_ref[0:0 + 1, 0:1]
        so1[...] = so_ref[...] * sc_ref[3:3 + 1, 0:1]
        so2[...] = so_ref[...] * sc_ref[2:2 + 1, 0:1]
        gs_ref[...] = jnp.zeros_like(gs_ref)
        gb_ref[...] = jnp.zeros_like(gb_ref)
        prepare(0, x[0])
        multiply(x[0], pre[0])
        prepare(1, x[1])

    for par in (0, 1):
        @pl.when((i > 0) & (i < tiles) & (i % 2 == par))
        def _():
            finish(pre[1 - par])
            prepare(jnp.minimum(i + 1, tiles - 1), x[1 - par])
            multiply(x[par], pre[par])

    @pl.when(i == tiles)
    def _():
        finish(pre[1])
        part = width_out // nf
        for o in range(nf):
            z_ref[:, 2 * o * part:(2 * o + 1) * part] = gs_ref[:, o * part:(o + 1) * part] * sc_ref[4:4 + 1, 0:1]
            z_ref[:, (2 * o + 1) * part:(2 * o + 2) * part] = gb_ref[:, o * part:(o + 1) * part]


def backward_kernel(nd, nf, e_ref, s_ref, z_ref, raw_ref, t_ref, sc_ref, wh_in, w8_in, wl_in, gh_in, g8_in, gl_in,
                    th_in, t8_in, tl_in, gw_out, sm_out, fr_out,
                    wh, w8, wl, gh, g8, gl, th, t8, tl, s1, s2, xh0, x80, xl0, xh1, x81, xl1, g0, g1, ge, gsin, et,
                    gw, sm, gf, ra, rp, rq, rp2, rq2, rc, ru, rb, r1, r2,
                    load, a_s, a_r, p_s, p_r, q_s, q_r, p2_s, p2_r, q2_s, q2_r, c_s, c_r, d_s, d_r, e_s, e_r, f_s, f_r,
                    ua_s, ua_r, ub_s, ub_r, uc_s, uc_r, ud_s, ud_r, ue_s, ue_r, u_s, u_r, y_s, y_r):
    members, width_in = s_ref.shape
    rows = gh.shape[0]
    count = e_ref.shape[0]
    chunks = width_in // CHUNK
    direct = chunks - DIRECT
    per = chunks // nf
    nx, ny, nchip = 2, nd // 4, nd // 2
    blk, dout = gw.shape[4], gw.shape[5]
    half, sblk = sm.shape[1] // 2, sm.shape[1] // nd
    feats = CHUNK // 16
    flocal = fr_out.shape[1]
    me, z = lax.axis_index("dp"), lax.axis_index("feat")
    core, chip = lax.rem(me, 2), me // 2
    cx, cy = lax.rem(chip, nx), chip // nx
    partner = me + 1 - 2 * core

    ready = greet([{"dp": lax.rem(me + o, nd)} for o in range(1, nd)] + [{"feat": lax.rem(z + o, nf)} for o in range(1, nf)])
    loads = [pltpu.make_async_copy(i, o, load.at[k]) for k, (i, o) in enumerate(
        ((th_in, th), (t8_in, t8), (tl_in, tl), (wh_in, wh), (w8_in, w8), (wl_in, wl), (gh_in, gh), (g8_in, g8), (gl_in, gl)))]
    for copy in loads:
        copy.start()

    def aligned(i, n):
        return pl.ds(pl.multiple_of(i, n), n)

    def place(i):
        return lax.rem(i, nf) * per + i // nf

    def owner(i):
        return lax.rem(i, nf)

    def far(i):
        return lax.rem(owner(i) - z + nf, nf)

    def device(y, x):
        return 2 * (y * nx + x) + core

    def other_y(k):
        return lax.rem(cy + k, ny)

    def from_y(k):
        return lax.rem(cy - k + ny, ny)

    def own(i):
        return 2 * place(i) + core

    def send_a(i):
        return send(gw.at[2 * place(i) + 1 - core], ra.at[i], a_s.at[i], a_r.at[i], dp=partner)

    def send_p(i):
        return send(gw.at[own(i), :, 1 - cx, 0], rp.at[i], p_s.at[i], p_r.at[i], dp=device(cy, 1 - cx))

    def send_q(i, k):
        return send(gw.at[own(i), other_y(k), :, 1], rq.at[i, k - 1], q_s.at[i, k - 1], q_r.at[i, k - 1], dp=device(other_y(k), cx))

    def send_p2(i, k):
        return send(gw.at[own(i), other_y(k), cx, 0], rp2.at[i, k - 1], p2_s.at[i, k - 1], p2_r.at[i, k - 1], dp=device(other_y(k), cx))

    def send_q2(i):
        return send(gw.at[own(i), cy, 1 - cx, 1], rq2.at[i], q2_s.at[i], q2_r.at[i], dp=device(cy, 1 - cx))

    def send_c(i, k):
        j = i // nf
        return send(gw.at[own(i), cy, cx], rc.at[j, k - 1], c_s.at[i], c_r.at[j, k - 1], feat=owner(i))

    def send_d(i, o, q):
        j = i // nf
        return send(gw.at[own(i), cy, cx], gw_out.at[2 * j + core, q // nx, lax.rem(q, nx)], d_s.at[j, o - 1], d_r.at[j, o - 1],
                    dp=2 * lax.rem(chip + o, nchip) + core)

    def send_e(i, side):
        j = i // nf
        return send(gw_out.at[2 * j + side], gw_out.at[2 * j + side], e_s.at[j], e_r.at[j], dp=partner)

    def step_b(i):
        send_a(i).wait_recv()
        gw[own(i)] += ra[i]
        send_p(i).start()
        for k in range(1, ny):
            send_q(i, k).start()

    def step_b2(i):
        send_p(i).wait_recv()
        gw[own(i), :, cx, 0] += rp[i]
        for k in range(1, ny):
            send_q(i, k).wait_recv()
            gw[own(i), cy, :, 1] += rq[i, k - 1]
        for k in range(1, ny):
            send_p2(i, k).start()
        send_q2(i).start()

    def step_c(i):
        send_q2(i).wait_recv()
        gw[own(i), cy, cx, 1] += rq2[i]
        for k in range(1, ny):
            send_p2(i, k).wait_recv()
            gw[own(i), cy, cx, 0] += rp2[i, k - 1]

        @pl.when(owner(i) != z)
        def _():
            send_c(i, far(i)).start()

    def step_d(i):
        @pl.when(owner(i) == z)
        def _():
            total = gw[own(i), cy, cx]
            for k in range(1, nf):
                send_c(i, k).wait_recv()
                total = total + rc[i // nf, k - 1]
            gw[own(i), cy, cx] = total
            gw_out[2 * (i // nf) + core, cy, cx] = total
            for o in range(1, nchip):
                send_d(i, o, chip).start()

    def step_e(i):
        @pl.when(owner(i) == z)
        def _():
            for o in range(1, nchip):
                send_d(i, o, lax.rem(chip - o + nchip, nchip)).wait_recv()
            send_e(i, core).start()

    def step_f(i):
        @pl.when(owner(i) == z)
        def _():
            send_e(i, 1 - core).wait_recv()

    def drain(i):
        send_a(i).wait_send()
        send_p(i).wait_send()
        send_q2(i).wait_send()
        for k in range(1, ny):
            send_q(i, k).wait_send()
            send_p2(i, k).wait_send()

        @pl.when(owner(i) != z)
        def _():
            send_c(i, far(i)).wait_send()

        @pl.when(owner(i) == z)
        def _():
            for o in range(1, nchip):
                send_d(i, o, chip).wait_send()
            send_e(i, core).wait_send()

    def rows_of(q, side):
        return aligned(side * half + q * sblk, sblk)

    def whole_half(side):
        return aligned(side * half, half)

    def send_ua(i):
        return send(sm.at[i, whole_half(1 - core)], ru.at[i], ua_s.at[i], ua_r.at[i], dp=partner)

    def send_ub(i, o):
        to = lax.rem(chip + o, nchip)
        return send(sm.at[i, rows_of(to, core)], rb.at[i, o - 1], ub_s.at[i, o - 1], ub_r.at[i, o - 1], dp=2 * to + core)

    def send_uc(i, k):
        j = i // nf
        return send(sm.at[i, rows_of(chip, core)], r2.at[j, k - 1], uc_s.at[i], uc_r.at[j, k - 1], feat=owner(i))

    def send_ud(i, o, q):
        j = i // nf
        return send(sm.at[i, rows_of(chip, core)], sm_out.at[j, rows_of(q, core)], ud_s.at[j, o - 1], ud_r.at[j, o - 1],
                    dp=2 * lax.rem(chip + o, nchip) + core)

    def send_ue(i, side):
        j = i // nf
        r = sm_out.at[j, whole_half(side)]
        return send(r, r, ue_s.at[j], ue_r.at[j], dp=partner)

    def send_u(i, o):
        to = lax.rem(me + o, nd)
        return send(sm.at[i, rows_of(to // 2, lax.rem(to, 2))], r1.at[i - direct, o - 1], u_s.at[i - direct, o - 1],
                    u_r.at[i - direct, o - 1], dp=to)

    def send_y(i, o, q):
        j = i - direct
        return send(sm.at[i, rows_of(chip, core)], sm_out.at[i // nf, rows_of(q // 2, lax.rem(q, 2))], y_s.at[j, o - 1], y_r.at[j, o - 1],
                    dp=lax.rem(me + o, nd))

    def send_f(i, k, src):
        j = i // nf
        return send(gf.at[i], fr_out.at[src, aligned(j * feats, feats)], f_s.at[i], f_r.at[j, k - 1], feat=owner(i))

    def start_f(i):
        @pl.when(owner(i) != z)
        def _():
            send_f(i, far(i), z).start()

        @pl.when(owner(i) == z)
        def _():
            fr_out[z, aligned((i // nf) * feats, feats), :] = gf[i]

    def wait_f(i):
        @pl.when(owner(i) == z)
        def _():
            for k in range(1, nf):
                send_f(i, k, lax.rem(z - k + nf, nf)).wait_recv()

    def start_ua(i):
        send_ua(i).start()
        start_f(i)

    def step_ub(i):
        send_ua(i).wait_recv()
        sm[i, whole_half(core), :] += ru[i]
        for o in range(1, nchip):
            send_ub(i, o).start()

    def step_uc(i):
        r = rows_of(chip, core)
        total = sm[i, r, :]
        for o in range(1, nchip):
            send_ub(i, o).wait_recv()
            total = total + rb[i, o - 1]
        sm[i, r, :] = total

        @pl.when(owner(i) != z)
        def _():
            send_uc(i, far(i)).start()

    def gather_z(i):
        r = rows_of(chip, core)
        total = sm[i, r, :]
        for k in range(1, nf):
            send_uc(i, k).wait_recv()
            total = total + r2[i // nf, k - 1]
        sm[i, r, :] = total
        sm_out[i // nf, r, :] = total

    def step_ud(i):
        @pl.when(owner(i) == z)
        def _():
            gather_z(i)
            for o in range(1, nchip):
                send_ud(i, o, chip).start()

    def step_ue(i):
        @pl.when(owner(i) == z)
        def _():
            for o in range(1, nchip):
                send_ud(i, o, lax.rem(chip - o + nchip, nchip)).wait_recv()
            send_ue(i, core).start()

    def step_uf(i):
        @pl.when(owner(i) == z)
        def _():
            send_ue(i, 1 - core).wait_recv()

        wait_f(i)

    def drain_small(i):
        send_ua(i).wait_send()
        for o in range(1, nchip):
            send_ub(i, o).wait_send()

        @pl.when(owner(i) != z)
        def _():
            send_uc(i, far(i)).wait_send()
            send_f(i, far(i), z).wait_send()

        @pl.when(owner(i) == z)
        def _():
            for o in range(1, nchip):
                send_ud(i, o, chip).wait_send()
            send_ue(i, core).wait_send()

    def start_u(i):
        for o in range(1, nd):
            send_u(i, o).start()
        start_f(i)

    def step_v(i):
        r = rows_of(chip, core)
        total = sm[i, r, :]
        for o in range(1, nd):
            send_u(i, o).wait_recv()
            total = total + r1[i - direct, o - 1]
        sm[i, r, :] = total

        @pl.when(owner(i) != z)
        def _():
            send_uc(i, far(i)).start()

    def step_y(i):
        @pl.when(owner(i) == z)
        def _():
            gather_z(i)
            for o in range(1, nd):
                send_y(i, o, me).start()

    def step_w(i):
        @pl.when(owner(i) == z)
        def _():
            for o in range(1, nd):
                send_y(i, o, lax.rem(me - o + nd, nd)).wait_recv()

        wait_f(i)

    def drain_direct(i):
        for o in range(1, nd):
            send_u(i, o).wait_send()

        @pl.when(owner(i) != z)
        def _():
            send_uc(i, far(i)).wait_send()
            send_f(i, far(i), z).wait_send()

        @pl.when(owner(i) == z)
        def _():
            for o in range(1, nd):
                send_y(i, o, me).wait_send()

    def when_chunk(i, f, first=0, end=chunks):
        @pl.when((i >= first) & (i < end))
        def _():
            f(i)

    def early(j):
        @pl.when(j == 0)
        def _():
            ready()

        for i in (2 * j, 2 * j + 1):
            send_a(i).start()
        for i in (2 * j - 2, 2 * j - 1):
            when_chunk(i, step_b)
        for i in (2 * j - 4, 2 * j - 3):
            when_chunk(i, step_b2)
        for i in (2 * j - 6, 2 * j - 5):
            when_chunk(i, step_c)

    def late(t):
        @pl.when(t == 0)
        def _():
            for i in range(chunks - 2, chunks):
                step_b(i)

        when_chunk(t - 1, start_ua, 0, direct)
        when_chunk(t - 1, start_u, direct)

        @pl.when(t == 1)
        def _():
            step_b2(chunks - 4)

        when_chunk(t + chunks - 4, step_b2, chunks - 3)
        when_chunk(t + 2, step_c, 2)
        when_chunk(t - 2, step_ub, 0, direct)
        when_chunk(t - 3, step_uc, 0, direct)

        @pl.when(t == 1)
        def _():
            step_d(0)

        when_chunk(t, step_d, 1)
        when_chunk(t - 1, step_e)
        when_chunk(t - 2, step_f)
        when_chunk(t - 4, step_ud, 0, direct)
        when_chunk(t - 5, step_ue, 0, direct)
        when_chunk(t - 6, step_uf, 0, direct)

    x = ((xh0, x80, xl0), (xh1, x81, xl1))
    gt = (th, t8, tl)
    s1[...] = s_ref[...] * sc_ref[0:0 + 1, 0:1]
    s2[...] = s_ref[...] * sc_ref[6:6 + 1, 0:1]

    def cols(i):
        return aligned(place(i) * CHUNK, CHUNK)

    def prepare(i, to):
        for n in range(0, count, TILE):
            v = (e_ref[n:n + TILE, cols(i)][:, None, :] * s1[:, cols(i)][None]).reshape(TILE * members, CHUNK)
            r = slice(n * members, (n + TILE) * members)
            to[0][r, :], to[1][r, :], to[2][r, :] = split3(v)

    prepare(0, x[0])
    for copy in loads[:3]:
        copy.wait()

    def weights(j, carry):
        for par in (0, 1):
            i = 2 * j + par
            r = product([t[...] for t in gt], [t[...] for t in x[par]], dot)
            gw[aligned(2 * place(i), 2)] = (r.T * sc_ref[5:5 + 1, 0:1]).reshape(2, ny, nx, 2, blk, dout)
            prepare(jnp.minimum(i + 1, chunks - 1), x[1 - par])
        early(j)
        return carry

    lax.fori_loop(0, chunks // 2, weights, 0)

    for copy in loads[3:]:
        copy.wait()
    gsin[...] = jnp.zeros_like(gsin)
    g1[...] = jnp.zeros_like(g1)
    step = g0.shape[0]
    objs = step // members
    parts = rows // step

    def finish(i, t, g):
        g3 = g[...].reshape(objs, members, CHUNK)
        ns = slice(t * objs, (t + 1) * objs)
        ge[ns, :] = jnp.sum(g3 * s2[:, cols(i)][None], axis=1)
        gsin[...] += jnp.sum(g3 * e_ref[ns, cols(i)][:, None, :], axis=0)

    def table(i):
        c = place(i)
        first = c * feats
        base = (first // flocal) * (3 * flocal) + lax.rem(first, flocal)
        for j in range(CHUNK // 128):
            et[j * 128:(j + 1) * 128, :] = ge[:, j * 128:(j + 1) * 128].T
        lane = lax.broadcasted_iota(jnp.int32, (16, 128), 1)
        level = lax.broadcasted_iota(jnp.int32, (64, 128), 0).astype(F32)
        for p in range(feats // 2):
            row = base + 2 * p
            lh, ll = split2(table_pair(t_ref, c * (feats // 2) + p))
            enc = encode_pair(raw_ref, flocal, row)
            g = et[p * 32:(p + 1) * 32, :]
            gh_, gl_ = split2(g)
            eh, el = split2(enc)
            both = dot_nt(jnp.concatenate([gh_, gl_], axis=0), eh)
            full = both[:32] + both[32:] + dot_nt(gh_, el)
            sm[i, p * 16:(p + 1) * 16, :] = jnp.where(lane < 64, full[:16], full[16:])
            hot = []
            for f in (row, row + 1):
                here = 1.0 - raw_ref[pl.ds(f + 2 * flocal, 1), :]
                hot.append(jnp.where(level == raw_ref[pl.ds(f, 1), :], here, 0.0))
            one = jnp.concatenate(hot, axis=0).astype(BF16)
            both = dot(jnp.concatenate([lh, ll], axis=0), one)
            picked = (both[:32] + both[32:]) * g
            gf[i, 2 * p:2 * p + 1, :] = jnp.sum(picked[:16], axis=0, keepdims=True)
            gf[i, 2 * p + 1:2 * p + 2, :] = jnp.sum(picked[16:], axis=0, keepdims=True)
        at = feats * 8
        for j in range(CHUNK // 128):
            sm[i, at:at + members, :] = gsin[:, j * 128:(j + 1) * 128] * sc_ref[7:7 + 1, 0:1]
            at += members
        sm[i, at:at + members, :] = z_ref[:, aligned(c * 128, 128)]
        at += members
        sm[i, at:, :] = jnp.zeros_like(sm[i, at:, :])
        gsin[...] = jnp.zeros_like(gsin)

    def inputs(i, carry):
        before = jnp.maximum(i - 1, 0)
        wc = [t[cols(i), :] for t in (wh, w8, wl)]
        finish(before, parts - 1, g1)
        table(before)
        for t in range(parts):
            to, fro = (g0, g1) if t % 2 == 0 else (g1, g0)
            rs = slice(t * step, (t + 1) * step)
            to[...] = product([r[rs, :] for r in (gh, g8, gl)], wc, dot_nt)
            if t > 0:
                finish(i, t - 1, fro)
        late(i)
        return carry

    lax.fori_loop(0, chunks, inputs, 0)
    last = chunks - 1
    finish(last, parts - 1, g1)
    table(last)
    start_u(last)
    step_v(last - 1)
    step_uc(last - 2)
    step_ud(last - 3)
    step_ue(last - 4)
    step_e(last)
    step_f(last - 1)
    step_uf(last - 5)
    step_v(last)
    step_y(last - 1)
    step_ud(last - 2)
    step_ue(last - 3)
    step_uf(last - 4)
    step_y(last)
    step_ue(last - 2)
    step_uf(last - 3)
    step_f(last)
    step_w(last - 1)
    step_uf(last - 2)

    def close(i, carry):
        drain(i)
        when_chunk(i, drain_small, 0, direct)
        when_chunk(i, drain_direct, direct)
        return carry

    lax.fori_loop(0, chunks, close, 0)
    step_w(last)


def final_kernel(nf, bins, gw_ref, sm_ref, fr_ref, frac_ref, tab_ref, bias_ref, miss_ref, sin_ref, gw_out, so_ref, bo_ref):
    gw_out[...] = gw_ref[...]
    flocal = fr_ref.shape[1]
    for o in range(nf):
        frac_ref[:, o * 128:(o + 1) * 128] = fr_ref[o]
    members = sin_ref.shape[0]
    feats = CHUNK // 16
    width = so_ref.shape[1]
    small = []
    for j in range(sm_ref.shape[0]):
        for p in range(feats // 2):
            block = sm_ref[j, p * 16:(p + 1) * 16, :]
            for odd in (0, 1):
                f = j * feats + 2 * p + odd
                tab_ref[f] = block[:, odd * 64:odd * 64 + bins]
                bias_ref[:, f:f + 1] = block[:, odd * 64 + bins:odd * 64 + bins + 1]
                miss_ref[:, f:f + 1] = block[:, odd * 64 + bins + 1:odd * 64 + bins + 2]
        at = feats * 8
        for q in range(CHUNK // 128):
            sin_ref[:, j * CHUNK + q * 128:j * CHUNK + (q + 1) * 128] = sm_ref[j, at:at + members, :]
            at += members
        small.append(sm_ref[j, at:at + members, :])
    small = small[0] if len(small) == 1 else jnp.concatenate(small, axis=1)
    so_ref[...] = small[:, :width]
    bo_ref[...] = small[:, width:]


def params(**kw):
    return pltpu.CompilerParams(vmem_limit_bytes=VMEM_LIMIT, **kw)


def whole(shape):
    return pl.BlockSpec(shape, lambda *_: (0,) * len(shape))


def exchange(nd, nf, bins, fr, ms, tab, bias, miss, s, so, w, ct):
    flocal, total = bins.shape
    width = tab.shape[1]
    count, (din, dout) = total // nf, w.shape
    parts = 8
    ins = (bins, fr, ms, tab, bias, miss, s, so)
    shapes = [jax.ShapeDtypeStruct(x, F32) for x in ((nf * 3 * flocal, count), (nf * flocal // 2 * width, 128), (count, din), (8, 128))]
    far = [jax.ShapeDtypeStruct(w.shape, d) for d in (BF16, F8, F8)]
    dma = pltpu.SemaphoreType.DMA
    anywhere = pl.BlockSpec(memory_space=pl.ANY)
    return pl.pallas_call(
        functools.partial(exchange_kernel, nd, nf),
        out_shape=shapes + far,
        in_specs=[whole(x.shape) for x in ins] + [anywhere] * 2,
        out_specs=[whole(x.shape) for x in shapes] + [anywhere] * 3,
        scratch_shapes=[pltpu.VMEM((3 * flocal, total), F32), pltpu.VMEM((din, count), F32), pltpu.VMEM(w.shape, F32),
                        pltpu.VMEM((parts, ct.shape[0] // parts) + ct.shape[1:], F32)]
        + [pltpu.VMEM(x.shape, x.dtype) for x in far]
        + [dma((parts + 1,)), dma((3,))] + [dma((nf - 1,))] * 4 + [dma((nf - 1, nd // 2 - 1))] * 2 + [dma((nf - 1,))] * 2,
        compiler_params=params(collective_id=0, has_side_effects=True),
    )(*ins, w, ct)


def forward(nf, e, s, wp, so, bo, ct, sc):
    count, din = e.shape
    members, dout = so.shape
    rows, tiles, block = count * members, count // TILE, TILE * members
    lag = lambda i: jnp.maximum(i - 1, 0)
    big = pl.BlockSpec((TILE, members, dout), lambda i: (lag(i), 0, 0))
    nat = pl.BlockSpec((block, dout), lambda i: (lag(i), 0))
    tra = pl.BlockSpec((dout, block), lambda i: (0, lag(i)))
    return pl.pallas_call(
        functools.partial(forward_kernel, nf),
        out_shape=[jax.ShapeDtypeStruct((count, members, dout), F32)]
        + [jax.ShapeDtypeStruct((rows, dout), d) for d in (BF16, F8, F8)]
        + [jax.ShapeDtypeStruct((dout, rows), d) for d in (BF16, F8, F8)]
        + [jax.ShapeDtypeStruct((members, 2 * dout), F32)],
        grid=(tiles + 1,),
        in_specs=[whole(e.shape), whole(s.shape)] + [whole(w.shape) for w in wp] + [whole(so.shape), whole(bo.shape), big, whole(sc.shape)],
        out_specs=[big, nat, nat, nat, tra, tra, tra, whole((members, 2 * dout))],
        scratch_shapes=[pltpu.VMEM(so.shape, F32)] * 2 + [pltpu.VMEM(s.shape, F32), pltpu.VMEM(so.shape, F32), pltpu.VMEM(so.shape, F32)]
        + [pltpu.VMEM((block, din), d) for d in (BF16, F8, F8)] * 2
        + [pltpu.VMEM((block, dout), F32)] * 2,
        compiler_params=params(),
    )(e, s, *wp, so, bo, ct, sc)


def backward(nd, nf, e, s, zs, raw, t, wp, gp, gt, sc):
    count, din = e.shape
    members = s.shape[0]
    rows, dout = gp[0].shape
    step = rows // 4
    chunks, nchip = din // CHUNK, nd // 2
    per = chunks // nf
    ny, blk, half, sblk = nd // 4, CHUNK // nd // 2, 256 // 2, 256 // nd
    feats, flocal = CHUNK // 16, raw.shape[0] // (3 * nf)
    layout = (ny, 2, 2, blk, dout)
    shapes = [jax.ShapeDtypeStruct(x, F32) for x in ((2 * per,) + layout, (per, 256, 128), (nf, flocal, 128))]
    ins = (e, s, zs, raw, t)
    far = (*wp, *gp, *gt)
    dma = pltpu.SemaphoreType.DMA
    f32 = lambda *shape: pltpu.VMEM(shape, F32)
    return pl.pallas_call(
        functools.partial(backward_kernel, nd, nf),
        out_shape=shapes,
        in_specs=[whole(x.shape) for x in ins] + [whole(sc.shape)] + [pl.BlockSpec(memory_space=pl.ANY)] * len(far),
        out_specs=[whole(x.shape) for x in shapes],
        scratch_shapes=[pltpu.VMEM(x.shape, x.dtype) for x in far]
        + [f32(*s.shape)] * 2
        + [pltpu.VMEM((rows, CHUNK), d) for d in (BF16, F8, F8)] * 2
        + [f32(step, CHUNK)] * 2
        + [f32(count, CHUNK), f32(members, CHUNK), f32(CHUNK, count)]
        + [f32(2 * chunks, *layout), f32(chunks, 256, 128), f32(chunks, feats, count)]
        + [f32(chunks, *layout), f32(chunks, ny, blk, dout), f32(chunks, ny - 1, 2, blk, dout), f32(chunks, ny - 1, blk, dout),
           f32(chunks, blk, dout), f32(per, nf - 1, 2, blk, dout)]
        + [f32(chunks, half, 128), f32(chunks, nchip - 1, sblk, 128), f32(DIRECT, nd - 1, sblk, 128), f32(per, nf - 1, sblk, 128)]
        + [dma((9,))]
        + [dma((chunks,))] * 4 + [dma((chunks, ny - 1))] * 4 + [dma((chunks,))] * 2 + [dma((chunks,)), dma((per, nf - 1))]
        + [dma((per, nchip - 1))] * 2 + [dma((per,))] * 2 + [dma((chunks,)), dma((per, nf - 1))]
        + [dma((chunks,))] * 2 + [dma((chunks, nchip - 1))] * 2 + [dma((chunks,)), dma((per, nf - 1))]
        + [dma((per, nchip - 1))] * 2 + [dma((per,))] * 2
        + [dma((DIRECT, nd - 1))] * 4,
        compiler_params=params(collective_id=1, has_side_effects=True),
    )(*ins, sc, *far)


def final(nf, bins, gw, sm, fr):
    per, flocal = sm.shape[0], fr.shape[1]
    members, width = 32, gw.shape[1] // nf
    shapes = [jax.ShapeDtypeStruct(x, F32) for x in (
        (flocal, nf * 128), (flocal, 16, bins), (16, flocal), (16, flocal), (members, per * CHUNK), gw.shape, (members, width), (members, width))]
    ins = (gw, sm, fr)
    return pl.pallas_call(functools.partial(final_kernel, nf, bins), out_shape=shapes, in_specs=[whole(x.shape) for x in ins],
                          out_specs=[whole(x.shape) for x in shapes], compiler_params=params())(*ins)


def shards(nd, nf, bins, fractions, missing, bin_table, bin_bias, miss_vector, scale_in, weight, scale_out, bias_out, cotangent):
    raw, packed, e, sc, *wp = exchange(nd, nf, bins.T, fractions.T, missing.T, jnp.transpose(bin_table, (0, 2, 1)), bin_bias.T,
                                       miss_vector.T, scale_in, scale_out, weight, cotangent)
    hidden, *rest = forward(nf, e, scale_in, wp, scale_out, bias_out, cotangent, sc)
    gw, sm, fr = backward(nd, nf, e, scale_in, rest[6], raw, packed, wp, rest[:3], rest[3:6], sc)
    gw = gw.reshape(-1, weight.shape[1])
    frac, table, bias, miss, sin, gw, so, bo = final(nf, bin_table.shape[1], gw, sm, fr)
    return hidden, frac.T, jnp.transpose(table, (0, 2, 1)), bias.T, miss.T, sin, gw, so, bo


def solution(mesh):
    placed = (P("dp", "feat"), P("dp", "feat"), P("dp", "feat"), P("feat", None, None), P("feat", None), P("feat", None),
              P(), P(), P(), P(), P(("dp", "feat"), None, None))
    return jax.shard_map(
        functools.partial(shards, mesh.shape["dp"], mesh.shape["feat"]),
        mesh=mesh,
        in_specs=placed,
        out_specs=(P(("dp", "feat"), None, None), P("dp", "feat"), P("feat", None, None), P("feat", None), P("feat", None),
                   P(None, "feat"), P("feat", None), P(None, "feat"), P(None, "feat")),
        check_vma=False,
    )
```

```python
import functools

import jax
import jax.numpy as jnp
from jax import lax
from jax.experimental import pallas as pl
from jax.experimental.pallas import tpu as pltpu
from jax.sharding import PartitionSpec as P

F32, BF16, F8 = jnp.float32, jnp.bfloat16, jnp.float8_e4m3fn
VMEM_LIMIT = 63 << 20
TILE = 16
DIRECT = 2
CHUNK = 256
TOP = 224.0
LO = 256.0
GELU_A = 0.7978845608028654
GELU_B = GELU_A * 0.044715


def dot(a, b):
    return jnp.dot(a, b, preferred_element_type=F32)


def dot_nt(a, b):
    return lax.dot_general(a, b, (((1,), (1,)), ((), ())), preferred_element_type=F32)


def split3(x):
    hi = x.astype(BF16)
    return hi, x.astype(F8), ((x - hi.astype(F32)) * LO).astype(F8)


def split2(x):
    hi = x.astype(BF16)
    return hi, (x - hi.astype(F32)).astype(BF16)


def product(a, b, mul):
    ah, a8, al = a
    bh, b8, bl = b
    return mul(ah, bh) + (mul(a8, bl) + mul(al, b8)) * (1.0 / LO)


def encode_pair(raw_ref, flocal, first):
    level = lax.broadcasted_iota(jnp.int32, (48, 128), 0).astype(F32)
    row = lax.broadcasted_iota(jnp.int32, (16, 128), 0)
    parts = []
    for f in (first, first + 1):
        b, fr, m = [raw_ref[pl.ds(f + k * flocal, 1), :] for k in range(3)]
        here = 1.0 - m
        parts.append(jnp.clip((b - level) + fr, 0.0, 1.0) * here)
        parts.append(jnp.where(row == 0, here, jnp.where(row == 1, m, 0.0)))
    return jnp.concatenate(parts, axis=0)


def table_pair(t_ref, p):
    blk = t_ref[pl.ds(pl.multiple_of(p * 16, 16), 16), :]
    lane = lax.broadcasted_iota(jnp.int32, (16, 128), 1)
    zero = jnp.zeros_like(blk)
    return jnp.concatenate([jnp.where(lane < 64, blk, zero), jnp.where(lane < 64, zero, blk)], axis=0)


def send(src, dst, ssem, rsem, **where):
    return pltpu.make_async_remote_copy(src_ref=src, dst_ref=dst, send_sem=ssem, recv_sem=rsem, device_id=where,
                                        device_id_type=pl.DeviceIdType.MESH)


def greet(partners):
    barrier = pltpu.get_barrier_semaphore()
    for where in partners:
        pl.semaphore_signal(barrier, inc=1, device_id=where, device_id_type=pl.DeviceIdType.MESH)
    return lambda: pl.semaphore_wait(barrier, len(partners))


def exchange_kernel(nd, nf, bins_ref, fr_ref, ms_ref, tab_ref, bias_ref, miss_ref, s_ref, so_ref, w_in, ct_in,
                    raw_ref, t_ref, e_ref, sc_ref, wh_out, w8_out, wl_out,
                    mine, et, w, ct, wh, w8, wl, load, store, r_s, r_r, x_s, x_r, y_s, y_r, z_s, z_r):
    flocal, total = bins_ref.shape
    count = total // nf
    bins, width = tab_ref.shape[2], tab_ref.shape[1]
    me, z = lax.axis_index("dp"), lax.axis_index("feat")
    nchip = nd // 2
    core, chip = lax.rem(me, 2), me // 2
    partner = me + 1 - 2 * core
    parts = ct.shape[0]
    step = ct_in.shape[0] // parts

    ready = greet([{"feat": lax.rem(z + o, nf)} for o in range(1, nf)]
                  + [{"dp": 2 * lax.rem(chip + o, nchip) + core} for o in range(1, nchip)] + [{"dp": partner}])
    loads = [pltpu.make_async_copy(w_in, w, load.at[0])] + [
        pltpu.make_async_copy(ct_in.at[pl.ds(i * step, step)], ct.at[i], load.at[i + 1]) for i in range(parts)]
    loads[0].start()

    def rows(q):
        return pl.ds(pl.multiple_of(q * (3 * flocal), 3 * flocal), 3 * flocal)

    size = flocal // 2 * width // nd

    def entries(q, piece, n):
        return t_ref.at[pl.ds(pl.multiple_of(q * (nd * size) + piece * size, 8), n * size)]

    mine[0:flocal, :] = bins_ref[...].astype(F32)
    mine[flocal:2 * flocal, :] = fr_ref[...]
    mine[2 * flocal:, :] = ms_ref[...].astype(F32)
    raw_ref[rows(z), :] = mine[:, pl.ds(pl.multiple_of(z * count, count), count)]
    blank = jnp.zeros((width, 64 - bins - 2), F32)
    for p in range(flocal // 2):
        block = []
        for f in (2 * p, 2 * p + 1):
            block += [tab_ref[f], bias_ref[:, f:f + 1], miss_ref[:, f:f + 1], blank]
        t_ref[pl.ds(pl.multiple_of(z * (flocal // 2 * width) + p * width, width), width), :] = jnp.concatenate(block, axis=1)

    def send_raw(o, q):
        to = lax.rem(z + o, nf)
        return send(mine.at[:, pl.ds(pl.multiple_of(to * count, count), count)], raw_ref.at[rows(q)],
                    r_s.at[o - 1], r_r.at[o - 1], feat=to)

    def send_x(o, q):
        r = entries(q, core * nchip + chip, 1)
        return send(r, r, x_s.at[o - 1], x_r.at[o - 1], feat=lax.rem(z + o, nf))

    def send_y(o, k, c):
        r = entries(lax.rem(z - o + nf, nf), core * nchip + c, 1)
        return send(r, r, y_s.at[o - 1, k - 1], y_r.at[o - 1, k - 1], dp=2 * lax.rem(chip + k, nchip) + core)

    def send_z(o, side):
        r = entries(lax.rem(z - o + nf, nf), side * nchip, nchip)
        return send(r, r, z_s.at[o - 1], z_r.at[o - 1], dp=partner)

    others = range(1, nf)
    ready()
    for o in others:
        send_x(o, z).start()
    for o in others:
        send_raw(o, z).start()

    def top(v):
        return jnp.maximum(jnp.max(jnp.max(jnp.abs(v), axis=0, keepdims=True), axis=1, keepdims=True), 1e-30)

    at_once = 8
    pairs = flocal // 2
    entries_local = flocal * width

    def embed(q):
        def body(j, c):
            for k in range(at_once):
                p = q * pairs + j * at_once + k
                first = q * (3 * flocal) + 2 * (j * at_once + k)
                lh, ll = split2(table_pair(t_ref, p))
                eh, el = split2(encode_pair(raw_ref, flocal, first))
                both = dot(jnp.concatenate([lh, ll], axis=0), eh)
                et[pl.ds(pl.multiple_of(p * 32, 32), 32), :] = both[:32] + both[32:] + dot(lh, el)
            return c

        lax.fori_loop(0, pairs // at_once, body, 0)
        for j in range(entries_local // 128):
            at = pl.ds(pl.multiple_of(q * entries_local + j * 128, 128), 128)
            e_ref[:, at] = et[at, :].T

    embed(z)
    for o in others:
        send_x(o, lax.rem(z - o + nf, nf)).wait_recv()
        for k in range(1, nchip):
            send_y(o, k, chip).start()

    loads[0].wait()
    for copy in loads[1:]:
        copy.start()
    sw = TOP / top(w[...])
    for i in range(0, w.shape[0], 256):
        r = slice(i, i + 256)
        wh[r, :], w8[r, :], wl[r, :] = split3(w[r, :] * sw)
    stores = [pltpu.make_async_copy(i, o, store.at[k]) for k, (i, o) in enumerate(((wh, wh_out), (w8, w8_out), (wl, wl_out)))]
    for copy in stores:
        copy.start()

    for o in others:
        for k in range(1, nchip):
            send_y(o, k, lax.rem(chip - k + nchip, nchip)).wait_recv()
        send_z(o, core).start()
    tc = jnp.full((1, 1), 1e-30, F32)
    for i in range(parts):
        loads[i + 1].wait()
        tc = jnp.maximum(tc, top(ct[i].reshape(-1, ct.shape[-1])))
    for o in others:
        q = lax.rem(z - o + nf, nf)
        send_z(o, 1 - core).wait_recv()
        send_raw(o, q).wait_recv()
        embed(q)
    sx = TOP / (top(et[...]) * top(s_ref[...]))
    sg = TOP / (1.2 * tc * top(so_ref[...]))
    for k, v in enumerate((sx, sw, sg, 1.0 / (sx * sw), 1.0 / (sx * sw), 1.0 / (sg * sx), 1.0 / (sg * sw), 1.0 / (sg * sw))):
        sc_ref[k:k + 1, :] = jnp.broadcast_to(v, (1, 128))
    for copy in stores:
        copy.wait()
    for o in others:
        send_raw(o, z).wait_send()
        send_x(o, z).wait_send()
        for k in range(1, nchip):
            send_y(o, k, chip).wait_send()
        send_z(o, core).wait_send()


def forward_kernel(nf, e_ref, s_ref, wh_in, w8_in, wl_in, so_ref, bo_ref, ct_ref, sc_ref,
                   hid_ref, gh_ref, g8_ref, gl_ref, th_ref, t8_ref, tl_ref, z_ref,
                   gs_ref, gb_ref, s1, so1, so2, wh_ref, w8_ref, wl_ref, load, xh0, x80, xl0, xh1, x81, xl1, pre0, pre1):
    i = pl.program_id(0)
    tiles = pl.num_programs(0) - 1
    members, width_out = so_ref.shape
    rows = TILE * members
    x = ((xh0, x80, xl0), (xh1, x81, xl1))
    pre = (pre0, pre1)
    w = (wh_ref, w8_ref, wl_ref)

    def prepare(tile, to):
        for n in range(TILE):
            v = s1[...] * e_ref[pl.ds(tile * TILE + n, 1), :]
            r = slice(n * members, (n + 1) * members)
            to[0][r, :], to[1][r, :], to[2][r, :] = split3(v)

    def multiply(a, to):
        to[...] = product([r[...] for r in a], [r[...] for r in w], dot)

    def finish(p):
        for h0 in range(0, width_out, 128):
            hs = slice(h0, h0 + 128)
            sa, sb, bo = so1[:, hs], so2[:, hs], bo_ref[:, hs]
            gs, gb = gs_ref[:, hs], gb_ref[:, hs]
            for n in range(TILE):
                r = slice(n * members, (n + 1) * members)
                q = p[r, hs]
                v = q * sa + bo
                v2 = v * v
                half = 0.5 + 0.5 * jnp.tanh(v * (GELU_B * v2 + GELU_A))
                hid = v * half
                hid_ref[n, :, hs] = hid
                g = half + hid * (1.0 - half) * ((6.0 * GELU_B) * v2 + 2.0 * GELU_A)
                ga = ct_ref[n, :, hs] * g
                gs = gs + ga * q
                gb = gb + ga
                gh_ref[r, hs], g8_ref[r, hs], gl_ref[r, hs] = split3(ga * sb)
            gs_ref[:, hs], gb_ref[:, hs] = gs, gb
        th_ref[...] = gh_ref[...].T
        t8_ref[...] = g8_ref[...].T
        tl_ref[...] = gl_ref[...].T

    @pl.when(i == 0)
    def _():
        loads = [pltpu.make_async_copy(a, b, load.at[k]) for k, (a, b) in enumerate(
            ((wh_in, wh_ref), (w8_in, w8_ref), (wl_in, wl_ref)))]
        for copy in loads:
            copy.start()
        s1[...] = s_ref[...] * sc_ref[0:0 + 1, 0:1]
        so1[...] = so_ref[...] * sc_ref[3:3 + 1, 0:1]
        so2[...] = so_ref[...] * sc_ref[2:2 + 1, 0:1]
        gs_ref[...] = jnp.zeros_like(gs_ref)
        gb_ref[...] = jnp.zeros_like(gb_ref)
        prepare(0, x[0])
        for copy in loads:
            copy.wait()
        prepare(1, x[1])
        multiply(x[0], pre[0])

    for par in (0, 1):
        @pl.when((i > 0) & (i < tiles) & (i % 2 == par))
        def _():
            finish(pre[1 - par])
            prepare(jnp.minimum(i + 1, tiles - 1), x[1 - par])
            multiply(x[par], pre[par])

    @pl.when(i == tiles)
    def _():
        finish(pre[1])
        part = width_out // nf
        for o in range(nf):
            z_ref[:, 2 * o * part:(2 * o + 1) * part] = gs_ref[:, o * part:(o + 1) * part] * sc_ref[4:4 + 1, 0:1]
            z_ref[:, (2 * o + 1) * part:(2 * o + 2) * part] = gb_ref[:, o * part:(o + 1) * part]


def backward_kernel(nd, nf, e_ref, s_ref, z_ref, raw_ref, t_ref, sc_ref, wh_in, w8_in, wl_in, gh_in, g8_in, gl_in,
                    th_in, t8_in, tl_in, gw_out, sm_out, fr_out,
                    wh, w8, wl, gh, g8, gl, th, t8, tl, s1, s2, xh0, x80, xl0, xh1, x81, xl1, g0, g1, ge, gsin, et,
                    gw, sm, gf, ra, rp, rq, rp2, rq2, rc, ru, rb, r1, r2,
                    load, a_s, a_r, p_s, p_r, q_s, q_r, p2_s, p2_r, q2_s, q2_r, c_s, c_r, d_s, d_r, e_s, e_r, f_s, f_r,
                    ua_s, ua_r, ub_s, ub_r, uc_s, uc_r, ud_s, ud_r, ue_s, ue_r, u_s, u_r, y_s, y_r):
    members, width_in = s_ref.shape
    rows = gh.shape[0]
    count = e_ref.shape[0]
    chunks = width_in // CHUNK
    direct = chunks - DIRECT
    per = chunks // nf
    nx, ny, nchip = 2, nd // 4, nd // 2
    blk, dout = gw.shape[4], gw.shape[5]
    half, sblk = sm.shape[1] // 2, sm.shape[1] // nd
    feats = CHUNK // 16
    flocal = fr_out.shape[1]
    me, z = lax.axis_index("dp"), lax.axis_index("feat")
    core, chip = lax.rem(me, 2), me // 2
    cx, cy = lax.rem(chip, nx), chip // nx
    partner = me + 1 - 2 * core

    ready = greet([{"dp": lax.rem(me + o, nd)} for o in range(1, nd)] + [{"feat": lax.rem(z + o, nf)} for o in range(1, nf)])
    loads = [pltpu.make_async_copy(i, o, load.at[k]) for k, (i, o) in enumerate(
        ((th_in, th), (t8_in, t8), (tl_in, tl), (wh_in, wh), (w8_in, w8), (wl_in, wl), (gh_in, gh), (g8_in, g8), (gl_in, gl)))]
    for copy in loads[:3]:
        copy.start()

    def aligned(i, n):
        return pl.ds(pl.multiple_of(i, n), n)

    def place(i):
        return lax.rem(i, nf) * per + i // nf

    def owner(i):
        return lax.rem(i, nf)

    def far(i):
        return lax.rem(owner(i) - z + nf, nf)

    def device(y, x):
        return 2 * (y * nx + x) + core

    def other_y(k):
        return lax.rem(cy + k, ny)

    def from_y(k):
        return lax.rem(cy - k + ny, ny)

    def own(i):
        return 2 * place(i) + core

    def send_a(i):
        return send(gw.at[2 * place(i) + 1 - core], ra.at[i], a_s.at[i], a_r.at[i], dp=partner)

    def send_p(i):
        return send(gw.at[own(i), :, 1 - cx, 0], rp.at[i], p_s.at[i], p_r.at[i], dp=device(cy, 1 - cx))

    def send_q(i, k):
        return send(gw.at[own(i), other_y(k), :, 1], rq.at[i, k - 1], q_s.at[i, k - 1], q_r.at[i, k - 1], dp=device(other_y(k), cx))

    def send_p2(i, k):
        return send(gw.at[own(i), other_y(k), cx, 0], rp2.at[i, k - 1], p2_s.at[i, k - 1], p2_r.at[i, k - 1], dp=device(other_y(k), cx))

    def send_q2(i):
        return send(gw.at[own(i), cy, 1 - cx, 1], rq2.at[i], q2_s.at[i], q2_r.at[i], dp=device(cy, 1 - cx))

    def send_c(i, k):
        j = i // nf
        return send(gw.at[own(i), cy, cx], rc.at[j, k - 1], c_s.at[i], c_r.at[j, k - 1], feat=owner(i))

    def send_d(i, o, q):
        j = i // nf
        return send(gw.at[own(i), cy, cx], gw_out.at[2 * j + core, q // nx, lax.rem(q, nx)], d_s.at[j, o - 1], d_r.at[j, o - 1],
                    dp=2 * lax.rem(chip + o, nchip) + core)

    def send_e(i, side):
        j = i // nf
        return send(gw_out.at[2 * j + side], gw_out.at[2 * j + side], e_s.at[j], e_r.at[j], dp=partner)

    def step_b(i):
        send_a(i).wait_recv()
        gw[own(i)] += ra[i]
        send_p(i).start()
        for k in range(1, ny):
            send_q(i, k).start()

    def step_b2(i):
        send_p(i).wait_recv()
        gw[own(i), :, cx, 0] += rp[i]
        for k in range(1, ny):
            send_q(i, k).wait_recv()
            gw[own(i), cy, :, 1] += rq[i, k - 1]
        for k in range(1, ny):
            send_p2(i, k).start()
        send_q2(i).start()

    def step_c(i):
        send_q2(i).wait_recv()
        gw[own(i), cy, cx, 1] += rq2[i]
        for k in range(1, ny):
            send_p2(i, k).wait_recv()
            gw[own(i), cy, cx, 0] += rp2[i, k - 1]

        @pl.when(owner(i) != z)
        def _():
            send_c(i, far(i)).start()

    def step_d(i):
        @pl.when(owner(i) == z)
        def _():
            total = gw[own(i), cy, cx]
            for k in range(1, nf):
                send_c(i, k).wait_recv()
                total = total + rc[i // nf, k - 1]
            gw[own(i), cy, cx] = total
            gw_out[2 * (i // nf) + core, cy, cx] = total
            for o in range(1, nchip):
                send_d(i, o, chip).start()

    def step_e(i):
        @pl.when(owner(i) == z)
        def _():
            for o in range(1, nchip):
                send_d(i, o, lax.rem(chip - o + nchip, nchip)).wait_recv()
            send_e(i, core).start()

    def step_f(i):
        @pl.when(owner(i) == z)
        def _():
            send_e(i, 1 - core).wait_recv()

    def drain(i):
        send_a(i).wait_send()
        send_p(i).wait_send()
        send_q2(i).wait_send()
        for k in range(1, ny):
            send_q(i, k).wait_send()
            send_p2(i, k).wait_send()

        @pl.when(owner(i) != z)
        def _():
            send_c(i, far(i)).wait_send()

        @pl.when(owner(i) == z)
        def _():
            for o in range(1, nchip):
                send_d(i, o, chip).wait_send()
            send_e(i, core).wait_send()

    def rows_of(q, side):
        return aligned(side * half + q * sblk, sblk)

    def whole_half(side):
        return aligned(side * half, half)

    def send_ua(i):
        return send(sm.at[i, whole_half(1 - core)], ru.at[i], ua_s.at[i], ua_r.at[i], dp=partner)

    def send_ub(i, o):
        to = lax.rem(chip + o, nchip)
        return send(sm.at[i, rows_of(to, core)], rb.at[i, o - 1], ub_s.at[i, o - 1], ub_r.at[i, o - 1], dp=2 * to + core)

    def send_uc(i, k):
        j = i // nf
        return send(sm.at[i, rows_of(chip, core)], r2.at[j, k - 1], uc_s.at[i], uc_r.at[j, k - 1], feat=owner(i))

    def send_ud(i, o, q):
        j = i // nf
        return send(sm.at[i, rows_of(chip, core)], sm_out.at[j, rows_of(q, core)], ud_s.at[j, o - 1], ud_r.at[j, o - 1],
                    dp=2 * lax.rem(chip + o, nchip) + core)

    def send_ue(i, side):
        j = i // nf
        r = sm_out.at[j, whole_half(side)]
        return send(r, r, ue_s.at[j], ue_r.at[j], dp=partner)

    def send_u(i, o):
        to = lax.rem(me + o, nd)
        return send(sm.at[i, rows_of(to // 2, lax.rem(to, 2))], r1.at[i - direct, o - 1], u_s.at[i - direct, o - 1],
                    u_r.at[i - direct, o - 1], dp=to)

    def send_y(i, o, q):
        j = i - direct
        return send(sm.at[i, rows_of(chip, core)], sm_out.at[i // nf, rows_of(q // 2, lax.rem(q, 2))], y_s.at[j, o - 1], y_r.at[j, o - 1],
                    dp=lax.rem(me + o, nd))

    def send_f(i, k, src):
        j = i // nf
        return send(gf.at[i], fr_out.at[src, aligned(j * feats, feats)], f_s.at[i], f_r.at[j, k - 1], feat=owner(i))

    def start_f(i):
        @pl.when(owner(i) != z)
        def _():
            send_f(i, far(i), z).start()

        @pl.when(owner(i) == z)
        def _():
            fr_out[z, aligned((i // nf) * feats, feats), :] = gf[i]

    def wait_f(i):
        @pl.when(owner(i) == z)
        def _():
            for k in range(1, nf):
                send_f(i, k, lax.rem(z - k + nf, nf)).wait_recv()

    def start_ua(i):
        send_ua(i).start()
        start_f(i)

    def step_ub(i):
        send_ua(i).wait_recv()
        sm[i, whole_half(core), :] += ru[i]
        for o in range(1, nchip):
            send_ub(i, o).start()

    def step_uc(i):
        r = rows_of(chip, core)
        total = sm[i, r, :]
        for o in range(1, nchip):
            send_ub(i, o).wait_recv()
            total = total + rb[i, o - 1]
        sm[i, r, :] = total

        @pl.when(owner(i) != z)
        def _():
            send_uc(i, far(i)).start()

    def gather_z(i):
        r = rows_of(chip, core)
        total = sm[i, r, :]
        for k in range(1, nf):
            send_uc(i, k).wait_recv()
            total = total + r2[i // nf, k - 1]
        sm[i, r, :] = total
        sm_out[i // nf, r, :] = total

    def step_ud(i):
        @pl.when(owner(i) == z)
        def _():
            gather_z(i)
            for o in range(1, nchip):
                send_ud(i, o, chip).start()

    def step_ue(i):
        @pl.when(owner(i) == z)
        def _():
            for o in range(1, nchip):
                send_ud(i, o, lax.rem(chip - o + nchip, nchip)).wait_recv()
            send_ue(i, core).start()

    def step_uf(i):
        @pl.when(owner(i) == z)
        def _():
            send_ue(i, 1 - core).wait_recv()

        wait_f(i)

    def drain_small(i):
        send_ua(i).wait_send()
        for o in range(1, nchip):
            send_ub(i, o).wait_send()

        @pl.when(owner(i) != z)
        def _():
            send_uc(i, far(i)).wait_send()
            send_f(i, far(i), z).wait_send()

        @pl.when(owner(i) == z)
        def _():
            for o in range(1, nchip):
                send_ud(i, o, chip).wait_send()
            send_ue(i, core).wait_send()

    def start_u(i):
        for o in range(1, nd):
            send_u(i, o).start()
        start_f(i)

    def step_v(i):
        r = rows_of(chip, core)
        total = sm[i, r, :]
        for o in range(1, nd):
            send_u(i, o).wait_recv()
            total = total + r1[i - direct, o - 1]
        sm[i, r, :] = total

        @pl.when(owner(i) != z)
        def _():
            send_uc(i, far(i)).start()

    def step_y(i):
        @pl.when(owner(i) == z)
        def _():
            gather_z(i)
            for o in range(1, nd):
                send_y(i, o, me).start()

    def step_w(i):
        @pl.when(owner(i) == z)
        def _():
            for o in range(1, nd):
                send_y(i, o, lax.rem(me - o + nd, nd)).wait_recv()

        wait_f(i)

    def drain_direct(i):
        for o in range(1, nd):
            send_u(i, o).wait_send()

        @pl.when(owner(i) != z)
        def _():
            send_uc(i, far(i)).wait_send()
            send_f(i, far(i), z).wait_send()

        @pl.when(owner(i) == z)
        def _():
            for o in range(1, nd):
                send_y(i, o, me).wait_send()

    def when_chunk(i, f, first=0, end=chunks):
        @pl.when((i >= first) & (i < end))
        def _():
            f(i)

    start_a = lambda i: send_a(i).start()
    stages = ((start_a, (0, 1, 2, 3)), (step_b, (1, 2, 3, 4)), (step_b2, (3, 4, 5, 6)), (step_c, (5, 6, 7, 8)),
              (step_d, (7, 8, 9, 10)), (step_e, (9, 10, 11)))

    def pairs(k, among):
        for step, times in stages:
            for j, at in enumerate(times):
                if at in among:
                    @pl.when(k == at)
                    def _():
                        for i in (2 * j, 2 * j + 1):
                            step(i)

    def early(j):
        @pl.when(j == 0)
        def _():
            ready()

        pairs(j, range(4))

    def late(t):
        when_chunk(t - 1, start_ua, 0, direct)
        when_chunk(t - 1, start_u, direct)
        pairs(t + 4, range(4, 12))
        when_chunk(t - 2, step_ub, 0, direct)
        when_chunk(t - 4, step_uc, 0, direct)
        when_chunk(t - 6, step_ud, 0, direct)

    x = ((xh0, x80, xl0), (xh1, x81, xl1))
    gt = (th, t8, tl)
    s1[...] = s_ref[...] * sc_ref[0:0 + 1, 0:1]
    s2[...] = s_ref[...] * sc_ref[6:6 + 1, 0:1]

    def cols(i):
        return aligned(place(i) * CHUNK, CHUNK)

    def prepare(i, to):
        for n in range(0, count, TILE):
            v = (e_ref[n:n + TILE, cols(i)][:, None, :] * s1[:, cols(i)][None]).reshape(TILE * members, CHUNK)
            r = slice(n * members, (n + TILE) * members)
            to[0][r, :], to[1][r, :], to[2][r, :] = split3(v)

    prepare(0, x[0])
    for copy in loads[:3]:
        copy.wait()
    for copy in loads[3:]:
        copy.start()

    def weights(j, carry):
        for par in (0, 1):
            i = 2 * j + par
            r = product([t[...] for t in gt], [t[...] for t in x[par]], dot)
            gw[aligned(2 * place(i), 2)] = (r.T * sc_ref[5:5 + 1, 0:1]).reshape(2, ny, nx, 2, blk, dout)
            prepare(jnp.minimum(i + 1, chunks - 1), x[1 - par])
        early(j)
        return carry

    lax.fori_loop(0, chunks // 2, weights, 0)

    for copy in loads[3:]:
        copy.wait()
    gsin[...] = jnp.zeros_like(gsin)
    g1[...] = jnp.zeros_like(g1)
    step = g0.shape[0]
    objs = step // members
    parts = rows // step

    def finish(i, t, g):
        g3 = g[...].reshape(objs, members, CHUNK)
        ns = slice(t * objs, (t + 1) * objs)
        ge[ns, :] = jnp.sum(g3 * s2[:, cols(i)][None], axis=1)
        gsin[...] += jnp.sum(g3 * e_ref[ns, cols(i)][:, None, :], axis=0)

    def table(i):
        c = place(i)
        first = c * feats
        base = (first // flocal) * (3 * flocal) + lax.rem(first, flocal)
        for j in range(CHUNK // 128):
            et[j * 128:(j + 1) * 128, :] = ge[:, j * 128:(j + 1) * 128].T
        lane = lax.broadcasted_iota(jnp.int32, (16, 128), 1)
        level = lax.broadcasted_iota(jnp.int32, (64, 128), 0).astype(F32)
        for p in range(feats // 2):
            row = base + 2 * p
            lh, ll = split2(table_pair(t_ref, c * (feats // 2) + p))
            enc = encode_pair(raw_ref, flocal, row)
            g = et[p * 32:(p + 1) * 32, :]
            gh_, gl_ = split2(g)
            eh, el = split2(enc)
            both = dot_nt(jnp.concatenate([gh_, gl_], axis=0), eh)
            full = both[:32] + both[32:] + dot_nt(gh_, el)
            sm[i, p * 16:(p + 1) * 16, :] = jnp.where(lane < 64, full[:16], full[16:])
            hot = []
            for f in (row, row + 1):
                here = 1.0 - raw_ref[pl.ds(f + 2 * flocal, 1), :]
                hot.append(jnp.where(level == raw_ref[pl.ds(f, 1), :], here, 0.0))
            one = jnp.concatenate(hot, axis=0).astype(BF16)
            both = dot(jnp.concatenate([lh, ll], axis=0), one)
            picked = (both[:32] + both[32:]) * g
            gf[i, 2 * p:2 * p + 1, :] = jnp.sum(picked[:16], axis=0, keepdims=True)
            gf[i, 2 * p + 1:2 * p + 2, :] = jnp.sum(picked[16:], axis=0, keepdims=True)
        at = feats * 8
        for j in range(CHUNK // 128):
            sm[i, at:at + members, :] = gsin[:, j * 128:(j + 1) * 128] * sc_ref[7:7 + 1, 0:1]
            at += members
        sm[i, at:at + members, :] = z_ref[:, aligned(c * 128, 128)]
        at += members
        sm[i, at:, :] = jnp.zeros_like(sm[i, at:, :])
        gsin[...] = jnp.zeros_like(gsin)

    def inputs(i, carry):
        before = jnp.maximum(i - 1, 0)
        wc = [t[cols(i), :] for t in (wh, w8, wl)]
        finish(before, parts - 1, g1)
        table(before)
        for t in range(parts):
            to, fro = (g0, g1) if t % 2 == 0 else (g1, g0)
            rs = slice(t * step, (t + 1) * step)
            to[...] = product([r[rs, :] for r in (gh, g8, gl)], wc, dot_nt)
            if t > 0:
                finish(i, t - 1, fro)
        late(i)
        return carry

    lax.fori_loop(0, chunks, inputs, 0)
    last = chunks - 1
    finish(last, parts - 1, g1)
    table(last)
    start_u(last)
    step_e(last - 1)
    step_e(last)
    step_v(last - 1)
    for i in range(direct - 2, direct):
        step_uc(i)
    for i in range(direct - 4, direct - 2):
        step_ud(i)
    for i in range(direct - 4):
        step_ue(i)
    step_v(last)
    step_y(last - 1)
    for i in range(direct - 2, direct):
        step_ud(i)
    for i in range(direct - 4, direct - 2):
        step_ue(i)
    step_y(last)
    for i in range(direct - 2, direct):
        step_ue(i)
    for i in range(chunks):
        step_f(i)
    for i in range(direct):
        step_uf(i)
    step_w(last - 1)

    def close(i, carry):
        drain(i)
        when_chunk(i, drain_small, 0, direct)
        when_chunk(i, drain_direct, direct)
        return carry

    lax.fori_loop(0, chunks, close, 0)
    step_w(last)


def final_kernel(nf, bins, gw_in, sm_ref, fr_ref, frac_ref, tab_ref, bias_ref, miss_ref, sin_ref, gw_out, so_ref, bo_ref, sem):
    copy = pltpu.make_async_copy(gw_in, gw_out, sem)
    copy.start()
    flocal = fr_ref.shape[1]
    for o in range(nf):
        frac_ref[:, o * 128:(o + 1) * 128] = fr_ref[o]
    members = sin_ref.shape[0]
    feats = CHUNK // 16
    width = so_ref.shape[1]
    small = []
    for j in range(sm_ref.shape[0]):
        for p in range(feats // 2):
            block = sm_ref[j, p * 16:(p + 1) * 16, :]
            for odd in (0, 1):
                f = j * feats + 2 * p + odd
                tab_ref[f] = block[:, odd * 64:odd * 64 + bins]
                bias_ref[:, f:f + 1] = block[:, odd * 64 + bins:odd * 64 + bins + 1]
                miss_ref[:, f:f + 1] = block[:, odd * 64 + bins + 1:odd * 64 + bins + 2]
        at = feats * 8
        for q in range(CHUNK // 128):
            sin_ref[:, j * CHUNK + q * 128:j * CHUNK + (q + 1) * 128] = sm_ref[j, at:at + members, :]
            at += members
        small.append(sm_ref[j, at:at + members, :])
    small = small[0] if len(small) == 1 else jnp.concatenate(small, axis=1)
    so_ref[...] = small[:, :width]
    bo_ref[...] = small[:, width:]
    copy.wait()


def params(**kw):
    return pltpu.CompilerParams(vmem_limit_bytes=VMEM_LIMIT, **kw)


def whole(shape):
    return pl.BlockSpec(shape, lambda *_: (0,) * len(shape))


def exchange(nd, nf, bins, fr, ms, tab, bias, miss, s, so, w, ct):
    flocal, total = bins.shape
    width = tab.shape[1]
    count, (din, dout) = total // nf, w.shape
    parts = 8
    ins = (bins, fr, ms, tab, bias, miss, s, so)
    shapes = [jax.ShapeDtypeStruct(x, F32) for x in ((nf * 3 * flocal, count), (nf * flocal // 2 * width, 128), (count, din), (8, 128))]
    far = [jax.ShapeDtypeStruct(w.shape, d) for d in (BF16, F8, F8)]
    dma = pltpu.SemaphoreType.DMA
    anywhere = pl.BlockSpec(memory_space=pl.ANY)
    return pl.pallas_call(
        functools.partial(exchange_kernel, nd, nf),
        out_shape=shapes + far,
        in_specs=[whole(x.shape) for x in ins] + [anywhere] * 2,
        out_specs=[whole(x.shape) for x in shapes] + [anywhere] * 3,
        scratch_shapes=[pltpu.VMEM((3 * flocal, total), F32), pltpu.VMEM((din, count), F32), pltpu.VMEM(w.shape, F32),
                        pltpu.VMEM((parts, ct.shape[0] // parts) + ct.shape[1:], F32)]
        + [pltpu.VMEM(x.shape, x.dtype) for x in far]
        + [dma((parts + 1,)), dma((3,))] + [dma((nf - 1,))] * 4 + [dma((nf - 1, nd // 2 - 1))] * 2 + [dma((nf - 1,))] * 2,
        compiler_params=params(collective_id=0, has_side_effects=True),
    )(*ins, w, ct)


def forward(nf, e, s, wp, so, bo, ct, sc):
    count, din = e.shape
    members, dout = so.shape
    rows, tiles, block = count * members, count // TILE, TILE * members
    lag = lambda i: jnp.maximum(i - 1, 0)
    big = pl.BlockSpec((TILE, members, dout), lambda i: (lag(i), 0, 0))
    nat = pl.BlockSpec((block, dout), lambda i: (lag(i), 0))
    tra = pl.BlockSpec((dout, block), lambda i: (0, lag(i)))
    return pl.pallas_call(
        functools.partial(forward_kernel, nf),
        out_shape=[jax.ShapeDtypeStruct((count, members, dout), F32)]
        + [jax.ShapeDtypeStruct((rows, dout), d) for d in (BF16, F8, F8)]
        + [jax.ShapeDtypeStruct((dout, rows), d) for d in (BF16, F8, F8)]
        + [jax.ShapeDtypeStruct((members, 2 * dout), F32)],
        grid=(tiles + 1,),
        in_specs=[whole(e.shape), whole(s.shape)] + [pl.BlockSpec(memory_space=pl.ANY)] * 3 + [whole(so.shape), whole(bo.shape), big, whole(sc.shape)],
        out_specs=[big, nat, nat, nat, tra, tra, tra, whole((members, 2 * dout))],
        scratch_shapes=[pltpu.VMEM(so.shape, F32)] * 2 + [pltpu.VMEM(s.shape, F32), pltpu.VMEM(so.shape, F32), pltpu.VMEM(so.shape, F32)]
        + [pltpu.VMEM(w.shape, w.dtype) for w in wp] + [pltpu.SemaphoreType.DMA((3,))]
        + [pltpu.VMEM((block, din), d) for d in (BF16, F8, F8)] * 2
        + [pltpu.VMEM((block, dout), F32)] * 2,
        compiler_params=params(),
    )(e, s, *wp, so, bo, ct, sc)


def backward(nd, nf, e, s, zs, raw, t, wp, gp, gt, sc):
    count, din = e.shape
    members = s.shape[0]
    rows, dout = gp[0].shape
    step = rows // 4
    chunks, nchip = din // CHUNK, nd // 2
    per = chunks // nf
    ny, blk, half, sblk = nd // 4, CHUNK // nd // 2, 256 // 2, 256 // nd
    feats, flocal = CHUNK // 16, raw.shape[0] // (3 * nf)
    layout = (ny, 2, 2, blk, dout)
    shapes = [jax.ShapeDtypeStruct(x, F32) for x in ((2 * per,) + layout, (per, 256, 128), (nf, flocal, 128))]
    ins = (e, s, zs, raw, t)
    far = (*wp, *gp, *gt)
    dma = pltpu.SemaphoreType.DMA
    f32 = lambda *shape: pltpu.VMEM(shape, F32)
    return pl.pallas_call(
        functools.partial(backward_kernel, nd, nf),
        out_shape=shapes,
        in_specs=[whole(x.shape) for x in ins] + [whole(sc.shape)] + [pl.BlockSpec(memory_space=pl.ANY)] * len(far),
        out_specs=[whole(x.shape) for x in shapes],
        scratch_shapes=[pltpu.VMEM(x.shape, x.dtype) for x in far]
        + [f32(*s.shape)] * 2
        + [pltpu.VMEM((rows, CHUNK), d) for d in (BF16, F8, F8)] * 2
        + [f32(step, CHUNK)] * 2
        + [f32(count, CHUNK), f32(members, CHUNK), f32(CHUNK, count)]
        + [f32(2 * chunks, *layout), f32(chunks, 256, 128), f32(chunks, feats, count)]
        + [f32(chunks, *layout), f32(chunks, ny, blk, dout), f32(chunks, ny - 1, 2, blk, dout), f32(chunks, ny - 1, blk, dout),
           f32(chunks, blk, dout), f32(per, nf - 1, 2, blk, dout)]
        + [f32(chunks, half, 128), f32(chunks, nchip - 1, sblk, 128), f32(DIRECT, nd - 1, sblk, 128), f32(per, nf - 1, sblk, 128)]
        + [dma((9,))]
        + [dma((chunks,))] * 4 + [dma((chunks, ny - 1))] * 4 + [dma((chunks,))] * 2 + [dma((chunks,)), dma((per, nf - 1))]
        + [dma((per, nchip - 1))] * 2 + [dma((per,))] * 2 + [dma((chunks,)), dma((per, nf - 1))]
        + [dma((chunks,))] * 2 + [dma((chunks, nchip - 1))] * 2 + [dma((chunks,)), dma((per, nf - 1))]
        + [dma((per, nchip - 1))] * 2 + [dma((per,))] * 2
        + [dma((DIRECT, nd - 1))] * 4,
        compiler_params=params(collective_id=1, has_side_effects=True),
    )(*ins, sc, *far)


def final(nf, bins, gw, sm, fr):
    per, flocal = sm.shape[0], fr.shape[1]
    members, width = 32, gw.shape[1] // nf
    shapes = [jax.ShapeDtypeStruct(x, F32) for x in (
        (flocal, nf * 128), (flocal, 16, bins), (16, flocal), (16, flocal), (members, per * CHUNK), gw.shape, (members, width), (members, width))]
    ins = (gw, sm, fr)
    anywhere = pl.BlockSpec(memory_space=pl.ANY)
    return pl.pallas_call(functools.partial(final_kernel, nf, bins), out_shape=shapes,
                          in_specs=[anywhere] + [whole(x.shape) for x in ins[1:]],
                          out_specs=[whole(x.shape) for x in shapes],
                          scratch_shapes=[pltpu.SemaphoreType.DMA], compiler_params=params())(*ins)


def shards(nd, nf, bins, fractions, missing, bin_table, bin_bias, miss_vector, scale_in, weight, scale_out, bias_out, cotangent):
    raw, packed, e, sc, *wp = exchange(nd, nf, bins.T, fractions.T, missing.T, jnp.transpose(bin_table, (0, 2, 1)), bin_bias.T,
                                       miss_vector.T, scale_in, scale_out, weight, cotangent)
    hidden, *rest = forward(nf, e, scale_in, wp, scale_out, bias_out, cotangent, sc)
    gw, sm, fr = backward(nd, nf, e, scale_in, rest[6], raw, packed, wp, rest[:3], rest[3:6], sc)
    gw = gw.reshape(-1, weight.shape[1])
    frac, table, bias, miss, sin, gw, so, bo = final(nf, bin_table.shape[1], gw, sm, fr)
    return hidden, frac.T, jnp.transpose(table, (0, 2, 1)), bias.T, miss.T, sin, gw, so, bo


def solution(mesh):
    placed = (P("dp", "feat"), P("dp", "feat"), P("dp", "feat"), P("feat", None, None), P("feat", None), P("feat", None),
              P(), P(), P(), P(), P(("dp", "feat"), None, None))
    return jax.shard_map(
        functools.partial(shards, mesh.shape["dp"], mesh.shape["feat"]),
        mesh=mesh,
        in_specs=placed,
        out_specs=(P(("dp", "feat"), None, None), P("dp", "feat"), P("feat", None, None), P("feat", None), P("feat", None),
                   P(None, "feat"), P("feat", None), P(None, "feat"), P(None, "feat")),
        check_vma=False,
    )
```

```python
import functools

import jax
import jax.numpy as jnp
from jax import lax
from jax.experimental import pallas as pl
from jax.experimental.pallas import tpu as pltpu
from jax.sharding import PartitionSpec as P

F32, BF16, F8 = jnp.float32, jnp.bfloat16, jnp.float8_e4m3fn
VMEM_LIMIT = 63 << 20
TILE = 16
DIRECT = 2
CHUNK = 256
TOP = 224.0
TOP_WEIGHT = 400.0
LO = 256.0
GELU_A = 0.7978845608028654
GELU_B = GELU_A * 0.044715


def dot(a, b):
    return jnp.dot(a, b, preferred_element_type=F32)


def dot_nt(a, b):
    return lax.dot_general(a, b, (((1,), (1,)), ((), ())), preferred_element_type=F32)


def split3(x):
    hi = x.astype(BF16)
    return hi, x.astype(F8), ((x - hi.astype(F32)) * LO).astype(F8)


def split2(x):
    hi = x.astype(BF16)
    return hi, (x - hi.astype(F32)).astype(BF16)


def split3_weight(x):
    hi = x.astype(BF16)
    return hi, (x * (1.0 / LO)).astype(F8), (x - hi.astype(F32)).astype(F8)


def encode_pair(raw_ref, flocal, first):
    level = lax.broadcasted_iota(jnp.int32, (48, 128), 0).astype(F32)
    row = lax.broadcasted_iota(jnp.int32, (16, 128), 0)
    parts = []
    for f in (first, first + 1):
        b, fr, m = [raw_ref[pl.ds(f + k * flocal, 1), :] for k in range(3)]
        here = 1.0 - m
        parts.append(jnp.clip((b - level) + fr, 0.0, 1.0) * here)
        parts.append(jnp.where(row == 0, here, jnp.where(row == 1, m, 0.0)))
    return jnp.concatenate(parts, axis=0)


def table_pair(t_ref, p):
    blk = t_ref[pl.ds(pl.multiple_of(p * 16, 16), 16), :]
    lane = lax.broadcasted_iota(jnp.int32, (16, 128), 1)
    zero = jnp.zeros_like(blk)
    return jnp.concatenate([jnp.where(lane < 64, blk, zero), jnp.where(lane < 64, zero, blk)], axis=0)


def send(src, dst, ssem, rsem, **where):
    return pltpu.make_async_remote_copy(src_ref=src, dst_ref=dst, send_sem=ssem, recv_sem=rsem, device_id=where,
                                        device_id_type=pl.DeviceIdType.MESH)


def greet(partners):
    barrier = pltpu.get_barrier_semaphore()
    for where in partners:
        pl.semaphore_signal(barrier, inc=1, device_id=where, device_id_type=pl.DeviceIdType.MESH)
    return lambda: pl.semaphore_wait(barrier, len(partners))


def exchange_kernel(nd, nf, bins_ref, fr_ref, ms_ref, tab_ref, bias_ref, miss_ref, s_ref, so_ref, w_in, ct_in,
                    raw_ref, t_ref, e_ref, sc_ref, wh_out, w8_out, wl_out,
                    mine, et, w, ct, wh, w8, wl, load, store, r_s, r_r, x_s, x_r, y_s, y_r, z_s, z_r):
    flocal, total = bins_ref.shape
    count = total // nf
    bins, width = tab_ref.shape[2], tab_ref.shape[1]
    me, z = lax.axis_index("dp"), lax.axis_index("feat")
    nchip = nd // 2
    core, chip = lax.rem(me, 2), me // 2
    partner = me + 1 - 2 * core
    parts = ct.shape[0]
    step = ct_in.shape[0] // parts

    ready = greet([{"feat": lax.rem(z + o, nf)} for o in range(1, nf)]
                  + [{"dp": 2 * lax.rem(chip + o, nchip) + core} for o in range(1, nchip)] + [{"dp": partner}])
    loads = [pltpu.make_async_copy(w_in, w, load.at[0])] + [
        pltpu.make_async_copy(ct_in.at[pl.ds(i * step, step)], ct.at[i], load.at[i + 1]) for i in range(parts)]
    for copy in loads:
        copy.start()

    def rows(q):
        return pl.ds(pl.multiple_of(q * (3 * flocal), 3 * flocal), 3 * flocal)

    size = flocal // 2 * width // nd

    def entries(q, piece, n):
        return t_ref.at[pl.ds(pl.multiple_of(q * (nd * size) + piece * size, 8), n * size)]

    mine[0:flocal, :] = bins_ref[...].astype(F32)
    mine[flocal:2 * flocal, :] = fr_ref[...]
    mine[2 * flocal:, :] = ms_ref[...].astype(F32)
    raw_ref[rows(z), :] = mine[:, pl.ds(pl.multiple_of(z * count, count), count)]
    blank = jnp.zeros((width, 64 - bins - 2), F32)
    for p in range(flocal // 2):
        block = []
        for f in (2 * p, 2 * p + 1):
            block += [tab_ref[f], bias_ref[:, f:f + 1], miss_ref[:, f:f + 1], blank]
        t_ref[pl.ds(pl.multiple_of(z * (flocal // 2 * width) + p * width, width), width), :] = jnp.concatenate(block, axis=1)

    def send_raw(o, q):
        to = lax.rem(z + o, nf)
        return send(mine.at[:, pl.ds(pl.multiple_of(to * count, count), count)], raw_ref.at[rows(q)],
                    r_s.at[o - 1], r_r.at[o - 1], feat=to)

    def send_x(o, q):
        r = entries(q, core * nchip + chip, 1)
        return send(r, r, x_s.at[o - 1], x_r.at[o - 1], feat=lax.rem(z + o, nf))

    def send_y(o, k, c):
        r = entries(lax.rem(z - o + nf, nf), core * nchip + c, 1)
        return send(r, r, y_s.at[o - 1, k - 1], y_r.at[o - 1, k - 1], dp=2 * lax.rem(chip + k, nchip) + core)

    def send_z(o, side):
        r = entries(lax.rem(z - o + nf, nf), side * nchip, nchip)
        return send(r, r, z_s.at[o - 1], z_r.at[o - 1], dp=partner)

    others = range(1, nf)
    ready()
    for o in others:
        send_x(o, z).start()
    for o in others:
        send_raw(o, z).start()

    def top(v):
        return jnp.maximum(jnp.max(jnp.max(jnp.abs(v), axis=0, keepdims=True), axis=1, keepdims=True), 1e-30)

    pairs = flocal // 2
    at_once = min(16, pairs)
    entries_local = flocal * width

    def embed(q):
        def body(j, c):
            for k in range(at_once):
                p = q * pairs + j * at_once + k
                first = q * (3 * flocal) + 2 * (j * at_once + k)
                lh, ll = split2(table_pair(t_ref, p))
                eh, el = split2(encode_pair(raw_ref, flocal, first))
                both = dot(jnp.concatenate([lh, ll], axis=0), eh)
                et[pl.ds(pl.multiple_of(p * 32, 32), 32), :] = both[:32] + both[32:] + dot(lh, el)
            return c

        lax.fori_loop(0, pairs // at_once, body, 0)
        for j in range(entries_local // 128):
            at = pl.ds(pl.multiple_of(q * entries_local + j * 128, 128), 128)
            e_ref[:, at] = et[at, :].T

    embed(z)
    for o in others:
        send_x(o, lax.rem(z - o + nf, nf)).wait_recv()
        for k in range(1, nchip):
            send_y(o, k, chip).start()

    loads[0].wait()
    sw = TOP_WEIGHT / top(w[...])
    for i in range(0, w.shape[0], 256):
        r = slice(i, i + 256)
        wh[r, :], w8[r, :], wl[r, :] = split3_weight(w[r, :] * sw)
    stores = [pltpu.make_async_copy(i, o, store.at[k]) for k, (i, o) in enumerate(((wh, wh_out), (w8, w8_out), (wl, wl_out)))]
    for copy in stores:
        copy.start()

    for o in others:
        for k in range(1, nchip):
            send_y(o, k, lax.rem(chip - k + nchip, nchip)).wait_recv()
        send_z(o, core).start()
    tc = jnp.full((1, 1), 1e-30, F32)
    for i in range(parts):
        loads[i + 1].wait()
        tc = jnp.maximum(tc, top(ct[i].reshape(-1, ct.shape[-1])))
    for o in others:
        q = lax.rem(z - o + nf, nf)
        send_z(o, 1 - core).wait_recv()
        send_raw(o, q).wait_recv()
        embed(q)
    sx = TOP / (top(et[...]) * top(s_ref[...]))
    sg = TOP / (1.2 * tc * top(so_ref[...]))
    for k, v in enumerate((sx, sw, sg, 1.0 / (sx * sw), 1.0 / (sx * sw), 1.0 / (sg * sx), 1.0 / (sg * sw), 1.0 / (sg * sw))):
        sc_ref[k:k + 1, :] = jnp.broadcast_to(v, (1, 128))
    for copy in stores:
        copy.wait()
    for o in others:
        send_raw(o, z).wait_send()
        send_x(o, z).wait_send()
        for k in range(1, nchip):
            send_y(o, k, chip).wait_send()
        send_z(o, core).wait_send()


def forward_kernel(nf, e_ref, s_ref, wh_in, w8_in, wl_in, so_ref, bo_ref, ct_ref, sc_ref,
                   hid_ref, gh_ref, g8_ref, gl_ref, th_ref, t8_ref, tl_ref, z_ref,
                   gs_ref, gb_ref, s1, so1, so2, wh_ref, w8_ref, wl_ref, load, xh0, x80, xl0, xh1, x81, xl1, pre0, pre1):
    i = pl.program_id(0)
    tiles = pl.num_programs(0) - 1
    members, width_out = so_ref.shape
    rows = TILE * members
    x = ((xh0, x80, xl0), (xh1, x81, xl1))
    pre = (pre0, pre1)

    def prepare(tile, to):
        for n in range(TILE):
            v = s1[...] * e_ref[pl.ds(tile * TILE + n, 1), :]
            r = slice(n * members, (n + 1) * members)
            to[0][r, :], to[1][r, :], to[2][r, :] = split3(v)

    def multiply(a, to):
        to[...] = dot(a[0][...], wh_ref[...]) + (dot(a[1][...], wl_ref[...]) + dot(a[2][...], w8_ref[...]))

    def finish(p):
        for h0 in range(0, width_out, 128):
            hs = slice(h0, h0 + 128)
            sa, sb, bo = so1[:, hs], so2[:, hs], bo_ref[:, hs]
            gs, gb = gs_ref[:, hs], gb_ref[:, hs]
            for n in range(TILE):
                r = slice(n * members, (n + 1) * members)
                q = p[r, hs]
                v = q * sa + bo
                v2 = v * v
                half = 0.5 + 0.5 * jnp.tanh(v * (GELU_B * v2 + GELU_A))
                hid = v * half
                hid_ref[n, :, hs] = hid
                g = half + hid * (1.0 - half) * ((6.0 * GELU_B) * v2 + 2.0 * GELU_A)
                ga = ct_ref[n, :, hs] * g
                gs = gs + ga * q
                gb = gb + ga
                gh_ref[r, hs], g8_ref[r, hs], gl_ref[r, hs] = split3(ga * sb)
            gs_ref[:, hs], gb_ref[:, hs] = gs, gb
        th_ref[...] = gh_ref[...].T
        t8_ref[...] = g8_ref[...].T
        tl_ref[...] = gl_ref[...].T

    @pl.when(i == 0)
    def _():
        loads = [pltpu.make_async_copy(a, b, load.at[k]) for k, (a, b) in enumerate(
            ((wh_in, wh_ref), (w8_in, w8_ref), (wl_in, wl_ref)))]
        for copy in loads:
            copy.start()
        s1[...] = s_ref[...] * sc_ref[0:0 + 1, 0:1]
        so1[...] = so_ref[...] * sc_ref[3:3 + 1, 0:1]
        so2[...] = so_ref[...] * sc_ref[2:2 + 1, 0:1]
        gs_ref[...] = jnp.zeros_like(gs_ref)
        gb_ref[...] = jnp.zeros_like(gb_ref)
        prepare(0, x[0])
        for copy in loads:
            copy.wait()
        prepare(1, x[1])
        multiply(x[0], pre[0])

    for par in (0, 1):
        @pl.when((i > 0) & (i < tiles) & (i % 2 == par))
        def _():
            finish(pre[1 - par])
            prepare(jnp.minimum(i + 1, tiles - 1), x[1 - par])
            multiply(x[par], pre[par])

    @pl.when(i == tiles)
    def _():
        finish(pre[1])
        part = width_out // nf
        for o in range(nf):
            z_ref[:, 2 * o * part:(2 * o + 1) * part] = gs_ref[:, o * part:(o + 1) * part] * sc_ref[4:4 + 1, 0:1]
            z_ref[:, (2 * o + 1) * part:(2 * o + 2) * part] = gb_ref[:, o * part:(o + 1) * part]


def backward_kernel(nd, nf, e_ref, s_ref, z_ref, raw_ref, t_ref, sc_ref, wh_in, w8_in, wl_in, gh_in, g8_in, gl_in,
                    th_in, t8_in, tl_in, gw_out, sm_out, fr_out,
                    wh, w8, wl, gh, g8l, th, t8, tl, wcat, s1, s2, xh0, x80, xl0, xh1, x81, xl1, g0, g1, ge, gsin, et,
                    gw, sm, gf, ra, rp, rq, rp2, rq2, rc, ru, rb, r1, r2,
                    load, a_s, a_r, p_s, p_r, q_s, q_r, p2_s, p2_r, q2_s, q2_r, c_s, c_r, d_s, d_r, e_s, e_r, f_s, f_r,
                    ua_s, ua_r, ub_s, ub_r, uc_s, uc_r, ud_s, ud_r, ue_s, ue_r, u_s, u_r, y_s, y_r):
    members, width_in = s_ref.shape
    rows = gh.shape[0]
    count = e_ref.shape[0]
    chunks = width_in // CHUNK
    direct = chunks - DIRECT
    per = chunks // nf
    nx, ny, nchip = 2, nd // 4, nd // 2
    blk, dout = gw.shape[4], gw.shape[5]
    half, sblk = sm.shape[1] // 2, sm.shape[1] // nd
    feats = CHUNK // 16
    flocal = fr_out.shape[1]
    me, z = lax.axis_index("dp"), lax.axis_index("feat")
    core, chip = lax.rem(me, 2), me // 2
    cx, cy = lax.rem(chip, nx), chip // nx
    partner = me + 1 - 2 * core

    ready = greet([{"dp": lax.rem(me + o, nd)} for o in range(1, nd)] + [{"feat": lax.rem(z + o, nf)} for o in range(1, nf)])
    loads = [pltpu.make_async_copy(i, o, load.at[k]) for k, (i, o) in enumerate(
        ((th_in, th), (t8_in, t8), (tl_in, tl), (wh_in, wh), (w8_in, w8), (wl_in, wl), (gh_in, gh), (g8_in, g8l.at[:, :dout]), (gl_in, g8l.at[:, dout:])))]
    for copy in loads[:3]:
        copy.start()

    def aligned(i, n):
        return pl.ds(pl.multiple_of(i, n), n)

    def owner(i):
        return lax.rem(i + nf // 2 + 1, nf)

    def place(i):
        return owner(i) * per + i // nf

    def far(i):
        return lax.rem(owner(i) - z + nf, nf)

    def device(y, x):
        return 2 * (y * nx + x) + core

    def other_y(k):
        return lax.rem(cy + k, ny)

    def from_y(k):
        return lax.rem(cy - k + ny, ny)

    def own(i):
        return 2 * place(i) + core

    def send_a(i):
        return send(gw.at[2 * place(i) + 1 - core], ra.at[i], a_s.at[i], a_r.at[i], dp=partner)

    def send_p(i):
        return send(gw.at[own(i), :, 1 - cx, 0], rp.at[i], p_s.at[i], p_r.at[i], dp=device(cy, 1 - cx))

    def send_q(i, k):
        return send(gw.at[own(i), other_y(k), :, 1], rq.at[i, k - 1], q_s.at[i, k - 1], q_r.at[i, k - 1], dp=device(other_y(k), cx))

    def send_p2(i, k):
        return send(gw.at[own(i), other_y(k), cx, 0], rp2.at[i, k - 1], p2_s.at[i, k - 1], p2_r.at[i, k - 1], dp=device(other_y(k), cx))

    def send_q2(i):
        return send(gw.at[own(i), cy, 1 - cx, 1], rq2.at[i], q2_s.at[i], q2_r.at[i], dp=device(cy, 1 - cx))

    def send_c(i, k):
        j = i // nf
        return send(gw.at[own(i), cy, cx], rc.at[j, k - 1], c_s.at[i], c_r.at[j, k - 1], feat=owner(i))

    def send_d(i, o, q):
        j = i // nf
        return send(gw.at[own(i), cy, cx], gw_out.at[2 * j + core, q // nx, lax.rem(q, nx)], d_s.at[j, o - 1], d_r.at[j, o - 1],
                    dp=2 * lax.rem(chip + o, nchip) + core)

    def send_e(i, side):
        j = i // nf
        return send(gw_out.at[2 * j + side], gw_out.at[2 * j + side], e_s.at[j], e_r.at[j], dp=partner)

    def step_b(i):
        send_a(i).wait_recv()
        gw[own(i)] += ra[i]
        send_p(i).start()
        for k in range(1, ny):
            send_q(i, k).start()

    def step_b2(i):
        send_p(i).wait_recv()
        gw[own(i), :, cx, 0] += rp[i]
        for k in range(1, ny):
            send_q(i, k).wait_recv()
            gw[own(i), cy, :, 1] += rq[i, k - 1]
        for k in range(1, ny):
            send_p2(i, k).start()
        send_q2(i).start()

    def step_c(i):
        send_q2(i).wait_recv()
        gw[own(i), cy, cx, 1] += rq2[i]
        for k in range(1, ny):
            send_p2(i, k).wait_recv()
            gw[own(i), cy, cx, 0] += rp2[i, k - 1]

        @pl.when(owner(i) != z)
        def _():
            send_c(i, far(i)).start()

    def step_d(i):
        @pl.when(owner(i) == z)
        def _():
            total = gw[own(i), cy, cx]
            for k in range(1, nf):
                send_c(i, k).wait_recv()
                total = total + rc[i // nf, k - 1]
            gw[own(i), cy, cx] = total
            gw_out[2 * (i // nf) + core, cy, cx] = total
            for o in range(1, nchip):
                send_d(i, o, chip).start()

    def step_e(i):
        @pl.when(owner(i) == z)
        def _():
            for o in range(1, nchip):
                send_d(i, o, lax.rem(chip - o + nchip, nchip)).wait_recv()
            send_e(i, core).start()

    def step_f(i):
        @pl.when(owner(i) == z)
        def _():
            send_e(i, 1 - core).wait_recv()

    def drain(i):
        send_a(i).wait_send()
        send_p(i).wait_send()
        send_q2(i).wait_send()
        for k in range(1, ny):
            send_q(i, k).wait_send()
            send_p2(i, k).wait_send()

        @pl.when(owner(i) != z)
        def _():
            send_c(i, far(i)).wait_send()

        @pl.when(owner(i) == z)
        def _():
            for o in range(1, nchip):
                send_d(i, o, chip).wait_send()
            send_e(i, core).wait_send()

    def rows_of(q, side):
        return aligned(side * half + q * sblk, sblk)

    def whole_half(side):
        return aligned(side * half, half)

    def send_ua(i):
        return send(sm.at[i, whole_half(1 - core)], ru.at[i], ua_s.at[i], ua_r.at[i], dp=partner)

    def send_ub(i, o):
        to = lax.rem(chip + o, nchip)
        return send(sm.at[i, rows_of(to, core)], rb.at[i, o - 1], ub_s.at[i, o - 1], ub_r.at[i, o - 1], dp=2 * to + core)

    def send_uc(i, k):
        j = i // nf
        return send(sm.at[i, rows_of(chip, core)], r2.at[j, k - 1], uc_s.at[i], uc_r.at[j, k - 1], feat=owner(i))

    def send_ud(i, o, q):
        j = i // nf
        return send(sm.at[i, rows_of(chip, core)], sm_out.at[j, rows_of(q, core)], ud_s.at[j, o - 1], ud_r.at[j, o - 1],
                    dp=2 * lax.rem(chip + o, nchip) + core)

    def send_ue(i, side):
        j = i // nf
        r = sm_out.at[j, whole_half(side)]
        return send(r, r, ue_s.at[j], ue_r.at[j], dp=partner)

    def send_u(i, o):
        to = lax.rem(me + o, nd)
        return send(sm.at[i, rows_of(to // 2, lax.rem(to, 2))], r1.at[i - direct, o - 1], u_s.at[i - direct, o - 1],
                    u_r.at[i - direct, o - 1], dp=to)

    def send_y(i, o, q):
        j = i - direct
        return send(sm.at[i, rows_of(chip, core)], sm_out.at[i // nf, rows_of(q // 2, lax.rem(q, 2))], y_s.at[j, o - 1], y_r.at[j, o - 1],
                    dp=lax.rem(me + o, nd))

    def send_f(i, k, src):
        j = i // nf
        return send(gf.at[i], fr_out.at[src, aligned(j * feats, feats)], f_s.at[i], f_r.at[j, k - 1], feat=owner(i))

    def start_f(i):
        @pl.when(owner(i) != z)
        def _():
            send_f(i, far(i), z).start()

        @pl.when(owner(i) == z)
        def _():
            fr_out[z, aligned((i // nf) * feats, feats), :] = gf[i]

    def wait_f(i):
        @pl.when(owner(i) == z)
        def _():
            for k in range(1, nf):
                send_f(i, k, lax.rem(z - k + nf, nf)).wait_recv()

    def start_ua(i):
        send_ua(i).start()
        start_f(i)

    def step_ub(i):
        send_ua(i).wait_recv()
        sm[i, whole_half(core), :] += ru[i]
        for o in range(1, nchip):
            send_ub(i, o).start()

    def step_uc(i):
        r = rows_of(chip, core)
        total = sm[i, r, :]
        for o in range(1, nchip):
            send_ub(i, o).wait_recv()
            total = total + rb[i, o - 1]
        sm[i, r, :] = total

        @pl.when(owner(i) != z)
        def _():
            send_uc(i, far(i)).start()

    def gather_z(i):
        r = rows_of(chip, core)
        total = sm[i, r, :]
        for k in range(1, nf):
            send_uc(i, k).wait_recv()
            total = total + r2[i // nf, k - 1]
        sm[i, r, :] = total
        sm_out[i // nf, r, :] = total

    def step_ud(i):
        @pl.when(owner(i) == z)
        def _():
            gather_z(i)
            for o in range(1, nchip):
                send_ud(i, o, chip).start()

    def step_ue(i):
        @pl.when(owner(i) == z)
        def _():
            for o in range(1, nchip):
                send_ud(i, o, lax.rem(chip - o + nchip, nchip)).wait_recv()
            send_ue(i, core).start()

    def step_uf(i):
        @pl.when(owner(i) == z)
        def _():
            send_ue(i, 1 - core).wait_recv()

        wait_f(i)

    def drain_small(i):
        send_ua(i).wait_send()
        for o in range(1, nchip):
            send_ub(i, o).wait_send()

        @pl.when(owner(i) != z)
        def _():
            send_uc(i, far(i)).wait_send()
            send_f(i, far(i), z).wait_send()

        @pl.when(owner(i) == z)
        def _():
            for o in range(1, nchip):
                send_ud(i, o, chip).wait_send()
            send_ue(i, core).wait_send()

    def start_u(i):
        for o in range(1, nd):
            send_u(i, o).start()

    def step_v(i):
        r = rows_of(chip, core)
        total = sm[i, r, :]
        for o in range(1, nd):
            send_u(i, o).wait_recv()
            total = total + r1[i - direct, o - 1]
        sm[i, r, :] = total

        @pl.when(owner(i) != z)
        def _():
            send_uc(i, far(i)).start()

    def step_y(i):
        @pl.when(owner(i) == z)
        def _():
            gather_z(i)
            for o in range(1, nd):
                send_y(i, o, me).start()

    def step_w(i):
        @pl.when(owner(i) == z)
        def _():
            for o in range(1, nd):
                send_y(i, o, lax.rem(me - o + nd, nd)).wait_recv()

        wait_f(i)

    def drain_direct(i):
        for o in range(1, nd):
            send_u(i, o).wait_send()

        @pl.when(owner(i) != z)
        def _():
            send_uc(i, far(i)).wait_send()
            send_f(i, far(i), z).wait_send()

        @pl.when(owner(i) == z)
        def _():
            for o in range(1, nd):
                send_y(i, o, me).wait_send()

    def when_chunk(i, f, first=0, end=chunks):
        @pl.when((i >= first) & (i < end))
        def _():
            f(i)

    start_a = lambda i: send_a(i).start()
    stages = ((start_a, (0, 1, 2, 3)), (step_b, (1, 2, 3, 4)), (step_b2, (3, 4, 5, 6)), (step_c, (5, 6, 7, 8)),
              (step_d, (7, 8, 9, 10)), (step_e, (9, 10, 11)))

    def pairs(k, among):
        for step, times in stages:
            for j, at in enumerate(times):
                if at in among:
                    @pl.when(k == at)
                    def _():
                        for i in (2 * j, 2 * j + 1):
                            step(i)

    def early(j):
        @pl.when(j == 0)
        def _():
            ready()

        pairs(j, range(4))

    def late(t):
        when_chunk(t - 1, start_ua, 0, direct)
        when_chunk(t - 1, start_u, direct)
        when_chunk(t - 1, start_f, direct)
        pairs(t + 4, range(4, 12))
        when_chunk(t - 2, step_ub, 0, direct)
        when_chunk(t - 4, step_uc, 0, direct)
        when_chunk(t - 6, step_ud, 0, direct)

    x = ((xh0, x80, xl0), (xh1, x81, xl1))
    s1[...] = s_ref[...] * sc_ref[0:0 + 1, 0:1]
    s2[...] = s_ref[...] * sc_ref[6:6 + 1, 0:1]

    def cols(i):
        return aligned(place(i) * CHUNK, CHUNK)

    def prepare(i, to):
        for n in range(0, count, TILE):
            v = (e_ref[n:n + TILE, cols(i)][:, None, :] * s1[:, cols(i)][None]).reshape(TILE * members, CHUNK)
            r = slice(n * members, (n + TILE) * members)
            to[0][r, :], to[1][r, :], to[2][r, :] = split3(v)

    prepare(0, x[0])
    for copy in loads[:3]:
        copy.wait()
    for copy in loads[3:]:
        copy.start()

    def weights(j, carry):
        for par in (0, 1):
            i = 2 * j + par
            xh, x8, xl = x[par]
            r = dot(th[...], xh[...]) + (dot(t8[...], xl[...]) + dot(tl[...], x8[...])) * (1.0 / LO)
            gw[aligned(2 * place(i), 2)] = (r.T * sc_ref[5:5 + 1, 0:1]).reshape(2, ny, nx, 2, blk, dout)
            prepare(jnp.minimum(i + 1, chunks - 1), x[1 - par])
        early(j)
        return carry

    lax.fori_loop(0, chunks // 2, weights, 0)

    for copy in loads[3:]:
        copy.wait()
    gsin[...] = jnp.zeros_like(gsin)
    g1[...] = jnp.zeros_like(g1)
    step = g0.shape[0]
    objs = step // members
    parts = rows // step

    def finish(i, t, g):
        g3 = g[...].reshape(objs, members, CHUNK)
        ns = slice(t * objs, (t + 1) * objs)
        ge[ns, :] = jnp.sum(g3 * s2[:, cols(i)][None], axis=1)
        gsin[...] += jnp.sum(g3 * e_ref[ns, cols(i)][:, None, :], axis=0)

    def table(i):
        c = place(i)
        first = c * feats
        base = (first // flocal) * (3 * flocal) + lax.rem(first, flocal)
        for j in range(CHUNK // 128):
            et[j * 128:(j + 1) * 128, :] = ge[:, j * 128:(j + 1) * 128].T
        lane = lax.broadcasted_iota(jnp.int32, (16, 128), 1)
        for p in range(feats // 2):
            row = base + 2 * p
            enc = encode_pair(raw_ref, flocal, row)
            gh_, gl_ = split2(et[p * 32:(p + 1) * 32, :])
            eh, el = split2(enc)
            both = dot_nt(jnp.concatenate([gh_, gl_], axis=0), eh)
            full = both[:32] + both[32:] + dot_nt(gh_, el)
            sm[i, p * 16:(p + 1) * 16, :] = jnp.where(lane < 64, full[:16], full[16:])
        at = feats * 8
        for j in range(CHUNK // 128):
            sm[i, at:at + members, :] = gsin[:, j * 128:(j + 1) * 128] * sc_ref[7:7 + 1, 0:1]
            at += members
        sm[i, at:at + members, :] = z_ref[:, aligned(c * 128, 128)]
        at += members
        sm[i, at:, :] = jnp.zeros_like(sm[i, at:, :])
        gsin[...] = jnp.zeros_like(gsin)

    def slopes(i):
        c = place(i)
        first = c * feats
        base = (first // flocal) * (3 * flocal) + lax.rem(first, flocal)
        level = lax.broadcasted_iota(jnp.int32, (64, 128), 0).astype(F32)
        for p in range(feats // 2):
            row = base + 2 * p
            lh, ll = split2(table_pair(t_ref, c * (feats // 2) + p))
            g = et[p * 32:(p + 1) * 32, :]
            hot = []
            for f in (row, row + 1):
                here = 1.0 - raw_ref[pl.ds(f + 2 * flocal, 1), :]
                hot.append(jnp.where(level == raw_ref[pl.ds(f, 1), :], here, 0.0))
            one = jnp.concatenate(hot, axis=0).astype(BF16)
            both = dot(jnp.concatenate([lh, ll], axis=0), one)
            picked = (both[:32] + both[32:]) * g
            gf[i, 2 * p:2 * p + 1, :] = jnp.sum(picked[:16], axis=0, keepdims=True)
            gf[i, 2 * p + 1:2 * p + 2, :] = jnp.sum(picked[16:], axis=0, keepdims=True)

    def inputs(i, carry):
        before = jnp.maximum(i - 1, 0)
        wc = wh[cols(i), :]
        wcat[:, :dout] = wl[cols(i), :]
        wcat[:, dout:] = w8[cols(i), :]
        finish(before, parts - 1, g1)
        table(before)
        slopes(before)
        for t in range(parts):
            to, fro = (g0, g1) if t % 2 == 0 else (g1, g0)
            rs = slice(t * step, (t + 1) * step)
            to[...] = dot_nt(gh[rs, :], wc) + dot_nt(g8l[rs, :], wcat[...])
            if t > 0:
                finish(i, t - 1, fro)
        late(i)
        return carry

    lax.fori_loop(0, chunks, inputs, 0)
    last = chunks - 1
    finish(last, parts - 1, g1)
    table(last)
    start_u(last)
    slopes(last)
    start_f(last)
    step_e(last - 1)
    step_e(last)
    step_v(last - 1)
    for i in range(direct - 2, direct):
        step_uc(i)
    for i in range(direct - 4, direct - 2):
        step_ud(i)
    for i in range(direct - 4):
        step_ue(i)
    step_v(last)
    step_y(last - 1)
    for i in range(direct - 2, direct):
        step_ud(i)
    for i in range(direct - 4, direct - 2):
        step_ue(i)
    step_y(last)
    for i in range(direct - 2, direct):
        step_ue(i)
    for i in range(chunks):
        step_f(i)
    for i in range(direct):
        step_uf(i)
    step_w(last - 1)

    def close(i, carry):
        drain(i)
        when_chunk(i, drain_small, 0, direct)
        when_chunk(i, drain_direct, direct)
        return carry

    lax.fori_loop(0, chunks, close, 0)
    step_w(last)


def final_kernel(nf, bins, gw_in, sm_ref, fr_ref, frac_ref, tab_ref, bias_ref, miss_ref, sin_ref, gw_out, so_ref, bo_ref, sem):
    copy = pltpu.make_async_copy(gw_in, gw_out, sem)
    copy.start()
    flocal = fr_ref.shape[1]
    for o in range(nf):
        frac_ref[:, o * 128:(o + 1) * 128] = fr_ref[o]
    members = sin_ref.shape[0]
    feats = CHUNK // 16
    width = so_ref.shape[1]
    small = []
    for j in range(sm_ref.shape[0]):
        for p in range(feats // 2):
            block = sm_ref[j, p * 16:(p + 1) * 16, :]
            for odd in (0, 1):
                f = j * feats + 2 * p + odd
                tab_ref[f] = block[:, odd * 64:odd * 64 + bins]
                bias_ref[:, f:f + 1] = block[:, odd * 64 + bins:odd * 64 + bins + 1]
                miss_ref[:, f:f + 1] = block[:, odd * 64 + bins + 1:odd * 64 + bins + 2]
        at = feats * 8
        for q in range(CHUNK // 128):
            sin_ref[:, j * CHUNK + q * 128:j * CHUNK + (q + 1) * 128] = sm_ref[j, at:at + members, :]
            at += members
        small.append(sm_ref[j, at:at + members, :])
    small = small[0] if len(small) == 1 else jnp.concatenate(small, axis=1)
    so_ref[...] = small[:, :width]
    bo_ref[...] = small[:, width:]
    copy.wait()


def params(**kw):
    return pltpu.CompilerParams(vmem_limit_bytes=VMEM_LIMIT, **kw)


def whole(shape):
    return pl.BlockSpec(shape, lambda *_: (0,) * len(shape))


def exchange(nd, nf, bins, fr, ms, tab, bias, miss, s, so, w, ct):
    flocal, total = bins.shape
    width = tab.shape[1]
    count, (din, dout) = total // nf, w.shape
    parts = 8
    ins = (bins, fr, ms, tab, bias, miss, s, so)
    shapes = [jax.ShapeDtypeStruct(x, F32) for x in ((nf * 3 * flocal, count), (nf * flocal // 2 * width, 128), (count, din), (8, 128))]
    far = [jax.ShapeDtypeStruct(w.shape, d) for d in (BF16, F8, F8)]
    dma = pltpu.SemaphoreType.DMA
    anywhere = pl.BlockSpec(memory_space=pl.ANY)
    return pl.pallas_call(
        functools.partial(exchange_kernel, nd, nf),
        out_shape=shapes + far,
        in_specs=[whole(x.shape) for x in ins] + [anywhere] * 2,
        out_specs=[whole(x.shape) for x in shapes] + [anywhere] * 3,
        scratch_shapes=[pltpu.VMEM((3 * flocal, total), F32), pltpu.VMEM((din, count), F32), pltpu.VMEM(w.shape, F32),
                        pltpu.VMEM((parts, ct.shape[0] // parts) + ct.shape[1:], F32)]
        + [pltpu.VMEM(x.shape, x.dtype) for x in far]
        + [dma((parts + 1,)), dma((3,))] + [dma((nf - 1,))] * 4 + [dma((nf - 1, nd // 2 - 1))] * 2 + [dma((nf - 1,))] * 2,
        compiler_params=params(collective_id=0, has_side_effects=True),
    )(*ins, w, ct)


def forward(nf, e, s, wp, so, bo, ct, sc):
    count, din = e.shape
    members, dout = so.shape
    rows, tiles, block = count * members, count // TILE, TILE * members
    lag = lambda i: jnp.maximum(i - 1, 0)
    big = pl.BlockSpec((TILE, members, dout), lambda i: (lag(i), 0, 0))
    nat = pl.BlockSpec((block, dout), lambda i: (lag(i), 0))
    tra = pl.BlockSpec((dout, block), lambda i: (0, lag(i)))
    return pl.pallas_call(
        functools.partial(forward_kernel, nf),
        out_shape=[jax.ShapeDtypeStruct((count, members, dout), F32)]
        + [jax.ShapeDtypeStruct((rows, dout), d) for d in (BF16, F8, F8)]
        + [jax.ShapeDtypeStruct((dout, rows), d) for d in (BF16, F8, F8)]
        + [jax.ShapeDtypeStruct((members, 2 * dout), F32)],
        grid=(tiles + 1,),
        in_specs=[whole(e.shape), whole(s.shape)] + [pl.BlockSpec(memory_space=pl.ANY)] * 3 + [whole(so.shape), whole(bo.shape), big, whole(sc.shape)],
        out_specs=[big, nat, nat, nat, tra, tra, tra, whole((members, 2 * dout))],
        scratch_shapes=[pltpu.VMEM(so.shape, F32)] * 2 + [pltpu.VMEM(s.shape, F32), pltpu.VMEM(so.shape, F32), pltpu.VMEM(so.shape, F32)]
        + [pltpu.VMEM(w.shape, w.dtype) for w in wp] + [pltpu.SemaphoreType.DMA((3,))]
        + [pltpu.VMEM((block, din), d) for d in (BF16, F8, F8)] * 2
        + [pltpu.VMEM((block, dout), F32)] * 2,
        compiler_params=params(),
    )(e, s, *wp, so, bo, ct, sc)


def backward(nd, nf, e, s, zs, raw, t, wp, gp, gt, sc):
    count, din = e.shape
    members = s.shape[0]
    rows, dout = gp[0].shape
    step = rows // 16
    chunks, nchip = din // CHUNK, nd // 2
    per = chunks // nf
    ny, blk, half, sblk = nd // 4, CHUNK // nd // 2, 256 // 2, 256 // nd
    feats, flocal = CHUNK // 16, raw.shape[0] // (3 * nf)
    layout = (ny, 2, 2, blk, dout)
    shapes = [jax.ShapeDtypeStruct(x, F32) for x in ((2 * per,) + layout, (per, 256, 128), (nf, flocal, 128))]
    ins = (e, s, zs, raw, t)
    far = (*wp, *gp, *gt)
    dma = pltpu.SemaphoreType.DMA
    f32 = lambda *shape: pltpu.VMEM(shape, F32)
    return pl.pallas_call(
        functools.partial(backward_kernel, nd, nf),
        out_shape=shapes,
        in_specs=[whole(x.shape) for x in ins] + [whole(sc.shape)] + [pl.BlockSpec(memory_space=pl.ANY)] * len(far),
        out_specs=[whole(x.shape) for x in shapes],
        scratch_shapes=[pltpu.VMEM(x.shape, x.dtype) for x in (*wp, gp[0])] + [pltpu.VMEM((rows, 2 * dout), F8)]
        + [pltpu.VMEM(x.shape, x.dtype) for x in gt] + [pltpu.VMEM((CHUNK, 2 * dout), F8)]
        + [f32(*s.shape)] * 2
        + [pltpu.VMEM((rows, CHUNK), d) for d in (BF16, F8, F8)] * 2
        + [f32(step, CHUNK)] * 2
        + [f32(count, CHUNK), f32(members, CHUNK), f32(CHUNK, count)]
        + [f32(2 * chunks, *layout), f32(chunks, 256, 128), f32(chunks, feats, count)]
        + [f32(chunks, *layout), f32(chunks, ny, blk, dout), f32(chunks, ny - 1, 2, blk, dout), f32(chunks, ny - 1, blk, dout),
           f32(chunks, blk, dout), f32(per, nf - 1, 2, blk, dout)]
        + [f32(chunks, half, 128), f32(chunks, nchip - 1, sblk, 128), f32(DIRECT, nd - 1, sblk, 128), f32(per, nf - 1, sblk, 128)]
        + [dma((9,))]
        + [dma((chunks,))] * 4 + [dma((chunks, ny - 1))] * 4 + [dma((chunks,))] * 2 + [dma((chunks,)), dma((per, nf - 1))]
        + [dma((per, nchip - 1))] * 2 + [dma((per,))] * 2 + [dma((chunks,)), dma((per, nf - 1))]
        + [dma((chunks,))] * 2 + [dma((chunks, nchip - 1))] * 2 + [dma((chunks,)), dma((per, nf - 1))]
        + [dma((per, nchip - 1))] * 2 + [dma((per,))] * 2
        + [dma((DIRECT, nd - 1))] * 4,
        compiler_params=params(collective_id=1, has_side_effects=True),
    )(*ins, sc, *far)


def final(nf, bins, gw, sm, fr):
    per, flocal = sm.shape[0], fr.shape[1]
    members, width = 32, gw.shape[1] // nf
    shapes = [jax.ShapeDtypeStruct(x, F32) for x in (
        (flocal, nf * 128), (flocal, 16, bins), (16, flocal), (16, flocal), (members, per * CHUNK), gw.shape, (members, width), (members, width))]
    ins = (gw, sm, fr)
    anywhere = pl.BlockSpec(memory_space=pl.ANY)
    return pl.pallas_call(functools.partial(final_kernel, nf, bins), out_shape=shapes,
                          in_specs=[anywhere] + [whole(x.shape) for x in ins[1:]],
                          out_specs=[whole(x.shape) for x in shapes],
                          scratch_shapes=[pltpu.SemaphoreType.DMA], compiler_params=params())(*ins)


def shards(nd, nf, bins, fractions, missing, bin_table, bin_bias, miss_vector, scale_in, weight, scale_out, bias_out, cotangent):
    raw, packed, e, sc, *wp = exchange(nd, nf, bins.T, fractions.T, missing.T, jnp.transpose(bin_table, (0, 2, 1)), bin_bias.T,
                                       miss_vector.T, scale_in, scale_out, weight, cotangent)
    hidden, *rest = forward(nf, e, scale_in, wp, scale_out, bias_out, cotangent, sc)
    gw, sm, fr = backward(nd, nf, e, scale_in, rest[6], raw, packed, wp, rest[:3], rest[3:6], sc)
    gw = gw.reshape(-1, weight.shape[1])
    frac, table, bias, miss, sin, gw, so, bo = final(nf, bin_table.shape[1], gw, sm, fr)
    return hidden, frac.T, jnp.transpose(table, (0, 2, 1)), bias.T, miss.T, sin, gw, so, bo


def solution(mesh):
    placed = (P("dp", "feat"), P("dp", "feat"), P("dp", "feat"), P("feat", None, None), P("feat", None), P("feat", None),
              P(), P(), P(), P(), P(("dp", "feat"), None, None))
    return jax.shard_map(
        functools.partial(shards, mesh.shape["dp"], mesh.shape["feat"]),
        mesh=mesh,
        in_specs=placed,
        out_specs=(P(("dp", "feat"), None, None), P("dp", "feat"), P("feat", None, None), P("feat", None), P("feat", None),
                   P(None, "feat"), P("feat", None), P(None, "feat"), P(None, "feat")),
        check_vma=False,
    )
```

```python
import functools

import jax
import jax.numpy as jnp
from jax import lax
from jax.experimental import pallas as pl
from jax.experimental.pallas import tpu as pltpu
from jax.sharding import PartitionSpec as P

F32, BF16, F8 = jnp.float32, jnp.bfloat16, jnp.float8_e4m3fn
VMEM_LIMIT = 63 << 20
TILE = 16
DIRECT = 2
CHUNK = 256
TOP = 224.0
TOP_WEIGHT = 400.0
LO = 256.0
GELU_A = 0.7978845608028654
GELU_B = GELU_A * 0.044715


def dot(a, b):
    return jnp.dot(a, b, preferred_element_type=F32)


def dot_nt(a, b):
    return lax.dot_general(a, b, (((1,), (1,)), ((), ())), preferred_element_type=F32)


def split3(x):
    hi = x.astype(BF16)
    return hi, hi.astype(F8), ((x - hi.astype(F32)).astype(BF16) * BF16(LO)).astype(F8)


def split2(x):
    hi = x.astype(BF16)
    return hi, (x - hi.astype(F32)).astype(BF16)


def split3_weight(x):
    hi = x.astype(BF16)
    return hi, (x * (1.0 / LO)).astype(F8), (x - hi.astype(F32)).astype(F8)


def encode_pair(raw_ref, flocal, first):
    level = lax.broadcasted_iota(jnp.int32, (48, 128), 0).astype(F32)
    row = lax.broadcasted_iota(jnp.int32, (16, 128), 0)
    parts = []
    for f in (first, first + 1):
        b, fr, m = [raw_ref[pl.ds(f + k * flocal, 1), :] for k in range(3)]
        here = 1.0 - m
        parts.append(jnp.clip((b - level) + fr, 0.0, 1.0) * here)
        parts.append(jnp.where(row == 0, here, jnp.where(row == 1, m, 0.0)))
    return jnp.concatenate(parts, axis=0)


def table_pair(t_ref, p):
    blk = t_ref[pl.ds(pl.multiple_of(p * 16, 16), 16), :]
    lane = lax.broadcasted_iota(jnp.int32, (16, 128), 1)
    zero = jnp.zeros_like(blk)
    return jnp.concatenate([jnp.where(lane < 64, blk, zero), jnp.where(lane < 64, zero, blk)], axis=0)


def send(src, dst, ssem, rsem, **where):
    return pltpu.make_async_remote_copy(src_ref=src, dst_ref=dst, send_sem=ssem, recv_sem=rsem, device_id=where,
                                        device_id_type=pl.DeviceIdType.MESH)


def greet(partners):
    barrier = pltpu.get_barrier_semaphore()
    for where in partners:
        pl.semaphore_signal(barrier, inc=1, device_id=where, device_id_type=pl.DeviceIdType.MESH)
    return lambda: pl.semaphore_wait(barrier, len(partners))


def exchange_kernel(nd, nf, bins_ref, fr_ref, ms_ref, tab_ref, bias_ref, miss_ref, s_ref, so_ref, w_in, ct_in,
                    raw_ref, t_ref, e_ref, sc_ref, wh_out, w8_out, wl_out,
                    mine, et, w, ct, wh, w8, wl, load, store, r_s, r_r, x_s, x_r, y_s, y_r, z_s, z_r):
    flocal, total = bins_ref.shape
    count = total // nf
    bins, width = tab_ref.shape[2], tab_ref.shape[1]
    me, z = lax.axis_index("dp"), lax.axis_index("feat")
    nchip = nd // 2
    core, chip = lax.rem(me, 2), me // 2
    partner = me + 1 - 2 * core
    parts = ct.shape[0]
    step = ct_in.shape[0] // parts

    ready = greet([{"feat": lax.rem(z + o, nf)} for o in range(1, nf)]
                  + [{"dp": 2 * lax.rem(chip + o, nchip) + core} for o in range(1, nchip)] + [{"dp": partner}])
    loads = [pltpu.make_async_copy(w_in, w, load.at[0])] + [
        pltpu.make_async_copy(ct_in.at[pl.ds(i * step, step)], ct.at[i], load.at[i + 1]) for i in range(parts)]
    for copy in loads:
        copy.start()

    def rows(q):
        return pl.ds(pl.multiple_of(q * (3 * flocal), 3 * flocal), 3 * flocal)

    size = flocal // 2 * width // nd

    def entries(q, piece, n):
        return t_ref.at[pl.ds(pl.multiple_of(q * (nd * size) + piece * size, 8), n * size)]

    mine[0:flocal, :] = bins_ref[...].astype(F32)
    mine[flocal:2 * flocal, :] = fr_ref[...]
    mine[2 * flocal:, :] = ms_ref[...].astype(F32)
    raw_ref[rows(z), :] = mine[:, pl.ds(pl.multiple_of(z * count, count), count)]
    blank = jnp.zeros((width, 64 - bins - 2), F32)
    for p in range(flocal // 2):
        block = []
        for f in (2 * p, 2 * p + 1):
            block += [tab_ref[f], bias_ref[:, f:f + 1], miss_ref[:, f:f + 1], blank]
        t_ref[pl.ds(pl.multiple_of(z * (flocal // 2 * width) + p * width, width), width), :] = jnp.concatenate(block, axis=1)

    def send_raw(o, q):
        to = lax.rem(z + o, nf)
        return send(mine.at[:, pl.ds(pl.multiple_of(to * count, count), count)], raw_ref.at[rows(q)],
                    r_s.at[o - 1], r_r.at[o - 1], feat=to)

    def send_x(o, q):
        r = entries(q, core * nchip + chip, 1)
        return send(r, r, x_s.at[o - 1], x_r.at[o - 1], feat=lax.rem(z + o, nf))

    def send_y(o, k, c):
        r = entries(lax.rem(z - o + nf, nf), core * nchip + c, 1)
        return send(r, r, y_s.at[o - 1, k - 1], y_r.at[o - 1, k - 1], dp=2 * lax.rem(chip + k, nchip) + core)

    def send_z(o, side):
        r = entries(lax.rem(z - o + nf, nf), side * nchip, nchip)
        return send(r, r, z_s.at[o - 1], z_r.at[o - 1], dp=partner)

    others = range(1, nf)
    ready()
    for o in others:
        send_x(o, z).start()
    for o in others:
        send_raw(o, z).start()

    def top(v):
        return jnp.maximum(jnp.max(jnp.max(jnp.abs(v), axis=0, keepdims=True), axis=1, keepdims=True), 1e-30)

    pairs = flocal // 2
    at_once = min(16, pairs)
    entries_local = flocal * width

    def embed(q):
        def body(j, c):
            for k in range(at_once):
                p = q * pairs + j * at_once + k
                first = q * (3 * flocal) + 2 * (j * at_once + k)
                lh, ll = split2(table_pair(t_ref, p))
                eh, el = split2(encode_pair(raw_ref, flocal, first))
                both = dot(jnp.concatenate([lh, ll], axis=0), eh)
                et[pl.ds(pl.multiple_of(p * 32, 32), 32), :] = both[:32] + both[32:] + dot(lh, el)
            return c

        lax.fori_loop(0, pairs // at_once, body, 0)
        for j in range(entries_local // 128):
            at = pl.ds(pl.multiple_of(q * entries_local + j * 128, 128), 128)
            e_ref[:, at] = et[at, :].T

    embed(z)
    for o in others:
        send_x(o, lax.rem(z - o + nf, nf)).wait_recv()
        for k in range(1, nchip):
            send_y(o, k, chip).start()

    loads[0].wait()
    sw = TOP_WEIGHT / top(w[...])
    for i in range(0, w.shape[0], 256):
        r = slice(i, i + 256)
        wh[r, :], w8[r, :], wl[r, :] = split3_weight(w[r, :] * sw)
    stores = [pltpu.make_async_copy(i, o, store.at[k]) for k, (i, o) in enumerate(((wh, wh_out), (w8, w8_out), (wl, wl_out)))]
    for copy in stores:
        copy.start()

    for o in others:
        for k in range(1, nchip):
            send_y(o, k, lax.rem(chip - k + nchip, nchip)).wait_recv()
        send_z(o, core).start()
    tc = jnp.full((1, 1), 1e-30, F32)
    for i in range(parts):
        loads[i + 1].wait()
        tc = jnp.maximum(tc, top(ct[i].reshape(-1, ct.shape[-1])))
    for o in others:
        q = lax.rem(z - o + nf, nf)
        send_z(o, 1 - core).wait_recv()
        send_raw(o, q).wait_recv()
        embed(q)
    sx = TOP / (top(et[...]) * top(s_ref[...]))
    sg = TOP / (1.2 * tc * top(so_ref[...]))
    for k, v in enumerate((sx, sw, sg, 1.0 / (sx * sw), 1.0 / (sx * sw), 1.0 / (sg * sx), 1.0 / (sg * sw), 1.0 / (sg * sw))):
        sc_ref[k:k + 1, :] = jnp.broadcast_to(v, (1, 128))
    for copy in stores:
        copy.wait()
    for o in others:
        send_raw(o, z).wait_send()
        send_x(o, z).wait_send()
        for k in range(1, nchip):
            send_y(o, k, chip).wait_send()
        send_z(o, core).wait_send()


def forward_kernel(nf, e_ref, s_ref, wh_in, w8_in, wl_in, so_ref, bo_ref, ct_ref, sc_ref,
                   hid_ref, gh_ref, g8_ref, gl_ref, th_ref, t8_ref, tl_ref, z_ref,
                   gs_ref, gb_ref, s1, so1, so2, wh_ref, w8_ref, wl_ref, load, xh0, x80, xl0, xh1, x81, xl1, pre0, pre1):
    i = pl.program_id(0)
    tiles = pl.num_programs(0) - 1
    members, width_out = so_ref.shape
    rows = TILE * members
    x = ((xh0, x80, xl0), (xh1, x81, xl1))
    pre = (pre0, pre1)

    def prepare(tile, to):
        for n in range(TILE):
            v = s1[...] * e_ref[pl.ds(tile * TILE + n, 1), :]
            r = slice(n * members, (n + 1) * members)
            to[0][r, :], to[1][r, :], to[2][r, :] = split3(v)

    def multiply(a, to):
        to[...] = dot(a[0][...], wh_ref[...]) + (dot(a[1][...], wl_ref[...]) + dot(a[2][...], w8_ref[...]))

    def finish(p):
        for h0 in range(0, width_out, 128):
            hs = slice(h0, h0 + 128)
            sa, sb, bo = so1[:, hs], so2[:, hs], bo_ref[:, hs]
            gs, gb = gs_ref[:, hs], gb_ref[:, hs]
            for n in range(TILE):
                r = slice(n * members, (n + 1) * members)
                q = p[r, hs]
                v = q * sa + bo
                v2 = v * v
                half = 0.5 + 0.5 * jnp.tanh(v * (GELU_B * v2 + GELU_A))
                hid = v * half
                hid_ref[n, :, hs] = hid
                g = half + hid * (1.0 - half) * ((6.0 * GELU_B) * v2 + 2.0 * GELU_A)
                ga = ct_ref[n, :, hs] * g
                gs = gs + ga * q
                gb = gb + ga
                gh_ref[r, hs], g8_ref[r, hs], gl_ref[r, hs] = split3(ga * sb)
            gs_ref[:, hs], gb_ref[:, hs] = gs, gb
        th_ref[...] = gh_ref[...].T
        t8_ref[...] = g8_ref[...].T
        tl_ref[...] = gl_ref[...].T

    @pl.when(i == 0)
    def _():
        loads = [pltpu.make_async_copy(a, b, load.at[k]) for k, (a, b) in enumerate(
            ((wh_in, wh_ref), (w8_in, w8_ref), (wl_in, wl_ref)))]
        for copy in loads:
            copy.start()
        s1[...] = s_ref[...] * sc_ref[0:0 + 1, 0:1]
        so1[...] = so_ref[...] * sc_ref[3:3 + 1, 0:1]
        so2[...] = so_ref[...] * sc_ref[2:2 + 1, 0:1]
        gs_ref[...] = jnp.zeros_like(gs_ref)
        gb_ref[...] = jnp.zeros_like(gb_ref)
        prepare(0, x[0])
        for copy in loads:
            copy.wait()
        prepare(1, x[1])
        multiply(x[0], pre[0])

    for par in (0, 1):
        @pl.when((i > 0) & (i < tiles) & (i % 2 == par))
        def _():
            prepare(jnp.minimum(i + 1, tiles - 1), x[1 - par])
            finish(pre[1 - par])
            multiply(x[par], pre[par])

    @pl.when(i == tiles)
    def _():
        finish(pre[1])
        part = width_out // nf
        for o in range(nf):
            z_ref[:, 2 * o * part:(2 * o + 1) * part] = gs_ref[:, o * part:(o + 1) * part] * sc_ref[4:4 + 1, 0:1]
            z_ref[:, (2 * o + 1) * part:(2 * o + 2) * part] = gb_ref[:, o * part:(o + 1) * part]


def backward_kernel(nd, nf, e_ref, s_ref, z_ref, raw_ref, t_ref, sc_ref, wh_in, w8_in, wl_in, gh_in, g8_in, gl_in,
                    th_in, t8_in, tl_in, gw_out, sm_out, fr_out,
                    wh, w8, wl, gh, g8l, th, t8, tl, wcat, s1, s2, xh0, x80, xl0, xh1, x81, xl1, g0, g1, ge, gsin, et,
                    gw, sm, gf, ra, rp, rq, rp2, rq2, rc, ru, rb, r1, r2,
                    load, a_s, a_r, p_s, p_r, q_s, q_r, p2_s, p2_r, q2_s, q2_r, c_s, c_r, d_s, d_r, e_s, e_r, f_s, f_r,
                    ua_s, ua_r, ub_s, ub_r, uc_s, uc_r, ud_s, ud_r, ue_s, ue_r, u_s, u_r, y_s, y_r):
    members, width_in = s_ref.shape
    rows = gh.shape[0]
    count = e_ref.shape[0]
    chunks = width_in // CHUNK
    direct = chunks - DIRECT
    per = chunks // nf
    nx, ny, nchip = 2, nd // 4, nd // 2
    blk, dout = gw.shape[4], gw.shape[5]
    half, sblk = sm.shape[1] // 2, sm.shape[1] // nd
    feats = CHUNK // 16
    flocal = fr_out.shape[1]
    me, z = lax.axis_index("dp"), lax.axis_index("feat")
    core, chip = lax.rem(me, 2), me // 2
    cx, cy = lax.rem(chip, nx), chip // nx
    partner = me + 1 - 2 * core

    ready = greet([{"dp": lax.rem(me + o, nd)} for o in range(1, nd)] + [{"feat": lax.rem(z + o, nf)} for o in range(1, nf)])
    loads = [pltpu.make_async_copy(i, o, load.at[k]) for k, (i, o) in enumerate(
        ((th_in, th), (t8_in, t8), (tl_in, tl), (wh_in, wh), (w8_in, w8), (wl_in, wl), (gh_in, gh), (g8_in, g8l.at[:, :dout]), (gl_in, g8l.at[:, dout:])))]
    for copy in loads[:3]:
        copy.start()

    def aligned(i, n):
        return pl.ds(pl.multiple_of(i, n), n)

    def owner(i):
        return lax.rem(i + nf // 2 + 1, nf)

    def place(i):
        return owner(i) * per + i // nf

    def far(i):
        return lax.rem(owner(i) - z + nf, nf)

    def device(y, x):
        return 2 * (y * nx + x) + core

    def other_y(k):
        return lax.rem(cy + k, ny)

    def from_y(k):
        return lax.rem(cy - k + ny, ny)

    def own(i):
        return 2 * place(i) + core

    def send_a(i):
        return send(gw.at[2 * place(i) + 1 - core], ra.at[i], a_s.at[i], a_r.at[i], dp=partner)

    def send_p(i):
        return send(gw.at[own(i), :, 1 - cx, 0], rp.at[i], p_s.at[i], p_r.at[i], dp=device(cy, 1 - cx))

    def send_q(i, k):
        return send(gw.at[own(i), other_y(k), :, 1], rq.at[i, k - 1], q_s.at[i, k - 1], q_r.at[i, k - 1], dp=device(other_y(k), cx))

    def send_p2(i, k):
        return send(gw.at[own(i), other_y(k), cx, 0], rp2.at[i, k - 1], p2_s.at[i, k - 1], p2_r.at[i, k - 1], dp=device(other_y(k), cx))

    def send_q2(i):
        return send(gw.at[own(i), cy, 1 - cx, 1], rq2.at[i], q2_s.at[i], q2_r.at[i], dp=device(cy, 1 - cx))

    def send_c(i, k):
        j = i // nf
        return send(gw.at[own(i), cy, cx], rc.at[j, k - 1], c_s.at[i], c_r.at[j, k - 1], feat=owner(i))

    def send_d(i, o, q):
        j = i // nf
        return send(gw.at[own(i), cy, cx], gw_out.at[2 * j + core, q // nx, lax.rem(q, nx)], d_s.at[j, o - 1], d_r.at[j, o - 1],
                    dp=2 * lax.rem(chip + o, nchip) + core)

    def send_e(i, side):
        j = i // nf
        return send(gw_out.at[2 * j + side], gw_out.at[2 * j + side], e_s.at[j], e_r.at[j], dp=partner)

    def step_b(i):
        send_a(i).wait_recv()
        gw[own(i)] += ra[i]
        send_p(i).start()
        for k in range(1, ny):
            send_q(i, k).start()

    def step_b2(i):
        send_p(i).wait_recv()
        gw[own(i), :, cx, 0] += rp[i]
        for k in range(1, ny):
            send_q(i, k).wait_recv()
            gw[own(i), cy, :, 1] += rq[i, k - 1]
        for k in range(1, ny):
            send_p2(i, k).start()
        send_q2(i).start()

    def step_c(i):
        send_q2(i).wait_recv()
        gw[own(i), cy, cx, 1] += rq2[i]
        for k in range(1, ny):
            send_p2(i, k).wait_recv()
            gw[own(i), cy, cx, 0] += rp2[i, k - 1]

        @pl.when(owner(i) != z)
        def _():
            send_c(i, far(i)).start()

    def step_d(i):
        @pl.when(owner(i) == z)
        def _():
            total = gw[own(i), cy, cx]
            for k in range(1, nf):
                send_c(i, k).wait_recv()
                total = total + rc[i // nf, k - 1]
            gw[own(i), cy, cx] = total
            gw_out[2 * (i // nf) + core, cy, cx] = total
            for o in range(1, nchip):
                send_d(i, o, chip).start()

    def step_e(i):
        @pl.when(owner(i) == z)
        def _():
            for o in range(1, nchip):
                send_d(i, o, lax.rem(chip - o + nchip, nchip)).wait_recv()
            send_e(i, core).start()

    def step_f(i):
        @pl.when(owner(i) == z)
        def _():
            send_e(i, 1 - core).wait_recv()

    def drain(i):
        send_a(i).wait_send()
        send_p(i).wait_send()
        send_q2(i).wait_send()
        for k in range(1, ny):
            send_q(i, k).wait_send()
            send_p2(i, k).wait_send()

        @pl.when(owner(i) != z)
        def _():
            send_c(i, far(i)).wait_send()

        @pl.when(owner(i) == z)
        def _():
            for o in range(1, nchip):
                send_d(i, o, chip).wait_send()
            send_e(i, core).wait_send()

    def rows_of(q, side):
        return aligned(side * half + q * sblk, sblk)

    def whole_half(side):
        return aligned(side * half, half)

    def send_ua(i):
        return send(sm.at[i, whole_half(1 - core)], ru.at[i], ua_s.at[i], ua_r.at[i], dp=partner)

    def send_ub(i, o):
        to = lax.rem(chip + o, nchip)
        return send(sm.at[i, rows_of(to, core)], rb.at[i, o - 1], ub_s.at[i, o - 1], ub_r.at[i, o - 1], dp=2 * to + core)

    def send_uc(i, k):
        j = i // nf
        return send(sm.at[i, rows_of(chip, core)], r2.at[j, k - 1], uc_s.at[i], uc_r.at[j, k - 1], feat=owner(i))

    def send_ud(i, o, q):
        j = i // nf
        return send(sm.at[i, rows_of(chip, core)], sm_out.at[j, rows_of(q, core)], ud_s.at[j, o - 1], ud_r.at[j, o - 1],
                    dp=2 * lax.rem(chip + o, nchip) + core)

    def send_ue(i, side):
        j = i // nf
        r = sm_out.at[j, whole_half(side)]
        return send(r, r, ue_s.at[j], ue_r.at[j], dp=partner)

    def send_u(i, o):
        to = lax.rem(me + o, nd)
        return send(sm.at[i, rows_of(to // 2, lax.rem(to, 2))], r1.at[i - direct, o - 1], u_s.at[i - direct, o - 1],
                    u_r.at[i - direct, o - 1], dp=to)

    def send_y(i, o, q):
        j = i - direct
        return send(sm.at[i, rows_of(chip, core)], sm_out.at[i // nf, rows_of(q // 2, lax.rem(q, 2))], y_s.at[j, o - 1], y_r.at[j, o - 1],
                    dp=lax.rem(me + o, nd))

    def send_f(i, k, src):
        j = i // nf
        return send(gf.at[i], fr_out.at[src, aligned(j * feats, feats)], f_s.at[i], f_r.at[j, k - 1], feat=owner(i))

    def start_f(i):
        @pl.when(owner(i) != z)
        def _():
            send_f(i, far(i), z).start()

        @pl.when(owner(i) == z)
        def _():
            fr_out[z, aligned((i // nf) * feats, feats), :] = gf[i]

    def wait_f(i):
        @pl.when(owner(i) == z)
        def _():
            for k in range(1, nf):
                send_f(i, k, lax.rem(z - k + nf, nf)).wait_recv()

    def start_ua(i):
        send_ua(i).start()
        start_f(i)

    def step_ub(i):
        send_ua(i).wait_recv()
        sm[i, whole_half(core), :] += ru[i]
        for o in range(1, nchip):
            send_ub(i, o).start()

    def step_uc(i):
        r = rows_of(chip, core)
        total = sm[i, r, :]
        for o in range(1, nchip):
            send_ub(i, o).wait_recv()
            total = total + rb[i, o - 1]
        sm[i, r, :] = total

        @pl.when(owner(i) != z)
        def _():
            send_uc(i, far(i)).start()

    def gather_z(i):
        r = rows_of(chip, core)
        total = sm[i, r, :]
        for k in range(1, nf):
            send_uc(i, k).wait_recv()
            total = total + r2[i // nf, k - 1]
        sm[i, r, :] = total
        sm_out[i // nf, r, :] = total

    def step_ud(i):
        @pl.when(owner(i) == z)
        def _():
            gather_z(i)
            for o in range(1, nchip):
                send_ud(i, o, chip).start()

    def step_ue(i):
        @pl.when(owner(i) == z)
        def _():
            for o in range(1, nchip):
                send_ud(i, o, lax.rem(chip - o + nchip, nchip)).wait_recv()
            send_ue(i, core).start()

    def step_uf(i):
        @pl.when(owner(i) == z)
        def _():
            send_ue(i, 1 - core).wait_recv()

        wait_f(i)

    def drain_small(i):
        send_ua(i).wait_send()
        for o in range(1, nchip):
            send_ub(i, o).wait_send()

        @pl.when(owner(i) != z)
        def _():
            send_uc(i, far(i)).wait_send()
            send_f(i, far(i), z).wait_send()

        @pl.when(owner(i) == z)
        def _():
            for o in range(1, nchip):
                send_ud(i, o, chip).wait_send()
            send_ue(i, core).wait_send()

    def start_u(i):
        for o in range(1, nd):
            send_u(i, o).start()

    def step_v(i):
        r = rows_of(chip, core)
        total = sm[i, r, :]
        for o in range(1, nd):
            send_u(i, o).wait_recv()
            total = total + r1[i - direct, o - 1]
        sm[i, r, :] = total

        @pl.when(owner(i) != z)
        def _():
            send_uc(i, far(i)).start()

    def step_y(i):
        @pl.when(owner(i) == z)
        def _():
            gather_z(i)
            for o in range(1, nd):
                send_y(i, o, me).start()

    def step_w(i):
        @pl.when(owner(i) == z)
        def _():
            for o in range(1, nd):
                send_y(i, o, lax.rem(me - o + nd, nd)).wait_recv()

        wait_f(i)

    def drain_direct(i):
        for o in range(1, nd):
            send_u(i, o).wait_send()

        @pl.when(owner(i) != z)
        def _():
            send_uc(i, far(i)).wait_send()
            send_f(i, far(i), z).wait_send()

        @pl.when(owner(i) == z)
        def _():
            for o in range(1, nd):
                send_y(i, o, me).wait_send()

    def when_chunk(i, f, first=0, end=chunks):
        @pl.when((i >= first) & (i < end))
        def _():
            f(i)

    start_a = lambda i: send_a(i).start()
    stages = ((start_a, (0, 1, 2, 3)), (step_b, (1, 2, 3, 4)), (step_b2, (3, 4, 5, 6)), (step_c, (5, 6, 7, 8)),
              (step_d, (7, 8, 9, 10)), (step_e, (9, 10, 11)))

    def pairs(k, among):
        for step, times in stages:
            for j, at in enumerate(times):
                if at in among:
                    @pl.when(k == at)
                    def _():
                        for i in (2 * j, 2 * j + 1):
                            step(i)

    def early(j):
        @pl.when(j == 0)
        def _():
            ready()

        pairs(j, range(4))

    def late(t):
        when_chunk(t - 1, start_ua, 0, direct)
        when_chunk(t - 1, start_u, direct)
        when_chunk(t - 1, start_f, direct)
        pairs(t + 4, range(4, 12))
        when_chunk(t - 2, step_ub, 0, direct)
        when_chunk(t - 4, step_uc, 0, direct)
        when_chunk(t - 6, step_ud, 0, direct)

    x = ((xh0, x80, xl0), (xh1, x81, xl1))
    s1[...] = s_ref[...] * sc_ref[0:0 + 1, 0:1]
    s2[...] = s_ref[...] * sc_ref[6:6 + 1, 0:1]

    def cols(i):
        return aligned(place(i) * CHUNK, CHUNK)

    def prepare(i, to):
        for n in range(0, count, TILE):
            v = (e_ref[n:n + TILE, cols(i)][:, None, :] * s1[:, cols(i)][None]).reshape(TILE * members, CHUNK)
            r = slice(n * members, (n + TILE) * members)
            to[0][r, :], to[1][r, :], to[2][r, :] = split3(v)

    prepare(0, x[0])
    for copy in loads[:3]:
        copy.wait()
    for copy in loads[3:]:
        copy.start()

    def weights(j, carry):
        for par in (0, 1):
            i = 2 * j + par
            xh, x8, xl = x[par]
            r = dot(th[...], xh[...]) + (dot(t8[...], xl[...]) + dot(tl[...], x8[...])) * (1.0 / LO)
            gw[aligned(2 * place(i), 2)] = (r.T * sc_ref[5:5 + 1, 0:1]).reshape(2, ny, nx, 2, blk, dout)
            prepare(jnp.minimum(i + 1, chunks - 1), x[1 - par])
        early(j)
        return carry

    lax.fori_loop(0, chunks // 2, weights, 0)

    for copy in loads[3:]:
        copy.wait()
    gsin[...] = jnp.zeros_like(gsin)
    g1[...] = jnp.zeros_like(g1)
    step = g0.shape[0]
    objs = step // members
    parts = rows // step

    def finish(i, t, g):
        g3 = g[...].reshape(objs, members, CHUNK)
        ns = slice(t * objs, (t + 1) * objs)
        ge[ns, :] = jnp.sum(g3 * s2[:, cols(i)][None], axis=1)
        gsin[...] += jnp.sum(g3 * e_ref[ns, cols(i)][:, None, :], axis=0)

    def table(i):
        c = place(i)
        first = c * feats
        base = (first // flocal) * (3 * flocal) + lax.rem(first, flocal)
        for j in range(CHUNK // 128):
            et[j * 128:(j + 1) * 128, :] = ge[:, j * 128:(j + 1) * 128].T
        lane = lax.broadcasted_iota(jnp.int32, (16, 128), 1)
        for p in range(feats // 2):
            row = base + 2 * p
            enc = encode_pair(raw_ref, flocal, row)
            gh_, gl_ = split2(et[p * 32:(p + 1) * 32, :])
            eh, el = split2(enc)
            both = dot_nt(jnp.concatenate([gh_, gl_], axis=0), eh)
            full = both[:32] + both[32:] + dot_nt(gh_, el)
            sm[i, p * 16:(p + 1) * 16, :] = jnp.where(lane < 64, full[:16], full[16:])
        at = feats * 8
        for j in range(CHUNK // 128):
            sm[i, at:at + members, :] = gsin[:, j * 128:(j + 1) * 128] * sc_ref[7:7 + 1, 0:1]
            at += members
        sm[i, at:at + members, :] = z_ref[:, aligned(c * 128, 128)]
        at += members
        sm[i, at:, :] = jnp.zeros_like(sm[i, at:, :])
        gsin[...] = jnp.zeros_like(gsin)

    def slopes(i):
        c = place(i)
        first = c * feats
        base = (first // flocal) * (3 * flocal) + lax.rem(first, flocal)
        level = lax.broadcasted_iota(jnp.int32, (64, 128), 0).astype(F32)
        for p in range(feats // 2):
            row = base + 2 * p
            lh, ll = split2(table_pair(t_ref, c * (feats // 2) + p))
            g = et[p * 32:(p + 1) * 32, :]
            hot = []
            for f in (row, row + 1):
                here = 1.0 - raw_ref[pl.ds(f + 2 * flocal, 1), :]
                hot.append(jnp.where(level == raw_ref[pl.ds(f, 1), :], here, 0.0))
            one = jnp.concatenate(hot, axis=0).astype(BF16)
            both = dot(jnp.concatenate([lh, ll], axis=0), one)
            picked = (both[:32] + both[32:]) * g
            gf[i, 2 * p:2 * p + 1, :] = jnp.sum(picked[:16], axis=0, keepdims=True)
            gf[i, 2 * p + 1:2 * p + 2, :] = jnp.sum(picked[16:], axis=0, keepdims=True)

    def inputs(i, carry):
        before = jnp.maximum(i - 1, 0)
        wc = wh[cols(i), :]
        wcat[:, :dout] = wl[cols(i), :]
        wcat[:, dout:] = w8[cols(i), :]
        finish(before, parts - 1, g1)
        table(before)
        slopes(before)
        for t in range(parts):
            to, fro = (g0, g1) if t % 2 == 0 else (g1, g0)
            rs = slice(t * step, (t + 1) * step)
            to[...] = dot_nt(gh[rs, :], wc) + dot_nt(g8l[rs, :], wcat[...])
            if t > 0:
                finish(i, t - 1, fro)
        late(i)
        return carry

    lax.fori_loop(0, chunks, inputs, 0)
    last = chunks - 1
    finish(last, parts - 1, g1)
    table(last)
    start_u(last)
    slopes(last)
    start_f(last)
    step_e(last - 1)
    step_e(last)
    step_v(last - 1)
    for i in range(direct - 2, direct):
        step_uc(i)
    for i in range(direct - 4, direct - 2):
        step_ud(i)
    for i in range(direct - 4):
        step_ue(i)
    step_v(last)
    step_y(last - 1)
    for i in range(direct - 2, direct):
        step_ud(i)
    for i in range(direct - 4, direct - 2):
        step_ue(i)
    step_y(last)
    for i in range(direct - 2, direct):
        step_ue(i)
    for i in range(chunks):
        step_f(i)
    for i in range(direct):
        step_uf(i)
    step_w(last - 1)

    def close(i, carry):
        drain(i)
        when_chunk(i, drain_small, 0, direct)
        when_chunk(i, drain_direct, direct)
        return carry

    lax.fori_loop(0, chunks, close, 0)
    step_w(last)


def final_kernel(nf, bins, gw_in, sm_ref, fr_ref, frac_ref, tab_ref, bias_ref, miss_ref, sin_ref, gw_out, so_ref, bo_ref):
    gw_out[...] = gw_in[...]
    flocal = fr_ref.shape[1]
    for o in range(nf):
        frac_ref[:, o * 128:(o + 1) * 128] = fr_ref[o]
    members = sin_ref.shape[0]
    feats = CHUNK // 16
    width = so_ref.shape[1]
    small = []
    for j in range(sm_ref.shape[0]):
        for p in range(feats // 2):
            block = sm_ref[j, p * 16:(p + 1) * 16, :]
            for odd in (0, 1):
                f = j * feats + 2 * p + odd
                tab_ref[f] = block[:, odd * 64:odd * 64 + bins]
                bias_ref[:, f:f + 1] = block[:, odd * 64 + bins:odd * 64 + bins + 1]
                miss_ref[:, f:f + 1] = block[:, odd * 64 + bins + 1:odd * 64 + bins + 2]
        at = feats * 8
        for q in range(CHUNK // 128):
            sin_ref[:, j * CHUNK + q * 128:j * CHUNK + (q + 1) * 128] = sm_ref[j, at:at + members, :]
            at += members
        small.append(sm_ref[j, at:at + members, :])
    small = small[0] if len(small) == 1 else jnp.concatenate(small, axis=1)
    so_ref[...] = small[:, :width]
    bo_ref[...] = small[:, width:]


def params(**kw):
    return pltpu.CompilerParams(vmem_limit_bytes=VMEM_LIMIT, **kw)


def whole(shape):
    return pl.BlockSpec(shape, lambda *_: (0,) * len(shape))


def exchange(nd, nf, bins, fr, ms, tab, bias, miss, s, so, w, ct):
    flocal, total = bins.shape
    width = tab.shape[1]
    count, (din, dout) = total // nf, w.shape
    parts = 8
    ins = (bins, fr, ms, tab, bias, miss, s, so)
    shapes = [jax.ShapeDtypeStruct(x, F32) for x in ((nf * 3 * flocal, count), (nf * flocal // 2 * width, 128), (count, din), (8, 128))]
    far = [jax.ShapeDtypeStruct(w.shape, d) for d in (BF16, F8, F8)]
    dma = pltpu.SemaphoreType.DMA
    anywhere = pl.BlockSpec(memory_space=pl.ANY)
    return pl.pallas_call(
        functools.partial(exchange_kernel, nd, nf),
        out_shape=shapes + far,
        in_specs=[whole(x.shape) for x in ins] + [anywhere] * 2,
        out_specs=[whole(x.shape) for x in shapes] + [anywhere] * 3,
        scratch_shapes=[pltpu.VMEM((3 * flocal, total), F32), pltpu.VMEM((din, count), F32), pltpu.VMEM(w.shape, F32),
                        pltpu.VMEM((parts, ct.shape[0] // parts) + ct.shape[1:], F32)]
        + [pltpu.VMEM(x.shape, x.dtype) for x in far]
        + [dma((parts + 1,)), dma((3,))] + [dma((nf - 1,))] * 4 + [dma((nf - 1, nd // 2 - 1))] * 2 + [dma((nf - 1,))] * 2,
        compiler_params=params(collective_id=0, has_side_effects=True),
    )(*ins, w, ct)


def forward(nf, e, s, wp, so, bo, ct, sc):
    count, din = e.shape
    members, dout = so.shape
    rows, tiles, block = count * members, count // TILE, TILE * members
    lag = lambda i: jnp.maximum(i - 1, 0)
    big = pl.BlockSpec((TILE, members, dout), lambda i: (lag(i), 0, 0))
    nat = pl.BlockSpec((block, dout), lambda i: (lag(i), 0))
    tra = pl.BlockSpec((dout, block), lambda i: (0, lag(i)))
    return pl.pallas_call(
        functools.partial(forward_kernel, nf),
        out_shape=[jax.ShapeDtypeStruct((count, members, dout), F32)]
        + [jax.ShapeDtypeStruct((rows, dout), d) for d in (BF16, F8, F8)]
        + [jax.ShapeDtypeStruct((dout, rows), d) for d in (BF16, F8, F8)]
        + [jax.ShapeDtypeStruct((members, 2 * dout), F32)],
        grid=(tiles + 1,),
        in_specs=[whole(e.shape), whole(s.shape)] + [pl.BlockSpec(memory_space=pl.ANY)] * 3 + [whole(so.shape), whole(bo.shape), big, whole(sc.shape)],
        out_specs=[big, nat, nat, nat, tra, tra, tra, whole((members, 2 * dout))],
        scratch_shapes=[pltpu.VMEM(so.shape, F32)] * 2 + [pltpu.VMEM(s.shape, F32), pltpu.VMEM(so.shape, F32), pltpu.VMEM(so.shape, F32)]
        + [pltpu.VMEM(w.shape, w.dtype) for w in wp] + [pltpu.SemaphoreType.DMA((3,))]
        + [pltpu.VMEM((block, din), d) for d in (BF16, F8, F8)] * 2
        + [pltpu.VMEM((block, dout), F32)] * 2,
        compiler_params=params(),
    )(e, s, *wp, so, bo, ct, sc)


def backward(nd, nf, e, s, zs, raw, t, wp, gp, gt, sc):
    count, din = e.shape
    members = s.shape[0]
    rows, dout = gp[0].shape
    step = rows // 16
    chunks, nchip = din // CHUNK, nd // 2
    per = chunks // nf
    ny, blk, half, sblk = nd // 4, CHUNK // nd // 2, 256 // 2, 256 // nd
    feats, flocal = CHUNK // 16, raw.shape[0] // (3 * nf)
    layout = (ny, 2, 2, blk, dout)
    shapes = [jax.ShapeDtypeStruct(x, F32) for x in ((2 * per,) + layout, (per, 256, 128), (nf, flocal, 128))]
    ins = (e, s, zs, raw, t)
    far = (*wp, *gp, *gt)
    dma = pltpu.SemaphoreType.DMA
    f32 = lambda *shape: pltpu.VMEM(shape, F32)
    return pl.pallas_call(
        functools.partial(backward_kernel, nd, nf),
        out_shape=shapes,
        in_specs=[whole(x.shape) for x in ins] + [whole(sc.shape)] + [pl.BlockSpec(memory_space=pl.ANY)] * len(far),
        out_specs=[whole(x.shape) for x in shapes],
        scratch_shapes=[pltpu.VMEM(x.shape, x.dtype) for x in (*wp, gp[0])] + [pltpu.VMEM((rows, 2 * dout), F8)]
        + [pltpu.VMEM(x.shape, x.dtype) for x in gt] + [pltpu.VMEM((CHUNK, 2 * dout), F8)]
        + [f32(*s.shape)] * 2
        + [pltpu.VMEM((rows, CHUNK), d) for d in (BF16, F8, F8)] * 2
        + [f32(step, CHUNK)] * 2
        + [f32(count, CHUNK), f32(members, CHUNK), f32(CHUNK, count)]
        + [f32(2 * chunks, *layout), f32(chunks, 256, 128), f32(chunks, feats, count)]
        + [f32(chunks, *layout), f32(chunks, ny, blk, dout), f32(chunks, ny - 1, 2, blk, dout), f32(chunks, ny - 1, blk, dout),
           f32(chunks, blk, dout), f32(per, nf - 1, 2, blk, dout)]
        + [f32(chunks, half, 128), f32(chunks, nchip - 1, sblk, 128), f32(DIRECT, nd - 1, sblk, 128), f32(per, nf - 1, sblk, 128)]
        + [dma((9,))]
        + [dma((chunks,))] * 4 + [dma((chunks, ny - 1))] * 4 + [dma((chunks,))] * 2 + [dma((chunks,)), dma((per, nf - 1))]
        + [dma((per, nchip - 1))] * 2 + [dma((per,))] * 2 + [dma((chunks,)), dma((per, nf - 1))]
        + [dma((chunks,))] * 2 + [dma((chunks, nchip - 1))] * 2 + [dma((chunks,)), dma((per, nf - 1))]
        + [dma((per, nchip - 1))] * 2 + [dma((per,))] * 2
        + [dma((DIRECT, nd - 1))] * 4,
        compiler_params=params(collective_id=1, has_side_effects=True),
    )(*ins, sc, *far)


def final(nf, bins, gw, sm, fr):
    per, flocal = sm.shape[0], fr.shape[1]
    members, width = 32, gw.shape[1] // nf
    shapes = [jax.ShapeDtypeStruct(x, F32) for x in (
        (flocal, nf * 128), (flocal, 16, bins), (16, flocal), (16, flocal), (members, per * CHUNK), gw.shape, (members, width), (members, width))]
    ins = (gw, sm, fr)
    return pl.pallas_call(functools.partial(final_kernel, nf, bins), out_shape=shapes,
                          in_specs=[whole(x.shape) for x in ins], out_specs=[whole(x.shape) for x in shapes],
                          compiler_params=params())(*ins)


def shards(nd, nf, bins, fractions, missing, bin_table, bin_bias, miss_vector, scale_in, weight, scale_out, bias_out, cotangent):
    raw, packed, e, sc, *wp = exchange(nd, nf, bins.T, fractions.T, missing.T, jnp.transpose(bin_table, (0, 2, 1)), bin_bias.T,
                                       miss_vector.T, scale_in, scale_out, weight, cotangent)
    hidden, *rest = forward(nf, e, scale_in, wp, scale_out, bias_out, cotangent, sc)
    gw, sm, fr = backward(nd, nf, e, scale_in, rest[6], raw, packed, wp, rest[:3], rest[3:6], sc)
    gw = gw.reshape(-1, weight.shape[1])
    frac, table, bias, miss, sin, gw, so, bo = final(nf, bin_table.shape[1], gw, sm, fr)
    return hidden, frac.T, jnp.transpose(table, (0, 2, 1)), bias.T, miss.T, sin, gw, so, bo


def solution(mesh):
    placed = (P("dp", "feat"), P("dp", "feat"), P("dp", "feat"), P("feat", None, None), P("feat", None), P("feat", None),
              P(), P(), P(), P(), P(("dp", "feat"), None, None))
    return jax.shard_map(
        functools.partial(shards, mesh.shape["dp"], mesh.shape["feat"]),
        mesh=mesh,
        in_specs=placed,
        out_specs=(P(("dp", "feat"), None, None), P("dp", "feat"), P("feat", None, None), P("feat", None), P("feat", None),
                   P(None, "feat"), P("feat", None), P(None, "feat"), P(None, "feat")),
        check_vma=False,
    )
```

```python
import functools

import jax
import jax.numpy as jnp
from jax import lax
from jax.experimental import pallas as pl
from jax.experimental.pallas import tpu as pltpu
from jax.sharding import PartitionSpec as P

F32, BF16, F8 = jnp.float32, jnp.bfloat16, jnp.float8_e4m3fn
VMEM_LIMIT = 63 << 20
TILE = 16
DIRECT = 2
CHUNK = 256
TOP = 224.0
TOP_WEIGHT = 400.0
LO = 256.0
GELU_A = 0.7978845608028654
GELU_B = GELU_A * 0.044715


def dot(a, b):
    return jnp.dot(a, b, preferred_element_type=F32)


def dot_nt(a, b):
    return lax.dot_general(a, b, (((1,), (1,)), ((), ())), preferred_element_type=F32)


def split3(x):
    hi = x.astype(BF16)
    return hi, hi.astype(F8), ((x - hi.astype(F32)).astype(BF16) * BF16(LO)).astype(F8)


def split2(x):
    hi = x.astype(BF16)
    return hi, (x - hi.astype(F32)).astype(BF16)


def split3_weight(x):
    hi = x.astype(BF16)
    return hi, (x * (1.0 / LO)).astype(F8), (x - hi.astype(F32)).astype(F8)


def encode_pair(raw_ref, flocal, first):
    level = lax.broadcasted_iota(jnp.int32, (48, 128), 0).astype(F32)
    row = lax.broadcasted_iota(jnp.int32, (16, 128), 0)
    high, low = [], []
    for f in (first, first + 1):
        b, fr, m = [raw_ref[pl.ds(f + k * flocal, 1), :] for k in range(3)]
        here = 1.0 - m
        rest = (fr - fr.astype(BF16).astype(F32)) * here
        high.append(jnp.clip((b - level) + fr, 0.0, 1.0) * here)
        high.append(jnp.where(row == 0, here, jnp.where(row == 1, m, 0.0)))
        low.append(jnp.where(level == b, rest, 0.0))
        low.append(jnp.zeros((16, 128), F32))
    return jnp.concatenate(high, axis=0).astype(BF16), jnp.concatenate(low, axis=0).astype(BF16)


def table_pair(t_ref, p):
    blk = t_ref[pl.ds(pl.multiple_of(p * 16, 16), 16), :]
    lane = lax.broadcasted_iota(jnp.int32, (16, 128), 1)
    zero = jnp.zeros_like(blk)
    return jnp.concatenate([jnp.where(lane < 64, blk, zero), jnp.where(lane < 64, zero, blk)], axis=0)


def send(src, dst, ssem, rsem, **where):
    return pltpu.make_async_remote_copy(src_ref=src, dst_ref=dst, send_sem=ssem, recv_sem=rsem, device_id=where,
                                        device_id_type=pl.DeviceIdType.MESH)


def greet(partners):
    barrier = pltpu.get_barrier_semaphore()
    for where in partners:
        pl.semaphore_signal(barrier, inc=1, device_id=where, device_id_type=pl.DeviceIdType.MESH)
    return lambda: pl.semaphore_wait(barrier, len(partners))


def exchange_kernel(nd, nf, bins_ref, fr_ref, ms_ref, tab_ref, bias_ref, miss_ref, s_ref, so_ref, w_in, ct_in,
                    raw_ref, t_ref, e_ref, sc_ref, wh_out, w8_out, wl_out,
                    mine, et, w, ct, wh, w8, wl, load, store, r_s, r_r, x_s, x_r, y_s, y_r, z_s, z_r):
    flocal, total = bins_ref.shape
    count = total // nf
    bins, width = tab_ref.shape[2], tab_ref.shape[1]
    me, z = lax.axis_index("dp"), lax.axis_index("feat")
    nchip = nd // 2
    core, chip = lax.rem(me, 2), me // 2
    partner = me + 1 - 2 * core
    parts = ct.shape[0]
    step = ct_in.shape[0] // parts

    ready = greet([{"feat": lax.rem(z + o, nf)} for o in range(1, nf)]
                  + [{"dp": 2 * lax.rem(chip + o, nchip) + core} for o in range(1, nchip)] + [{"dp": partner}])
    loads = [pltpu.make_async_copy(w_in, w, load.at[0])] + [
        pltpu.make_async_copy(ct_in.at[pl.ds(i * step, step)], ct.at[i], load.at[i + 1]) for i in range(parts)]
    for copy in loads:
        copy.start()

    def rows(q):
        return pl.ds(pl.multiple_of(q * (3 * flocal), 3 * flocal), 3 * flocal)

    size = flocal // 2 * width // nd

    def entries(q, piece, n):
        return t_ref.at[pl.ds(pl.multiple_of(q * (nd * size) + piece * size, 8), n * size)]

    mine[0:flocal, :] = bins_ref[...].astype(F32)
    mine[flocal:2 * flocal, :] = fr_ref[...]
    mine[2 * flocal:, :] = ms_ref[...].astype(F32)
    raw_ref[rows(z), :] = mine[:, pl.ds(pl.multiple_of(z * count, count), count)]
    blank = jnp.zeros((width, 64 - bins - 2), F32)
    for p in range(flocal // 2):
        block = []
        for f in (2 * p, 2 * p + 1):
            block += [tab_ref[f], bias_ref[:, f:f + 1], miss_ref[:, f:f + 1], blank]
        t_ref[pl.ds(pl.multiple_of(z * (flocal // 2 * width) + p * width, width), width), :] = jnp.concatenate(block, axis=1)

    def send_raw(o, q):
        to = lax.rem(z + o, nf)
        return send(mine.at[:, pl.ds(pl.multiple_of(to * count, count), count)], raw_ref.at[rows(q)],
                    r_s.at[o - 1], r_r.at[o - 1], feat=to)

    def send_x(o, q):
        r = entries(q, core * nchip + chip, 1)
        return send(r, r, x_s.at[o - 1], x_r.at[o - 1], feat=lax.rem(z + o, nf))

    def send_y(o, k, c):
        r = entries(lax.rem(z - o + nf, nf), core * nchip + c, 1)
        return send(r, r, y_s.at[o - 1, k - 1], y_r.at[o - 1, k - 1], dp=2 * lax.rem(chip + k, nchip) + core)

    def send_z(o, side):
        r = entries(lax.rem(z - o + nf, nf), side * nchip, nchip)
        return send(r, r, z_s.at[o - 1], z_r.at[o - 1], dp=partner)

    others = range(1, nf)
    ready()
    for o in others:
        send_x(o, z).start()
    for o in others:
        send_raw(o, z).start()

    def top(v):
        return jnp.maximum(jnp.max(jnp.max(jnp.abs(v), axis=0, keepdims=True), axis=1, keepdims=True), 1e-30)

    pairs = flocal // 2
    at_once = min(16, pairs)
    entries_local = flocal * width

    def embed(q):
        def body(j, c):
            for k in range(at_once):
                p = q * pairs + j * at_once + k
                first = q * (3 * flocal) + 2 * (j * at_once + k)
                lh, ll = split2(table_pair(t_ref, p))
                eh, el = encode_pair(raw_ref, flocal, first)
                both = dot(jnp.concatenate([lh, ll], axis=0), eh)
                et[pl.ds(pl.multiple_of(p * 32, 32), 32), :] = both[:32] + both[32:] + dot(lh, el)
            return c

        lax.fori_loop(0, pairs // at_once, body, 0)
        for j in range(entries_local // 128):
            at = pl.ds(pl.multiple_of(q * entries_local + j * 128, 128), 128)
            e_ref[:, at] = et[at, :].T

    embed(z)
    for o in others:
        send_x(o, lax.rem(z - o + nf, nf)).wait_recv()
        for k in range(1, nchip):
            send_y(o, k, chip).start()

    loads[0].wait()
    sw = TOP_WEIGHT / top(w[...])
    for i in range(0, w.shape[0], 256):
        r = slice(i, i + 256)
        wh[r, :], w8[r, :], wl[r, :] = split3_weight(w[r, :] * sw)
    stores = [pltpu.make_async_copy(i, o, store.at[k]) for k, (i, o) in enumerate(((wh, wh_out), (w8, w8_out), (wl, wl_out)))]
    for copy in stores:
        copy.start()

    for o in others:
        for k in range(1, nchip):
            send_y(o, k, lax.rem(chip - k + nchip, nchip)).wait_recv()
        send_z(o, core).start()
    tc = jnp.full((1, 1), 1e-30, F32)
    for i in range(parts):
        loads[i + 1].wait()
        tc = jnp.maximum(tc, top(ct[i].reshape(-1, ct.shape[-1])))
    for o in others:
        q = lax.rem(z - o + nf, nf)
        send_z(o, 1 - core).wait_recv()
        send_raw(o, q).wait_recv()
        embed(q)
    sx = TOP / (top(et[...]) * top(s_ref[...]))
    sg = TOP / (1.2 * tc * top(so_ref[...]))
    for k, v in enumerate((sx, sw, sg, 1.0 / (sx * sw), 1.0 / (sx * sw), 1.0 / (sg * sx), 1.0 / (sg * sw), 1.0 / (sg * sw))):
        sc_ref[k:k + 1, :] = jnp.broadcast_to(v, (1, 128))
    for copy in stores:
        copy.wait()
    for o in others:
        send_raw(o, z).wait_send()
        send_x(o, z).wait_send()
        for k in range(1, nchip):
            send_y(o, k, chip).wait_send()
        send_z(o, core).wait_send()


def forward_kernel(nf, e0_ref, e_ref, s_ref, wh_in, w8_in, wl_in, so_ref, bo_ref, ct_ref, sc_ref,
                   hid_ref, gh_ref, g8_ref, gl_ref, th_ref, t8_ref, tl_ref, z_ref,
                   gs_ref, gb_ref, s1, so1, so2, wh_ref, w8_ref, wl_ref, load, xh0, x80, xl0, xh1, x81, xl1, pre0, pre1):
    i = pl.program_id(0)
    tiles = pl.num_programs(0) - 1
    members, width_out = so_ref.shape
    rows = TILE * members
    x = ((xh0, x80, xl0), (xh1, x81, xl1))
    pre = (pre0, pre1)

    def prepare(e, to):
        for n in range(TILE):
            v = s1[...] * e[n:n + 1, :]
            r = slice(n * members, (n + 1) * members)
            to[0][r, :], to[1][r, :], to[2][r, :] = split3(v)

    def multiply(a, to):
        to[...] = dot(a[0][...], wh_ref[...]) + (dot(a[1][...], wl_ref[...]) + dot(a[2][...], w8_ref[...]))

    def finish(p):
        for h0 in range(0, width_out, 128):
            hs = slice(h0, h0 + 128)
            sa, sb, bo = so1[:, hs], so2[:, hs], bo_ref[:, hs]
            gs, gb = gs_ref[:, hs], gb_ref[:, hs]
            for n in range(TILE):
                r = slice(n * members, (n + 1) * members)
                q = p[r, hs]
                v = q * sa + bo
                v2 = v * v
                half = 0.5 + 0.5 * jnp.tanh(v * (GELU_B * v2 + GELU_A))
                hid = v * half
                hid_ref[n, :, hs] = hid
                g = half + hid * (1.0 - half) * ((6.0 * GELU_B) * v2 + 2.0 * GELU_A)
                ga = ct_ref[n, :, hs] * g
                gs = gs + ga * q
                gb = gb + ga
                gh_ref[r, hs], g8_ref[r, hs], gl_ref[r, hs] = split3(ga * sb)
            gs_ref[:, hs], gb_ref[:, hs] = gs, gb
        th_ref[...] = gh_ref[...].T
        t8_ref[...] = g8_ref[...].T
        tl_ref[...] = gl_ref[...].T

    @pl.when(i == 0)
    def _():
        loads = [pltpu.make_async_copy(a, b, load.at[k]) for k, (a, b) in enumerate(
            ((wh_in, wh_ref), (w8_in, w8_ref), (wl_in, wl_ref)))]
        for copy in loads:
            copy.start()
        s1[...] = s_ref[...] * sc_ref[0:0 + 1, 0:1]
        so1[...] = so_ref[...] * sc_ref[3:3 + 1, 0:1]
        so2[...] = so_ref[...] * sc_ref[2:2 + 1, 0:1]
        gs_ref[...] = jnp.zeros_like(gs_ref)
        gb_ref[...] = jnp.zeros_like(gb_ref)
        prepare(e0_ref, x[0])
        for copy in loads:
            copy.wait()
        prepare(e_ref, x[1])
        multiply(x[0], pre[0])

    for par in (0, 1):
        @pl.when((i > 0) & (i < tiles) & (i % 2 == par))
        def _():
            prepare(e_ref, x[1 - par])
            finish(pre[1 - par])
            multiply(x[par], pre[par])

    @pl.when(i == tiles)
    def _():
        finish(pre[1])
        part = width_out // nf
        for o in range(nf):
            z_ref[:, 2 * o * part:(2 * o + 1) * part] = gs_ref[:, o * part:(o + 1) * part] * sc_ref[4:4 + 1, 0:1]
            z_ref[:, (2 * o + 1) * part:(2 * o + 2) * part] = gb_ref[:, o * part:(o + 1) * part]


def backward_kernel(nd, nf, e_ref, s_ref, sc_ref, z_in, raw_in, t_in, wh_in, w8_in, wl_in, gh_in, g8_in, gl_in,
                    th_in, t8_in, tl_in, gw_out, sm_out, fr_out,
                    z_ref, raw_ref, t_ref, wh, w8, wl, gh, g8l, th, t8, tl, wcat, s1, s2, xh0, x80, xl0, xh1, x81, xl1, g0, g1, ge, gsin, et,
                    gw, sm, gf, ra, rp, rq, rp2, rq2, rc, ru, rb, r1, r2,
                    load, a_s, a_r, p_s, p_r, q_s, q_r, p2_s, p2_r, q2_s, q2_r, c_s, c_r, d_s, d_r, e_s, e_r, f_s, f_r,
                    ua_s, ua_r, ub_s, ub_r, uc_s, uc_r, ud_s, ud_r, ue_s, ue_r, u_s, u_r, y_s, y_r):
    members, width_in = s_ref.shape
    rows = gh.shape[0]
    count = e_ref.shape[0]
    chunks = width_in // CHUNK
    direct = chunks - DIRECT
    per = chunks // nf
    nx, ny, nchip = 2, nd // 4, nd // 2
    blk, dout = gw.shape[4], gw.shape[5]
    half, sblk = sm.shape[1] // 2, sm.shape[1] // nd
    feats = CHUNK // 16
    flocal = fr_out.shape[1]
    me, z = lax.axis_index("dp"), lax.axis_index("feat")
    core, chip = lax.rem(me, 2), me // 2
    cx, cy = lax.rem(chip, nx), chip // nx
    partner = me + 1 - 2 * core

    ready = greet([{"dp": lax.rem(me + o, nd)} for o in range(1, nd)] + [{"feat": lax.rem(z + o, nf)} for o in range(1, nf)])
    loads = [pltpu.make_async_copy(i, o, load.at[k]) for k, (i, o) in enumerate(
        ((th_in, th), (t8_in, t8), (tl_in, tl), (wh_in, wh), (w8_in, w8), (wl_in, wl), (gh_in, gh), (g8_in, g8l.at[:, :dout]), (gl_in, g8l.at[:, dout:]),
         (z_in, z_ref), (raw_in, raw_ref), (t_in, t_ref)))]
    for copy in loads[:3]:
        copy.start()

    def aligned(i, n):
        return pl.ds(pl.multiple_of(i, n), n)

    def owner(i):
        return lax.rem(i + nf // 2 + 1, nf)

    def place(i):
        return owner(i) * per + i // nf

    def far(i):
        return lax.rem(owner(i) - z + nf, nf)

    def device(y, x):
        return 2 * (y * nx + x) + core

    def other_y(k):
        return lax.rem(cy + k, ny)

    def from_y(k):
        return lax.rem(cy - k + ny, ny)

    def own(i):
        return 2 * place(i) + core

    def send_a(i):
        return send(gw.at[2 * place(i) + 1 - core], ra.at[i], a_s.at[i], a_r.at[i], dp=partner)

    def send_p(i):
        return send(gw.at[own(i), :, 1 - cx, 0], rp.at[i], p_s.at[i], p_r.at[i], dp=device(cy, 1 - cx))

    def send_q(i, k):
        return send(gw.at[own(i), other_y(k), :, 1], rq.at[i, k - 1], q_s.at[i, k - 1], q_r.at[i, k - 1], dp=device(other_y(k), cx))

    def send_p2(i, k):
        return send(gw.at[own(i), other_y(k), cx, 0], rp2.at[i, k - 1], p2_s.at[i, k - 1], p2_r.at[i, k - 1], dp=device(other_y(k), cx))

    def send_q2(i):
        return send(gw.at[own(i), cy, 1 - cx, 1], rq2.at[i], q2_s.at[i], q2_r.at[i], dp=device(cy, 1 - cx))

    def send_c(i, k):
        j = i // nf
        return send(gw.at[own(i), cy, cx], rc.at[j, k - 1], c_s.at[i], c_r.at[j, k - 1], feat=owner(i))

    def send_d(i, o, q):
        j = i // nf
        return send(gw.at[own(i), cy, cx], gw_out.at[2 * j + core, q // nx, lax.rem(q, nx)], d_s.at[j, o - 1], d_r.at[j, o - 1],
                    dp=2 * lax.rem(chip + o, nchip) + core)

    def send_e(i, side):
        j = i // nf
        return send(gw_out.at[2 * j + side], gw_out.at[2 * j + side], e_s.at[j], e_r.at[j], dp=partner)

    def step_b(i):
        send_a(i).wait_recv()
        gw[own(i)] += ra[i]
        send_p(i).start()
        for k in range(1, ny):
            send_q(i, k).start()

    def step_b2(i):
        send_p(i).wait_recv()
        gw[own(i), :, cx, 0] += rp[i]
        for k in range(1, ny):
            send_q(i, k).wait_recv()
            gw[own(i), cy, :, 1] += rq[i, k - 1]
        for k in range(1, ny):
            send_p2(i, k).start()
        send_q2(i).start()

    def step_c(i):
        send_q2(i).wait_recv()
        gw[own(i), cy, cx, 1] += rq2[i]
        for k in range(1, ny):
            send_p2(i, k).wait_recv()
            gw[own(i), cy, cx, 0] += rp2[i, k - 1]

        @pl.when(owner(i) != z)
        def _():
            send_c(i, far(i)).start()

    def step_d(i):
        @pl.when(owner(i) == z)
        def _():
            total = gw[own(i), cy, cx]
            for k in range(1, nf):
                send_c(i, k).wait_recv()
                total = total + rc[i // nf, k - 1]
            gw[own(i), cy, cx] = total
            gw_out[2 * (i // nf) + core, cy, cx] = total
            for o in range(1, nchip):
                send_d(i, o, chip).start()

    def step_e(i):
        @pl.when(owner(i) == z)
        def _():
            for o in range(1, nchip):
                send_d(i, o, lax.rem(chip - o + nchip, nchip)).wait_recv()
            send_e(i, core).start()

    def step_f(i):
        @pl.when(owner(i) == z)
        def _():
            send_e(i, 1 - core).wait_recv()

    def drain(i):
        send_a(i).wait_send()
        send_p(i).wait_send()
        send_q2(i).wait_send()
        for k in range(1, ny):
            send_q(i, k).wait_send()
            send_p2(i, k).wait_send()

        @pl.when(owner(i) != z)
        def _():
            send_c(i, far(i)).wait_send()

        @pl.when(owner(i) == z)
        def _():
            for o in range(1, nchip):
                send_d(i, o, chip).wait_send()
            send_e(i, core).wait_send()

    def rows_of(q, side):
        return aligned(side * half + q * sblk, sblk)

    def whole_half(side):
        return aligned(side * half, half)

    def send_ua(i):
        return send(sm.at[i, whole_half(1 - core)], ru.at[i], ua_s.at[i], ua_r.at[i], dp=partner)

    def send_ub(i, o):
        to = lax.rem(chip + o, nchip)
        return send(sm.at[i, rows_of(to, core)], rb.at[i, o - 1], ub_s.at[i, o - 1], ub_r.at[i, o - 1], dp=2 * to + core)

    def send_uc(i, k):
        j = i // nf
        return send(sm.at[i, rows_of(chip, core)], r2.at[j, k - 1], uc_s.at[i], uc_r.at[j, k - 1], feat=owner(i))

    def send_ud(i, o, q):
        j = i // nf
        return send(sm.at[i, rows_of(chip, core)], sm_out.at[j, rows_of(q, core)], ud_s.at[j, o - 1], ud_r.at[j, o - 1],
                    dp=2 * lax.rem(chip + o, nchip) + core)

    def send_ue(i, side):
        j = i // nf
        r = sm_out.at[j, whole_half(side)]
        return send(r, r, ue_s.at[j], ue_r.at[j], dp=partner)

    def send_u(i, o):
        to = lax.rem(me + o, nd)
        return send(sm.at[i, rows_of(to // 2, lax.rem(to, 2))], r1.at[i - direct, o - 1], u_s.at[i - direct, o - 1],
                    u_r.at[i - direct, o - 1], dp=to)

    def send_y(i, o, q):
        j = i - direct
        return send(sm.at[i, rows_of(chip, core)], sm_out.at[i // nf, rows_of(q // 2, lax.rem(q, 2))], y_s.at[j, o - 1], y_r.at[j, o - 1],
                    dp=lax.rem(me + o, nd))

    def send_f(i, k, src):
        j = i // nf
        return send(gf.at[i], fr_out.at[src, aligned(j * feats, feats)], f_s.at[i], f_r.at[j, k - 1], feat=owner(i))

    def start_f(i):
        @pl.when(owner(i) != z)
        def _():
            send_f(i, far(i), z).start()

        @pl.when(owner(i) == z)
        def _():
            fr_out[z, aligned((i // nf) * feats, feats), :] = gf[i]

    def wait_f(i):
        @pl.when(owner(i) == z)
        def _():
            for k in range(1, nf):
                send_f(i, k, lax.rem(z - k + nf, nf)).wait_recv()

    def start_ua(i):
        send_ua(i).start()
        start_f(i)

    def step_ub(i):
        send_ua(i).wait_recv()
        sm[i, whole_half(core), :] += ru[i]
        for o in range(1, nchip):
            send_ub(i, o).start()

    def step_uc(i):
        r = rows_of(chip, core)
        total = sm[i, r, :]
        for o in range(1, nchip):
            send_ub(i, o).wait_recv()
            total = total + rb[i, o - 1]
        sm[i, r, :] = total

        @pl.when(owner(i) != z)
        def _():
            send_uc(i, far(i)).start()

    def gather_z(i):
        r = rows_of(chip, core)
        total = sm[i, r, :]
        for k in range(1, nf):
            send_uc(i, k).wait_recv()
            total = total + r2[i // nf, k - 1]
        sm[i, r, :] = total
        sm_out[i // nf, r, :] = total

    def step_ud(i):
        @pl.when(owner(i) == z)
        def _():
            gather_z(i)
            for o in range(1, nchip):
                send_ud(i, o, chip).start()

    def step_ue(i):
        @pl.when(owner(i) == z)
        def _():
            for o in range(1, nchip):
                send_ud(i, o, lax.rem(chip - o + nchip, nchip)).wait_recv()
            send_ue(i, core).start()

    def step_uf(i):
        @pl.when(owner(i) == z)
        def _():
            send_ue(i, 1 - core).wait_recv()

        wait_f(i)

    def drain_small(i):
        send_ua(i).wait_send()
        for o in range(1, nchip):
            send_ub(i, o).wait_send()

        @pl.when(owner(i) != z)
        def _():
            send_uc(i, far(i)).wait_send()
            send_f(i, far(i), z).wait_send()

        @pl.when(owner(i) == z)
        def _():
            for o in range(1, nchip):
                send_ud(i, o, chip).wait_send()
            send_ue(i, core).wait_send()

    def start_u(i):
        for o in range(1, nd):
            send_u(i, o).start()

    def step_v(i):
        r = rows_of(chip, core)
        total = sm[i, r, :]
        for o in range(1, nd):
            send_u(i, o).wait_recv()
            total = total + r1[i - direct, o - 1]
        sm[i, r, :] = total

        @pl.when(owner(i) != z)
        def _():
            send_uc(i, far(i)).start()

    def step_y(i):
        @pl.when(owner(i) == z)
        def _():
            gather_z(i)
            for o in range(1, nd):
                send_y(i, o, me).start()

    def step_w(i):
        @pl.when(owner(i) == z)
        def _():
            for o in range(1, nd):
                send_y(i, o, lax.rem(me - o + nd, nd)).wait_recv()

        wait_f(i)

    def drain_direct(i):
        for o in range(1, nd):
            send_u(i, o).wait_send()

        @pl.when(owner(i) != z)
        def _():
            send_uc(i, far(i)).wait_send()
            send_f(i, far(i), z).wait_send()

        @pl.when(owner(i) == z)
        def _():
            for o in range(1, nd):
                send_y(i, o, me).wait_send()

    def when_chunk(i, f, first=0, end=chunks):
        @pl.when((i >= first) & (i < end))
        def _():
            f(i)

    start_a = lambda i: send_a(i).start()
    stages = ((start_a, (0, 1, 2, 3)), (step_b, (1, 2, 3, 4)), (step_b2, (3, 4, 5, 6)), (step_c, (5, 6, 7, 8)),
              (step_d, (7, 8, 9, 10)), (step_e, (9, 10, 11)))

    def pairs(k, among):
        for step, times in stages:
            for j, at in enumerate(times):
                if at in among:
                    @pl.when(k == at)
                    def _():
                        for i in (2 * j, 2 * j + 1):
                            step(i)

    def early(j):
        @pl.when(j == 0)
        def _():
            ready()

        pairs(j, range(4))

    def late(t):
        when_chunk(t - 1, start_ua, 0, direct)
        when_chunk(t - 1, start_u, direct)
        when_chunk(t - 1, start_f, direct)
        pairs(t + 4, range(4, 12))
        when_chunk(t - 2, step_ub, 0, direct)
        when_chunk(t - 4, step_uc, 0, direct)
        when_chunk(t - 6, step_ud, 0, direct)

    x = ((xh0, x80, xl0), (xh1, x81, xl1))
    s1[...] = s_ref[...] * sc_ref[0:0 + 1, 0:1]
    s2[...] = s_ref[...] * sc_ref[6:6 + 1, 0:1]

    def cols(i):
        return aligned(place(i) * CHUNK, CHUNK)

    def prepare(i, to):
        for n in range(0, count, TILE):
            v = (e_ref[n:n + TILE, cols(i)][:, None, :] * s1[:, cols(i)][None]).reshape(TILE * members, CHUNK)
            r = slice(n * members, (n + TILE) * members)
            to[0][r, :], to[1][r, :], to[2][r, :] = split3(v)

    prepare(0, x[0])
    for copy in loads[:3]:
        copy.wait()
    for copy in loads[3:]:
        copy.start()

    def weights(j, carry):
        for par in (0, 1):
            i = 2 * j + par
            xh, x8, xl = x[par]
            r = dot(th[...], xh[...]) + (dot(t8[...], xl[...]) + dot(tl[...], x8[...])) * (1.0 / LO)
            gw[aligned(2 * place(i), 2)] = (r.T * sc_ref[5:5 + 1, 0:1]).reshape(2, ny, nx, 2, blk, dout)
            prepare(jnp.minimum(i + 1, chunks - 1), x[1 - par])
        early(j)
        return carry

    lax.fori_loop(0, chunks // 2, weights, 0)

    for copy in loads[3:]:
        copy.wait()
    gsin[...] = jnp.zeros_like(gsin)
    g1[...] = jnp.zeros_like(g1)
    step = g0.shape[0]
    objs = step // members
    parts = rows // step

    def finish(i, t, g):
        g3 = g[...].reshape(objs, members, CHUNK)
        ns = slice(t * objs, (t + 1) * objs)
        ge[ns, :] = jnp.sum(g3 * s2[:, cols(i)][None], axis=1)
        gsin[...] += jnp.sum(g3 * e_ref[ns, cols(i)][:, None, :], axis=0)

    def table(i):
        c = place(i)
        first = c * feats
        base = (first // flocal) * (3 * flocal) + lax.rem(first, flocal)
        for j in range(CHUNK // 128):
            et[j * 128:(j + 1) * 128, :] = ge[:, j * 128:(j + 1) * 128].T
        lane = lax.broadcasted_iota(jnp.int32, (16, 128), 1)
        for p in range(feats // 2):
            row = base + 2 * p
            eh, el = encode_pair(raw_ref, flocal, row)
            gh_, gl_ = split2(et[p * 32:(p + 1) * 32, :])
            both = dot_nt(jnp.concatenate([gh_, gl_], axis=0), eh)
            full = both[:32] + both[32:] + dot_nt(gh_, el)
            sm[i, p * 16:(p + 1) * 16, :] = jnp.where(lane < 64, full[:16], full[16:])
        at = feats * 8
        for j in range(CHUNK // 128):
            sm[i, at:at + members, :] = gsin[:, j * 128:(j + 1) * 128] * sc_ref[7:7 + 1, 0:1]
            at += members
        sm[i, at:at + members, :] = z_ref[:, aligned(c * 128, 128)]
        at += members
        sm[i, at:, :] = jnp.zeros_like(sm[i, at:, :])
        gsin[...] = jnp.zeros_like(gsin)

    def slopes(i):
        c = place(i)
        first = c * feats
        base = (first // flocal) * (3 * flocal) + lax.rem(first, flocal)
        level = lax.broadcasted_iota(jnp.int32, (64, 128), 0).astype(F32)
        for p in range(feats // 2):
            row = base + 2 * p
            lh, ll = split2(table_pair(t_ref, c * (feats // 2) + p))
            g = et[p * 32:(p + 1) * 32, :]
            hot = []
            for f in (row, row + 1):
                here = 1.0 - raw_ref[pl.ds(f + 2 * flocal, 1), :]
                hot.append(jnp.where(level == raw_ref[pl.ds(f, 1), :], here, 0.0))
            one = jnp.concatenate(hot, axis=0).astype(BF16)
            both = dot(jnp.concatenate([lh, ll], axis=0), one)
            picked = (both[:32] + both[32:]) * g
            gf[i, 2 * p:2 * p + 1, :] = jnp.sum(picked[:16], axis=0, keepdims=True)
            gf[i, 2 * p + 1:2 * p + 2, :] = jnp.sum(picked[16:], axis=0, keepdims=True)

    def inputs(i, carry):
        before = jnp.maximum(i - 1, 0)
        wc = wh[cols(i), :]
        wcat[:, :dout] = wl[cols(i), :]
        wcat[:, dout:] = w8[cols(i), :]
        finish(before, parts - 1, g1)
        table(before)
        slopes(before)
        for t in range(parts):
            to, fro = (g0, g1) if t % 2 == 0 else (g1, g0)
            rs = slice(t * step, (t + 1) * step)
            to[...] = dot_nt(gh[rs, :], wc) + dot_nt(g8l[rs, :], wcat[...])
            if t > 0:
                finish(i, t - 1, fro)
        late(i)
        return carry

    lax.fori_loop(0, chunks, inputs, 0)
    last = chunks - 1
    finish(last, parts - 1, g1)
    table(last)
    start_u(last)
    slopes(last)
    start_f(last)
    for i in range(direct - 4):
        step_ue(i)
    for i in range(direct - 4, direct - 2):
        step_ud(i)
    step_e(last - 1)
    step_e(last)
    for i in range(direct - 2, direct):
        step_uc(i)
    step_v(last - 1)
    step_v(last)
    for i in range(direct - 4, direct - 2):
        step_ue(i)
    for i in range(direct - 2, direct):
        step_ud(i)
    step_y(last - 1)
    step_y(last)
    for i in range(direct - 2, direct):
        step_ue(i)
    for i in range(chunks):
        step_f(i)
    for i in range(direct):
        step_uf(i)
    step_w(last - 1)

    def close(i, carry):
        drain(i)
        when_chunk(i, drain_small, 0, direct)
        when_chunk(i, drain_direct, direct)
        return carry

    lax.fori_loop(0, chunks, close, 0)
    step_w(last)


def final_kernel(nf, bins, gw_in, sm_ref, fr_ref, frac_ref, tab_ref, bias_ref, miss_ref, sin_ref, gw_out, so_ref, bo_ref):
    gw_out[...] = gw_in[...]
    flocal = fr_ref.shape[1]
    for o in range(nf):
        frac_ref[:, o * 128:(o + 1) * 128] = fr_ref[o]
    members = sin_ref.shape[0]
    feats = CHUNK // 16
    width = so_ref.shape[1]
    small = []
    for j in range(sm_ref.shape[0]):
        for p in range(feats // 2):
            block = sm_ref[j, p * 16:(p + 1) * 16, :]
            for odd in (0, 1):
                f = j * feats + 2 * p + odd
                tab_ref[f] = block[:, odd * 64:odd * 64 + bins]
                bias_ref[:, f:f + 1] = block[:, odd * 64 + bins:odd * 64 + bins + 1]
                miss_ref[:, f:f + 1] = block[:, odd * 64 + bins + 1:odd * 64 + bins + 2]
        at = feats * 8
        for q in range(CHUNK // 128):
            sin_ref[:, j * CHUNK + q * 128:j * CHUNK + (q + 1) * 128] = sm_ref[j, at:at + members, :]
            at += members
        small.append(sm_ref[j, at:at + members, :])
    small = small[0] if len(small) == 1 else jnp.concatenate(small, axis=1)
    so_ref[...] = small[:, :width]
    bo_ref[...] = small[:, width:]


def params(**kw):
    return pltpu.CompilerParams(vmem_limit_bytes=VMEM_LIMIT, **kw)


def whole(shape):
    return pl.BlockSpec(shape, lambda *_: (0,) * len(shape))


def exchange(nd, nf, bins, fr, ms, tab, bias, miss, s, so, w, ct):
    flocal, total = bins.shape
    width = tab.shape[1]
    count, (din, dout) = total // nf, w.shape
    parts = 8
    ins = (bins, fr, ms, tab, bias, miss, s, so)
    shapes = [jax.ShapeDtypeStruct(x, F32) for x in ((nf * 3 * flocal, count), (nf * flocal // 2 * width, 128), (count, din), (8, 128))]
    far = [jax.ShapeDtypeStruct(w.shape, d) for d in (BF16, F8, F8)]
    dma = pltpu.SemaphoreType.DMA
    anywhere = pl.BlockSpec(memory_space=pl.ANY)
    return pl.pallas_call(
        functools.partial(exchange_kernel, nd, nf),
        out_shape=shapes + far,
        in_specs=[whole(x.shape) for x in ins] + [anywhere] * 2,
        out_specs=[whole(x.shape) for x in shapes] + [anywhere] * 3,
        scratch_shapes=[pltpu.VMEM((3 * flocal, total), F32), pltpu.VMEM((din, count), F32), pltpu.VMEM(w.shape, F32),
                        pltpu.VMEM((parts, ct.shape[0] // parts) + ct.shape[1:], F32)]
        + [pltpu.VMEM(x.shape, x.dtype) for x in far]
        + [dma((parts + 1,)), dma((3,))] + [dma((nf - 1,))] * 4 + [dma((nf - 1, nd // 2 - 1))] * 2 + [dma((nf - 1,))] * 2,
        compiler_params=params(collective_id=0, has_side_effects=True),
    )(*ins, w, ct)


def forward(nf, e, s, wp, so, bo, ct, sc):
    count, din = e.shape
    members, dout = so.shape
    rows, tiles, block = count * members, count // TILE, TILE * members
    lag = lambda i: jnp.maximum(i - 1, 0)
    big = pl.BlockSpec((TILE, members, dout), lambda i: (lag(i), 0, 0))
    nat = pl.BlockSpec((block, dout), lambda i: (lag(i), 0))
    tra = pl.BlockSpec((dout, block), lambda i: (0, lag(i)))
    return pl.pallas_call(
        functools.partial(forward_kernel, nf),
        out_shape=[jax.ShapeDtypeStruct((count, members, dout), F32)]
        + [jax.ShapeDtypeStruct((rows, dout), d) for d in (BF16, F8, F8)]
        + [jax.ShapeDtypeStruct((dout, rows), d) for d in (BF16, F8, F8)]
        + [jax.ShapeDtypeStruct((members, 2 * dout), F32)],
        grid=(tiles + 1,),
        in_specs=[pl.BlockSpec((TILE, din), lambda i: (0, 0)), pl.BlockSpec((TILE, din), lambda i: (jnp.minimum(i + 1, tiles - 1), 0)),
                  whole(s.shape)] + [pl.BlockSpec(memory_space=pl.ANY)] * 3 + [whole(so.shape), whole(bo.shape), big, whole(sc.shape)],
        out_specs=[big, nat, nat, nat, tra, tra, tra, whole((members, 2 * dout))],
        scratch_shapes=[pltpu.VMEM(so.shape, F32)] * 2 + [pltpu.VMEM(s.shape, F32), pltpu.VMEM(so.shape, F32), pltpu.VMEM(so.shape, F32)]
        + [pltpu.VMEM(w.shape, w.dtype) for w in wp] + [pltpu.SemaphoreType.DMA((3,))]
        + [pltpu.VMEM((block, din), d) for d in (BF16, F8, F8)] * 2
        + [pltpu.VMEM((block, dout), F32)] * 2,
        compiler_params=params(),
    )(e, e, s, *wp, so, bo, ct, sc)


def backward(nd, nf, e, s, zs, raw, t, wp, gp, gt, sc):
    count, din = e.shape
    members = s.shape[0]
    rows, dout = gp[0].shape
    step = rows // 16
    chunks, nchip = din // CHUNK, nd // 2
    per = chunks // nf
    ny, blk, half, sblk = nd // 4, CHUNK // nd // 2, 256 // 2, 256 // nd
    feats, flocal = CHUNK // 16, raw.shape[0] // (3 * nf)
    layout = (ny, 2, 2, blk, dout)
    shapes = [jax.ShapeDtypeStruct(x, F32) for x in ((2 * per,) + layout, (per, 256, 128), (nf, flocal, 128))]
    ins = (e, s, sc)
    far = (zs, raw, t, *wp, *gp, *gt)
    dma = pltpu.SemaphoreType.DMA
    f32 = lambda *shape: pltpu.VMEM(shape, F32)
    return pl.pallas_call(
        functools.partial(backward_kernel, nd, nf),
        out_shape=shapes,
        in_specs=[whole(x.shape) for x in ins] + [pl.BlockSpec(memory_space=pl.ANY)] * len(far),
        out_specs=[whole(x.shape) for x in shapes],
        scratch_shapes=[pltpu.VMEM(x.shape, x.dtype) for x in (zs, raw, t, *wp, gp[0])] + [pltpu.VMEM((rows, 2 * dout), F8)]
        + [pltpu.VMEM(x.shape, x.dtype) for x in gt] + [pltpu.VMEM((CHUNK, 2 * dout), F8)]
        + [f32(*s.shape)] * 2
        + [pltpu.VMEM((rows, CHUNK), d) for d in (BF16, F8, F8)] * 2
        + [f32(step, CHUNK)] * 2
        + [f32(count, CHUNK), f32(members, CHUNK), f32(CHUNK, count)]
        + [f32(2 * chunks, *layout), f32(chunks, 256, 128), f32(chunks, feats, count)]
        + [f32(chunks, *layout), f32(chunks, ny, blk, dout), f32(chunks, ny - 1, 2, blk, dout), f32(chunks, ny - 1, blk, dout),
           f32(chunks, blk, dout), f32(per, nf - 1, 2, blk, dout)]
        + [f32(chunks, half, 128), f32(chunks, nchip - 1, sblk, 128), f32(DIRECT, nd - 1, sblk, 128), f32(per, nf - 1, sblk, 128)]
        + [dma((12,))]
        + [dma((chunks,))] * 4 + [dma((chunks, ny - 1))] * 4 + [dma((chunks,))] * 2 + [dma((chunks,)), dma((per, nf - 1))]
        + [dma((per, nchip - 1))] * 2 + [dma((per,))] * 2 + [dma((chunks,)), dma((per, nf - 1))]
        + [dma((chunks,))] * 2 + [dma((chunks, nchip - 1))] * 2 + [dma((chunks,)), dma((per, nf - 1))]
        + [dma((per, nchip - 1))] * 2 + [dma((per,))] * 2
        + [dma((DIRECT, nd - 1))] * 4,
        compiler_params=params(collective_id=1, has_side_effects=True),
    )(*ins, *far)


def final(nf, bins, gw, sm, fr):
    per, flocal = sm.shape[0], fr.shape[1]
    members, width = 32, gw.shape[1] // nf
    shapes = [jax.ShapeDtypeStruct(x, F32) for x in (
        (flocal, nf * 128), (flocal, 16, bins), (16, flocal), (16, flocal), (members, per * CHUNK), gw.shape, (members, width), (members, width))]
    ins = (gw, sm, fr)
    return pl.pallas_call(functools.partial(final_kernel, nf, bins), out_shape=shapes,
                          in_specs=[whole(x.shape) for x in ins], out_specs=[whole(x.shape) for x in shapes],
                          compiler_params=params())(*ins)


def shards(nd, nf, bins, fractions, missing, bin_table, bin_bias, miss_vector, scale_in, weight, scale_out, bias_out, cotangent):
    raw, packed, e, sc, *wp = exchange(nd, nf, bins.T, fractions.T, missing.T, jnp.transpose(bin_table, (0, 2, 1)), bin_bias.T,
                                       miss_vector.T, scale_in, scale_out, weight, cotangent)
    hidden, *rest = forward(nf, e, scale_in, wp, scale_out, bias_out, cotangent, sc)
    gw, sm, fr = backward(nd, nf, e, scale_in, rest[6], raw, packed, wp, rest[:3], rest[3:6], sc)
    gw = gw.reshape(-1, weight.shape[1])
    frac, table, bias, miss, sin, gw, so, bo = final(nf, bin_table.shape[1], gw, sm, fr)
    return hidden, frac.T, jnp.transpose(table, (0, 2, 1)), bias.T, miss.T, sin, gw, so, bo


def solution(mesh):
    placed = (P("dp", "feat"), P("dp", "feat"), P("dp", "feat"), P("feat", None, None), P("feat", None), P("feat", None),
              P(), P(), P(), P(), P(("dp", "feat"), None, None))
    return jax.shard_map(
        functools.partial(shards, mesh.shape["dp"], mesh.shape["feat"]),
        mesh=mesh,
        in_specs=placed,
        out_specs=(P(("dp", "feat"), None, None), P("dp", "feat"), P("feat", None, None), P("feat", None), P("feat", None),
                   P(None, "feat"), P("feat", None), P(None, "feat"), P(None, "feat")),
        check_vma=False,
    )
```

```python
import functools

import jax
import jax.numpy as jnp
from jax import lax
from jax.experimental import pallas as pl
from jax.experimental.pallas import tpu as pltpu
from jax.sharding import PartitionSpec as P

F32, BF16, F8 = jnp.float32, jnp.bfloat16, jnp.float8_e4m3fn
VMEM_LIMIT = 63 << 20
TILE = 16
DIRECT = 2
CHUNK = 256
TOP = 224.0
TOP_WEIGHT = 400.0
LO = 256.0
GELU_A = 0.7978845608028654
GELU_B = GELU_A * 0.044715


def dot(a, b):
    return jnp.dot(a, b, preferred_element_type=F32)


def dot_nt(a, b):
    return lax.dot_general(a, b, (((1,), (1,)), ((), ())), preferred_element_type=F32)


def split3(x):
    hi = x.astype(BF16)
    return hi, hi.astype(F8), ((x - hi.astype(F32)).astype(BF16) * BF16(LO)).astype(F8)


def split2(x):
    hi = x.astype(BF16)
    return hi, (x - hi.astype(F32)).astype(BF16)


def split3_weight(x):
    hi = x.astype(BF16)
    return hi, (x * (1.0 / LO)).astype(F8), (x - hi.astype(F32)).astype(F8)


def encode_pair(raw_ref, flocal, first):
    level = lax.broadcasted_iota(jnp.int32, (48, 128), 0).astype(F32)
    row = lax.broadcasted_iota(jnp.int32, (16, 128), 0)
    high, low = [], []
    for f in (first, first + 1):
        b, fr, m = [raw_ref[pl.ds(f + k * flocal, 1), :] for k in range(3)]
        here = 1.0 - m
        rest = (fr - fr.astype(BF16).astype(F32)) * here
        high.append(jnp.clip((b - level) + fr, 0.0, 1.0) * here)
        high.append(jnp.where(row == 0, here, jnp.where(row == 1, m, 0.0)))
        low.append(jnp.where(level == b, rest, 0.0))
        low.append(jnp.zeros((16, 128), F32))
    return jnp.concatenate(high, axis=0).astype(BF16), jnp.concatenate(low, axis=0).astype(BF16)


def table_pair(t_ref, p):
    blk = t_ref[pl.ds(pl.multiple_of(p * 16, 16), 16), :]
    lane = lax.broadcasted_iota(jnp.int32, (16, 128), 1)
    zero = jnp.zeros_like(blk)
    return jnp.concatenate([jnp.where(lane < 64, blk, zero), jnp.where(lane < 64, zero, blk)], axis=0)


def send(src, dst, ssem, rsem, **where):
    return pltpu.make_async_remote_copy(src_ref=src, dst_ref=dst, send_sem=ssem, recv_sem=rsem, device_id=where,
                                        device_id_type=pl.DeviceIdType.MESH)


def greet(partners):
    barrier = pltpu.get_barrier_semaphore()
    for where in partners:
        pl.semaphore_signal(barrier, inc=1, device_id=where, device_id_type=pl.DeviceIdType.MESH)
    return lambda: pl.semaphore_wait(barrier, len(partners))


def exchange_kernel(nd, nf, bins_ref, fr_ref, ms_ref, tab_ref, bias_ref, miss_ref, s_ref, so_ref, w_in, ct_in,
                    raw_ref, t_ref, e_ref, sc_ref, wh_out, w8_out, wl_out,
                    mine, et, w, ct, wh, w8, wl, load, store, r_s, r_r, x_s, x_r, y_s, y_r, z_s, z_r):
    flocal, total = bins_ref.shape
    count = total // nf
    bins, width = tab_ref.shape[2], tab_ref.shape[1]
    me, z = lax.axis_index("dp"), lax.axis_index("feat")
    nchip = nd // 2
    core, chip = lax.rem(me, 2), me // 2
    partner = me + 1 - 2 * core
    parts = ct.shape[0]
    step = ct_in.shape[0] // parts

    ready = greet([{"feat": lax.rem(z + o, nf)} for o in range(1, nf)]
                  + [{"dp": 2 * lax.rem(chip + o, nchip) + core} for o in range(1, nchip)] + [{"dp": partner}])
    loads = [pltpu.make_async_copy(w_in, w, load.at[0])] + [
        pltpu.make_async_copy(ct_in.at[pl.ds(i * step, step)], ct.at[i], load.at[i + 1]) for i in range(parts)]
    for copy in loads:
        copy.start()

    def rows(q):
        return pl.ds(pl.multiple_of(q * (3 * flocal), 3 * flocal), 3 * flocal)

    size = flocal // 2 * width // nd

    def entries(q, piece, n):
        return t_ref.at[pl.ds(pl.multiple_of(q * (nd * size) + piece * size, 8), n * size)]

    mine[0:flocal, :] = bins_ref[...].astype(F32)
    mine[flocal:2 * flocal, :] = fr_ref[...]
    mine[2 * flocal:, :] = ms_ref[...].astype(F32)
    raw_ref[rows(z), :] = mine[:, pl.ds(pl.multiple_of(z * count, count), count)]
    blank = jnp.zeros((width, 64 - bins - 2), F32)
    for p in range(flocal // 2):
        block = []
        for f in (2 * p, 2 * p + 1):
            block += [tab_ref[f], bias_ref[:, f:f + 1], miss_ref[:, f:f + 1], blank]
        t_ref[pl.ds(pl.multiple_of(z * (flocal // 2 * width) + p * width, width), width), :] = jnp.concatenate(block, axis=1)

    def send_raw(o, q):
        to = lax.rem(z + o, nf)
        return send(mine.at[:, pl.ds(pl.multiple_of(to * count, count), count)], raw_ref.at[rows(q)],
                    r_s.at[o - 1], r_r.at[o - 1], feat=to)

    def send_x(o, q):
        r = entries(q, core * nchip + chip, 1)
        return send(r, r, x_s.at[o - 1], x_r.at[o - 1], feat=lax.rem(z + o, nf))

    def send_y(o, k, c):
        r = entries(lax.rem(z - o + nf, nf), core * nchip + c, 1)
        return send(r, r, y_s.at[o - 1, k - 1], y_r.at[o - 1, k - 1], dp=2 * lax.rem(chip + k, nchip) + core)

    def send_z(o, side):
        r = entries(lax.rem(z - o + nf, nf), side * nchip, nchip)
        return send(r, r, z_s.at[o - 1], z_r.at[o - 1], dp=partner)

    others = range(1, nf)
    ready()
    for o in others:
        send_x(o, z).start()
    for o in others:
        send_raw(o, z).start()

    def top(v):
        return jnp.maximum(jnp.max(jnp.max(jnp.abs(v), axis=0, keepdims=True), axis=1, keepdims=True), 1e-30)

    pairs = flocal // 2
    at_once = min(16, pairs)
    entries_local = flocal * width

    def embed(q):
        def body(j, c):
            for k in range(at_once):
                p = q * pairs + j * at_once + k
                first = q * (3 * flocal) + 2 * (j * at_once + k)
                lh, ll = split2(table_pair(t_ref, p))
                eh, el = encode_pair(raw_ref, flocal, first)
                both = dot(jnp.concatenate([lh, ll], axis=0), eh)
                et[pl.ds(pl.multiple_of(p * 32, 32), 32), :] = both[:32] + both[32:] + dot(lh, el)
            return c

        lax.fori_loop(0, pairs // at_once, body, 0)
        for j in range(entries_local // 128):
            at = pl.ds(pl.multiple_of(q * entries_local + j * 128, 128), 128)
            e_ref[:, at] = et[at, :].T

    embed(z)
    for o in others:
        send_x(o, lax.rem(z - o + nf, nf)).wait_recv()
        for k in range(1, nchip):
            send_y(o, k, chip).start()

    loads[0].wait()
    sw = TOP_WEIGHT / top(w[...])
    for i in range(0, w.shape[0], 256):
        r = slice(i, i + 256)
        wh[r, :], w8[r, :], wl[r, :] = split3_weight(w[r, :] * sw)
    stores = [pltpu.make_async_copy(i, o, store.at[k]) for k, (i, o) in enumerate(((wh, wh_out), (w8, w8_out), (wl, wl_out)))]
    for copy in stores:
        copy.start()

    for o in others:
        for k in range(1, nchip):
            send_y(o, k, lax.rem(chip - k + nchip, nchip)).wait_recv()
        send_z(o, core).start()
    tc = jnp.full((1, 1), 1e-30, F32)
    for i in range(parts):
        loads[i + 1].wait()
        tc = jnp.maximum(tc, top(ct[i].reshape(-1, ct.shape[-1])))
    for o in others:
        q = lax.rem(z - o + nf, nf)
        send_z(o, 1 - core).wait_recv()
        send_raw(o, q).wait_recv()
        embed(q)
    sx = TOP / jnp.maximum(top(et[...]) * top(s_ref[...]), 1e-30)
    sg = TOP / (1.2 * tc * top(so_ref[...]))
    for k, v in enumerate((sx, sw, sg, 1.0 / (sx * sw), 1.0 / (sx * sw), 1.0 / (sg * sx), 1.0 / (sg * sw), 1.0 / (sg * sw))):
        sc_ref[k:k + 1, :] = jnp.broadcast_to(v, (1, 128))
    for copy in stores:
        copy.wait()
    for o in others:
        send_raw(o, z).wait_send()
        send_x(o, z).wait_send()
        for k in range(1, nchip):
            send_y(o, k, chip).wait_send()
        send_z(o, core).wait_send()


def forward_kernel(nf, e0_ref, e_ref, s_ref, wh_in, w8_in, wl_in, so_ref, bo_ref, ct_ref, sc_ref,
                   hid_ref, gh_ref, g8_ref, gl_ref, th_ref, t8_ref, tl_ref, z_ref,
                   gs_ref, gb_ref, s1, so1, so2, wh_ref, w8_ref, wl_ref, load, xh0, x80, xl0, xh1, x81, xl1, pre0, pre1):
    i = pl.program_id(0)
    tiles = pl.num_programs(0) - 1
    members, width_out = so_ref.shape
    rows = TILE * members
    x = ((xh0, x80, xl0), (xh1, x81, xl1))
    pre = (pre0, pre1)

    def prepare(e, to):
        for n in range(TILE):
            v = s1[...] * e[n:n + 1, :]
            r = slice(n * members, (n + 1) * members)
            to[0][r, :], to[1][r, :], to[2][r, :] = split3(v)

    def multiply(a, to):
        to[...] = dot(a[0][...], wh_ref[...]) + (dot(a[1][...], wl_ref[...]) + dot(a[2][...], w8_ref[...]))

    def finish(p):
        for h0 in range(0, width_out, 128):
            hs = slice(h0, h0 + 128)
            sa, sb, bo = so1[:, hs], so2[:, hs], bo_ref[:, hs]
            gs, gb = gs_ref[:, hs], gb_ref[:, hs]
            for n in range(TILE):
                r = slice(n * members, (n + 1) * members)
                q = p[r, hs]
                v = q * sa + bo
                v2 = v * v
                half = 0.5 + 0.5 * jnp.tanh(v * (GELU_B * v2 + GELU_A))
                hid = v * half
                hid_ref[n, :, hs] = hid
                g = half + hid * (1.0 - half) * ((6.0 * GELU_B) * v2 + 2.0 * GELU_A)
                ga = ct_ref[n, :, hs] * g
                gs = gs + ga * q
                gb = gb + ga
                gh_ref[r, hs], g8_ref[r, hs], gl_ref[r, hs] = split3(ga * sb)
            gs_ref[:, hs], gb_ref[:, hs] = gs, gb
        th_ref[...] = gh_ref[...].T
        t8_ref[...] = g8_ref[...].T
        tl_ref[...] = gl_ref[...].T

    @pl.when(i == 0)
    def _():
        loads = [pltpu.make_async_copy(a, b, load.at[k]) for k, (a, b) in enumerate(
            ((wh_in, wh_ref), (w8_in, w8_ref), (wl_in, wl_ref)))]
        for copy in loads:
            copy.start()
        s1[...] = s_ref[...] * sc_ref[0:0 + 1, 0:1]
        so1[...] = so_ref[...] * sc_ref[3:3 + 1, 0:1]
        so2[...] = so_ref[...] * sc_ref[2:2 + 1, 0:1]
        gs_ref[...] = jnp.zeros_like(gs_ref)
        gb_ref[...] = jnp.zeros_like(gb_ref)
        prepare(e0_ref, x[0])
        for copy in loads:
            copy.wait()
        prepare(e_ref, x[1])
        multiply(x[0], pre[0])

    for par in (0, 1):
        @pl.when((i > 0) & (i < tiles) & (i % 2 == par))
        def _():
            prepare(e_ref, x[1 - par])
            finish(pre[1 - par])
            multiply(x[par], pre[par])

    @pl.when(i == tiles)
    def _():
        finish(pre[1])
        part = width_out // nf
        for o in range(nf):
            z_ref[:, 2 * o * part:(2 * o + 1) * part] = gs_ref[:, o * part:(o + 1) * part] * sc_ref[4:4 + 1, 0:1]
            z_ref[:, (2 * o + 1) * part:(2 * o + 2) * part] = gb_ref[:, o * part:(o + 1) * part]


def backward_kernel(nd, nf, e_ref, s_ref, sc_ref, z_in, raw_in, t_in, wh_in, w8_in, wl_in, gh_in, g8_in, gl_in,
                    th_in, t8_in, tl_in, gw_out, sm_out, fr_out,
                    z_ref, raw_ref, t_ref, wh, w8, wl, gh, g8l, th, t8, tl, wcat, s1, s2, xh0, x80, xl0, xh1, x81, xl1, g0, g1, ge, gsin, et,
                    gw, sm, gf, ra, rp, rq, rp2, rq2, rc, ru, rb, r1, r2,
                    load, a_s, a_r, p_s, p_r, q_s, q_r, p2_s, p2_r, q2_s, q2_r, c_s, c_r, d_s, d_r, e_s, e_r, f_s, f_r,
                    ua_s, ua_r, ub_s, ub_r, uc_s, uc_r, ud_s, ud_r, ue_s, ue_r, u_s, u_r, y_s, y_r):
    members, width_in = s_ref.shape
    rows = gh.shape[0]
    count = e_ref.shape[0]
    chunks = width_in // CHUNK
    direct = chunks - DIRECT
    per = chunks // nf
    nx, ny, nchip = 2, nd // 4, nd // 2
    blk, dout = gw.shape[4], gw.shape[5]
    half, sblk = sm.shape[1] // 2, sm.shape[1] // nd
    feats = CHUNK // 16
    flocal = fr_out.shape[1]
    me, z = lax.axis_index("dp"), lax.axis_index("feat")
    core, chip = lax.rem(me, 2), me // 2
    cx, cy = lax.rem(chip, nx), chip // nx
    partner = me + 1 - 2 * core

    ready = greet([{"dp": lax.rem(me + o, nd)} for o in range(1, nd)] + [{"feat": lax.rem(z + o, nf)} for o in range(1, nf)])
    loads = [pltpu.make_async_copy(i, o, load.at[k]) for k, (i, o) in enumerate(
        ((th_in, th), (t8_in, t8), (tl_in, tl), (wh_in, wh), (w8_in, w8), (wl_in, wl), (gh_in, gh), (g8_in, g8l.at[:, :dout]), (gl_in, g8l.at[:, dout:]),
         (z_in, z_ref), (raw_in, raw_ref), (t_in, t_ref)))]
    for copy in loads[:3]:
        copy.start()

    def aligned(i, n):
        return pl.ds(pl.multiple_of(i, n), n)

    def owner(i):
        return lax.rem(i + nf // 2 + 1, nf)

    def place(i):
        return owner(i) * per + i // nf

    def far(i):
        return lax.rem(owner(i) - z + nf, nf)

    def device(y, x):
        return 2 * (y * nx + x) + core

    def other_y(k):
        return lax.rem(cy + k, ny)

    def from_y(k):
        return lax.rem(cy - k + ny, ny)

    def own(i):
        return 2 * place(i) + core

    def send_a(i):
        return send(gw.at[2 * place(i) + 1 - core], ra.at[i], a_s.at[i], a_r.at[i], dp=partner)

    def send_p(i):
        return send(gw.at[own(i), :, 1 - cx, 0], rp.at[i], p_s.at[i], p_r.at[i], dp=device(cy, 1 - cx))

    def send_q(i, k):
        return send(gw.at[own(i), other_y(k), :, 1], rq.at[i, k - 1], q_s.at[i, k - 1], q_r.at[i, k - 1], dp=device(other_y(k), cx))

    def send_p2(i, k):
        return send(gw.at[own(i), other_y(k), cx, 0], rp2.at[i, k - 1], p2_s.at[i, k - 1], p2_r.at[i, k - 1], dp=device(other_y(k), cx))

    def send_q2(i):
        return send(gw.at[own(i), cy, 1 - cx, 1], rq2.at[i], q2_s.at[i], q2_r.at[i], dp=device(cy, 1 - cx))

    def send_c(i, k):
        j = i // nf
        return send(gw.at[own(i), cy, cx], rc.at[j, k - 1], c_s.at[i], c_r.at[j, k - 1], feat=owner(i))

    def send_d(i, o, q):
        j = i // nf
        return send(gw.at[own(i), cy, cx], gw_out.at[2 * j + core, q // nx, lax.rem(q, nx)], d_s.at[j, o - 1], d_r.at[j, o - 1],
                    dp=2 * lax.rem(chip + o, nchip) + core)

    def send_e(i, side):
        j = i // nf
        return send(gw_out.at[2 * j + side], gw_out.at[2 * j + side], e_s.at[j], e_r.at[j], dp=partner)

    def step_b(i):
        send_a(i).wait_recv()
        gw[own(i)] += ra[i]
        send_p(i).start()
        for k in range(1, ny):
            send_q(i, k).start()

    def step_b2(i):
        send_p(i).wait_recv()
        gw[own(i), :, cx, 0] += rp[i]
        for k in range(1, ny):
            send_q(i, k).wait_recv()
            gw[own(i), cy, :, 1] += rq[i, k - 1]
        for k in range(1, ny):
            send_p2(i, k).start()
        send_q2(i).start()

    def step_c(i):
        send_q2(i).wait_recv()
        gw[own(i), cy, cx, 1] += rq2[i]
        for k in range(1, ny):
            send_p2(i, k).wait_recv()
            gw[own(i), cy, cx, 0] += rp2[i, k - 1]

        @pl.when(owner(i) != z)
        def _():
            send_c(i, far(i)).start()

    def step_d(i):
        @pl.when(owner(i) == z)
        def _():
            total = gw[own(i), cy, cx]
            for k in range(1, nf):
                send_c(i, k).wait_recv()
                total = total + rc[i // nf, k - 1]
            gw[own(i), cy, cx] = total
            gw_out[2 * (i // nf) + core, cy, cx] = total
            for o in range(1, nchip):
                send_d(i, o, chip).start()

    def step_e(i):
        @pl.when(owner(i) == z)
        def _():
            for o in range(1, nchip):
                send_d(i, o, lax.rem(chip - o + nchip, nchip)).wait_recv()
            send_e(i, core).start()

    def step_f(i):
        @pl.when(owner(i) == z)
        def _():
            send_e(i, 1 - core).wait_recv()

    def drain(i):
        send_a(i).wait_send()
        send_p(i).wait_send()
        send_q2(i).wait_send()
        for k in range(1, ny):
            send_q(i, k).wait_send()
            send_p2(i, k).wait_send()

        @pl.when(owner(i) != z)
        def _():
            send_c(i, far(i)).wait_send()

        @pl.when(owner(i) == z)
        def _():
            for o in range(1, nchip):
                send_d(i, o, chip).wait_send()
            send_e(i, core).wait_send()

    def rows_of(q, side):
        return aligned(side * half + q * sblk, sblk)

    def whole_half(side):
        return aligned(side * half, half)

    def send_ua(i):
        return send(sm.at[i, whole_half(1 - core)], ru.at[i], ua_s.at[i], ua_r.at[i], dp=partner)

    def send_ub(i, o):
        to = lax.rem(chip + o, nchip)
        return send(sm.at[i, rows_of(to, core)], rb.at[i, o - 1], ub_s.at[i, o - 1], ub_r.at[i, o - 1], dp=2 * to + core)

    def send_uc(i, k):
        j = i // nf
        return send(sm.at[i, rows_of(chip, core)], r2.at[j, k - 1], uc_s.at[i], uc_r.at[j, k - 1], feat=owner(i))

    def send_ud(i, o, q):
        j = i // nf
        return send(sm.at[i, rows_of(chip, core)], sm_out.at[j, rows_of(q, core)], ud_s.at[j, o - 1], ud_r.at[j, o - 1],
                    dp=2 * lax.rem(chip + o, nchip) + core)

    def send_ue(i, side):
        j = i // nf
        r = sm_out.at[j, whole_half(side)]
        return send(r, r, ue_s.at[j], ue_r.at[j], dp=partner)

    def send_u(i, o):
        to = lax.rem(me + o, nd)
        return send(sm.at[i, rows_of(to // 2, lax.rem(to, 2))], r1.at[i - direct, o - 1], u_s.at[i - direct, o - 1],
                    u_r.at[i - direct, o - 1], dp=to)

    def send_y(i, o, q):
        j = i - direct
        return send(sm.at[i, rows_of(chip, core)], sm_out.at[i // nf, rows_of(q // 2, lax.rem(q, 2))], y_s.at[j, o - 1], y_r.at[j, o - 1],
                    dp=lax.rem(me + o, nd))

    def send_f(i, k, src):
        j = i // nf
        return send(gf.at[i], fr_out.at[src, aligned(j * feats, feats)], f_s.at[i], f_r.at[j, k - 1], feat=owner(i))

    def start_f(i):
        @pl.when(owner(i) != z)
        def _():
            send_f(i, far(i), z).start()

        @pl.when(owner(i) == z)
        def _():
            fr_out[z, aligned((i // nf) * feats, feats), :] = gf[i]

    def wait_f(i):
        @pl.when(owner(i) == z)
        def _():
            for k in range(1, nf):
                send_f(i, k, lax.rem(z - k + nf, nf)).wait_recv()

    def start_ua(i):
        send_ua(i).start()
        start_f(i)

    def step_ub(i):
        send_ua(i).wait_recv()
        sm[i, whole_half(core), :] += ru[i]
        for o in range(1, nchip):
            send_ub(i, o).start()

    def step_uc(i):
        r = rows_of(chip, core)
        total = sm[i, r, :]
        for o in range(1, nchip):
            send_ub(i, o).wait_recv()
            total = total + rb[i, o - 1]
        sm[i, r, :] = total

        @pl.when(owner(i) != z)
        def _():
            send_uc(i, far(i)).start()

    def gather_z(i):
        r = rows_of(chip, core)
        total = sm[i, r, :]
        for k in range(1, nf):
            send_uc(i, k).wait_recv()
            total = total + r2[i // nf, k - 1]
        sm[i, r, :] = total
        sm_out[i // nf, r, :] = total

    def step_ud(i):
        @pl.when(owner(i) == z)
        def _():
            gather_z(i)
            for o in range(1, nchip):
                send_ud(i, o, chip).start()

    def step_ue(i):
        @pl.when(owner(i) == z)
        def _():
            for o in range(1, nchip):
                send_ud(i, o, lax.rem(chip - o + nchip, nchip)).wait_recv()
            send_ue(i, core).start()

    def step_uf(i):
        @pl.when(owner(i) == z)
        def _():
            send_ue(i, 1 - core).wait_recv()

        wait_f(i)

    def drain_small(i):
        send_ua(i).wait_send()
        for o in range(1, nchip):
            send_ub(i, o).wait_send()

        @pl.when(owner(i) != z)
        def _():
            send_uc(i, far(i)).wait_send()
            send_f(i, far(i), z).wait_send()

        @pl.when(owner(i) == z)
        def _():
            for o in range(1, nchip):
                send_ud(i, o, chip).wait_send()
            send_ue(i, core).wait_send()

    def start_u(i):
        for o in range(1, nd):
            send_u(i, o).start()

    def step_v(i):
        r = rows_of(chip, core)
        total = sm[i, r, :]
        for o in range(1, nd):
            send_u(i, o).wait_recv()
            total = total + r1[i - direct, o - 1]
        sm[i, r, :] = total

        @pl.when(owner(i) != z)
        def _():
            send_uc(i, far(i)).start()

    def step_y(i):
        @pl.when(owner(i) == z)
        def _():
            gather_z(i)
            for o in range(1, nd):
                send_y(i, o, me).start()

    def step_w(i):
        @pl.when(owner(i) == z)
        def _():
            for o in range(1, nd):
                send_y(i, o, lax.rem(me - o + nd, nd)).wait_recv()

        wait_f(i)

    def drain_direct(i):
        for o in range(1, nd):
            send_u(i, o).wait_send()

        @pl.when(owner(i) != z)
        def _():
            send_uc(i, far(i)).wait_send()
            send_f(i, far(i), z).wait_send()

        @pl.when(owner(i) == z)
        def _():
            for o in range(1, nd):
                send_y(i, o, me).wait_send()

    def when_chunk(i, f, first=0, end=chunks):
        @pl.when((i >= first) & (i < end))
        def _():
            f(i)

    start_a = lambda i: send_a(i).start()
    stages = ((start_a, (0, 1, 2, 3)), (step_b, (1, 2, 3, 4)), (step_b2, (3, 4, 5, 6)), (step_c, (5, 6, 7, 8)),
              (step_d, (7, 8, 9, 10)), (step_e, (9, 10, 11)))

    def pairs(k, among):
        for step, times in stages:
            for j, at in enumerate(times):
                if at in among:
                    @pl.when(k == at)
                    def _():
                        for i in (2 * j, 2 * j + 1):
                            step(i)

    def early(j):
        @pl.when(j == 0)
        def _():
            ready()

        pairs(j, range(4))

    def late(t):
        when_chunk(t - 1, start_ua, 0, direct)
        when_chunk(t - 1, start_u, direct)
        when_chunk(t - 1, start_f, direct)
        pairs(t + 4, range(4, 12))
        when_chunk(t - 2, step_ub, 0, direct)
        when_chunk(t - 4, step_uc, 0, direct)
        when_chunk(t - 6, step_ud, 0, direct)

    x = ((xh0, x80, xl0), (xh1, x81, xl1))
    s1[...] = s_ref[...] * sc_ref[0:0 + 1, 0:1]
    s2[...] = s_ref[...] * sc_ref[6:6 + 1, 0:1]

    def cols(i):
        return aligned(place(i) * CHUNK, CHUNK)

    def prepare(i, to):
        for n in range(0, count, TILE):
            v = (e_ref[n:n + TILE, cols(i)][:, None, :] * s1[:, cols(i)][None]).reshape(TILE * members, CHUNK)
            r = slice(n * members, (n + TILE) * members)
            to[0][r, :], to[1][r, :], to[2][r, :] = split3(v)

    prepare(0, x[0])
    for copy in loads[:3]:
        copy.wait()
    for copy in loads[3:]:
        copy.start()

    def weights(j, carry):
        for par in (0, 1):
            i = 2 * j + par
            xh, x8, xl = x[par]
            r = dot(th[...], xh[...]) + (dot(t8[...], xl[...]) + dot(tl[...], x8[...])) * (1.0 / LO)
            gw[aligned(2 * place(i), 2)] = (r.T * sc_ref[5:5 + 1, 0:1]).reshape(2, ny, nx, 2, blk, dout)
            prepare(jnp.minimum(i + 1, chunks - 1), x[1 - par])
        early(j)
        return carry

    lax.fori_loop(0, chunks // 2, weights, 0)

    for copy in loads[3:]:
        copy.wait()
    gsin[...] = jnp.zeros_like(gsin)
    g1[...] = jnp.zeros_like(g1)
    step = g0.shape[0]
    objs = step // members
    parts = rows // step

    def finish(i, t, g):
        g3 = g[...].reshape(objs, members, CHUNK)
        ns = slice(t * objs, (t + 1) * objs)
        ge[ns, :] = jnp.sum(g3 * s2[:, cols(i)][None], axis=1)
        gsin[...] += jnp.sum(g3 * e_ref[ns, cols(i)][:, None, :], axis=0)

    def table(i):
        c = place(i)
        first = c * feats
        base = (first // flocal) * (3 * flocal) + lax.rem(first, flocal)
        for j in range(CHUNK // 128):
            et[j * 128:(j + 1) * 128, :] = ge[:, j * 128:(j + 1) * 128].T
        lane = lax.broadcasted_iota(jnp.int32, (16, 128), 1)
        for p in range(feats // 2):
            row = base + 2 * p
            eh, el = encode_pair(raw_ref, flocal, row)
            gh_, gl_ = split2(et[p * 32:(p + 1) * 32, :])
            both = dot_nt(jnp.concatenate([gh_, gl_], axis=0), eh)
            full = both[:32] + both[32:] + dot_nt(gh_, el)
            sm[i, p * 16:(p + 1) * 16, :] = jnp.where(lane < 64, full[:16], full[16:])
        at = feats * 8
        for j in range(CHUNK // 128):
            sm[i, at:at + members, :] = gsin[:, j * 128:(j + 1) * 128] * sc_ref[7:7 + 1, 0:1]
            at += members
        sm[i, at:at + members, :] = z_ref[:, aligned(c * 128, 128)]
        at += members
        sm[i, at:, :] = jnp.zeros_like(sm[i, at:, :])
        gsin[...] = jnp.zeros_like(gsin)

    def slopes(i):
        c = place(i)
        first = c * feats
        base = (first // flocal) * (3 * flocal) + lax.rem(first, flocal)
        level = lax.broadcasted_iota(jnp.int32, (64, 128), 0).astype(F32)
        for p in range(feats // 2):
            row = base + 2 * p
            lh, ll = split2(table_pair(t_ref, c * (feats // 2) + p))
            g = et[p * 32:(p + 1) * 32, :]
            hot = []
            for f in (row, row + 1):
                here = 1.0 - raw_ref[pl.ds(f + 2 * flocal, 1), :]
                hot.append(jnp.where(level == raw_ref[pl.ds(f, 1), :], here, 0.0))
            one = jnp.concatenate(hot, axis=0).astype(BF16)
            both = dot(jnp.concatenate([lh, ll], axis=0), one)
            picked = (both[:32] + both[32:]) * g
            gf[i, 2 * p:2 * p + 1, :] = jnp.sum(picked[:16], axis=0, keepdims=True)
            gf[i, 2 * p + 1:2 * p + 2, :] = jnp.sum(picked[16:], axis=0, keepdims=True)

    def inputs(i, carry):
        before = jnp.maximum(i - 1, 0)
        wc = wh[cols(i), :]
        wcat[:, :dout] = wl[cols(i), :]
        wcat[:, dout:] = w8[cols(i), :]
        finish(before, parts - 1, g1)
        table(before)
        slopes(before)
        for t in range(parts):
            to, fro = (g0, g1) if t % 2 == 0 else (g1, g0)
            rs = slice(t * step, (t + 1) * step)
            to[...] = dot_nt(gh[rs, :], wc) + dot_nt(g8l[rs, :], wcat[...])
            if t > 0:
                finish(i, t - 1, fro)
        late(i)
        return carry

    lax.fori_loop(0, chunks, inputs, 0)
    last = chunks - 1
    finish(last, parts - 1, g1)
    table(last)
    start_u(last)
    slopes(last)
    start_f(last)
    for i in range(direct - 4):
        step_ue(i)
    for i in range(direct - 4, direct - 2):
        step_ud(i)
    step_e(last - 1)
    step_e(last)
    for i in range(direct - 2, direct):
        step_uc(i)
    step_v(last - 1)
    step_v(last)
    for i in range(direct - 4, direct - 2):
        step_ue(i)
    for i in range(direct - 2, direct):
        step_ud(i)
    step_y(last - 1)
    step_y(last)
    for i in range(direct - 2, direct):
        step_ue(i)
    for i in range(chunks):
        step_f(i)
    for i in range(direct):
        step_uf(i)
    step_w(last - 1)

    def close(i, carry):
        drain(i)
        when_chunk(i, drain_small, 0, direct)
        when_chunk(i, drain_direct, direct)
        return carry

    lax.fori_loop(0, chunks, close, 0)
    step_w(last)


def final_kernel(nf, bins, gw_in, sm_ref, fr_ref, frac_ref, tab_ref, bias_ref, miss_ref, sin_ref, gw_out, so_ref, bo_ref):
    gw_out[...] = gw_in[...]
    flocal = fr_ref.shape[1]
    for o in range(nf):
        frac_ref[:, o * 128:(o + 1) * 128] = fr_ref[o]
    members = sin_ref.shape[0]
    feats = CHUNK // 16
    width = so_ref.shape[1]
    small = []
    for j in range(sm_ref.shape[0]):
        for p in range(feats // 2):
            block = sm_ref[j, p * 16:(p + 1) * 16, :]
            for odd in (0, 1):
                f = j * feats + 2 * p + odd
                tab_ref[f] = block[:, odd * 64:odd * 64 + bins]
                bias_ref[:, f:f + 1] = block[:, odd * 64 + bins:odd * 64 + bins + 1]
                miss_ref[:, f:f + 1] = block[:, odd * 64 + bins + 1:odd * 64 + bins + 2]
        at = feats * 8
        for q in range(CHUNK // 128):
            sin_ref[:, j * CHUNK + q * 128:j * CHUNK + (q + 1) * 128] = sm_ref[j, at:at + members, :]
            at += members
        small.append(sm_ref[j, at:at + members, :])
    small = small[0] if len(small) == 1 else jnp.concatenate(small, axis=1)
    so_ref[...] = small[:, :width]
    bo_ref[...] = small[:, width:]


def params(**kw):
    return pltpu.CompilerParams(vmem_limit_bytes=VMEM_LIMIT, **kw)


def whole(shape):
    return pl.BlockSpec(shape, lambda *_: (0,) * len(shape))


def exchange(nd, nf, bins, fr, ms, tab, bias, miss, s, so, w, ct):
    flocal, total = bins.shape
    width = tab.shape[1]
    count, (din, dout) = total // nf, w.shape
    parts = 8
    ins = (bins, fr, ms, tab, bias, miss, s, so)
    shapes = [jax.ShapeDtypeStruct(x, F32) for x in ((nf * 3 * flocal, count), (nf * flocal // 2 * width, 128), (count, din), (8, 128))]
    far = [jax.ShapeDtypeStruct(w.shape, d) for d in (BF16, F8, F8)]
    dma = pltpu.SemaphoreType.DMA
    anywhere = pl.BlockSpec(memory_space=pl.ANY)
    return pl.pallas_call(
        functools.partial(exchange_kernel, nd, nf),
        out_shape=shapes + far,
        in_specs=[whole(x.shape) for x in ins] + [anywhere] * 2,
        out_specs=[whole(x.shape) for x in shapes] + [anywhere] * 3,
        scratch_shapes=[pltpu.VMEM((3 * flocal, total), F32), pltpu.VMEM((din, count), F32), pltpu.VMEM(w.shape, F32),
                        pltpu.VMEM((parts, ct.shape[0] // parts) + ct.shape[1:], F32)]
        + [pltpu.VMEM(x.shape, x.dtype) for x in far]
        + [dma((parts + 1,)), dma((3,))] + [dma((nf - 1,))] * 4 + [dma((nf - 1, nd // 2 - 1))] * 2 + [dma((nf - 1,))] * 2,
        compiler_params=params(collective_id=0, has_side_effects=True),
    )(*ins, w, ct)


def forward(nf, e, s, wp, so, bo, ct, sc):
    count, din = e.shape
    members, dout = so.shape
    rows, tiles, block = count * members, count // TILE, TILE * members
    lag = lambda i: jnp.maximum(i - 1, 0)
    big = pl.BlockSpec((TILE, members, dout), lambda i: (lag(i), 0, 0))
    nat = pl.BlockSpec((block, dout), lambda i: (lag(i), 0))
    tra = pl.BlockSpec((dout, block), lambda i: (0, lag(i)))
    return pl.pallas_call(
        functools.partial(forward_kernel, nf),
        out_shape=[jax.ShapeDtypeStruct((count, members, dout), F32)]
        + [jax.ShapeDtypeStruct((rows, dout), d) for d in (BF16, F8, F8)]
        + [jax.ShapeDtypeStruct((dout, rows), d) for d in (BF16, F8, F8)]
        + [jax.ShapeDtypeStruct((members, 2 * dout), F32)],
        grid=(tiles + 1,),
        in_specs=[pl.BlockSpec((TILE, din), lambda i: (0, 0)), pl.BlockSpec((TILE, din), lambda i: (jnp.minimum(i + 1, tiles - 1), 0)),
                  whole(s.shape)] + [pl.BlockSpec(memory_space=pl.ANY)] * 3 + [whole(so.shape), whole(bo.shape), big, whole(sc.shape)],
        out_specs=[big, nat, nat, nat, tra, tra, tra, whole((members, 2 * dout))],
        scratch_shapes=[pltpu.VMEM(so.shape, F32)] * 2 + [pltpu.VMEM(s.shape, F32), pltpu.VMEM(so.shape, F32), pltpu.VMEM(so.shape, F32)]
        + [pltpu.VMEM(w.shape, w.dtype) for w in wp] + [pltpu.SemaphoreType.DMA((3,))]
        + [pltpu.VMEM((block, din), d) for d in (BF16, F8, F8)] * 2
        + [pltpu.VMEM((block, dout), F32)] * 2,
        compiler_params=params(),
    )(e, e, s, *wp, so, bo, ct, sc)


def backward(nd, nf, e, s, zs, raw, t, wp, gp, gt, sc):
    count, din = e.shape
    members = s.shape[0]
    rows, dout = gp[0].shape
    step = rows // 16
    chunks, nchip = din // CHUNK, nd // 2
    per = chunks // nf
    ny, blk, half, sblk = nd // 4, CHUNK // nd // 2, 256 // 2, 256 // nd
    feats, flocal = CHUNK // 16, raw.shape[0] // (3 * nf)
    layout = (ny, 2, 2, blk, dout)
    shapes = [jax.ShapeDtypeStruct(x, F32) for x in ((2 * per,) + layout, (per, 256, 128), (nf, flocal, 128))]
    ins = (e, s, sc)
    far = (zs, raw, t, *wp, *gp, *gt)
    dma = pltpu.SemaphoreType.DMA
    f32 = lambda *shape: pltpu.VMEM(shape, F32)
    return pl.pallas_call(
        functools.partial(backward_kernel, nd, nf),
        out_shape=shapes,
        in_specs=[whole(x.shape) for x in ins] + [pl.BlockSpec(memory_space=pl.ANY)] * len(far),
        out_specs=[whole(x.shape) for x in shapes],
        scratch_shapes=[pltpu.VMEM(x.shape, x.dtype) for x in (zs, raw, t, *wp, gp[0])] + [pltpu.VMEM((rows, 2 * dout), F8)]
        + [pltpu.VMEM(x.shape, x.dtype) for x in gt] + [pltpu.VMEM((CHUNK, 2 * dout), F8)]
        + [f32(*s.shape)] * 2
        + [pltpu.VMEM((rows, CHUNK), d) for d in (BF16, F8, F8)] * 2
        + [f32(step, CHUNK)] * 2
        + [f32(count, CHUNK), f32(members, CHUNK), f32(CHUNK, count)]
        + [f32(2 * chunks, *layout), f32(chunks, 256, 128), f32(chunks, feats, count)]
        + [f32(chunks, *layout), f32(chunks, ny, blk, dout), f32(chunks, ny - 1, 2, blk, dout), f32(chunks, ny - 1, blk, dout),
           f32(chunks, blk, dout), f32(per, nf - 1, 2, blk, dout)]
        + [f32(chunks, half, 128), f32(chunks, nchip - 1, sblk, 128), f32(DIRECT, nd - 1, sblk, 128), f32(per, nf - 1, sblk, 128)]
        + [dma((12,))]
        + [dma((chunks,))] * 4 + [dma((chunks, ny - 1))] * 4 + [dma((chunks,))] * 2 + [dma((chunks,)), dma((per, nf - 1))]
        + [dma((per, nchip - 1))] * 2 + [dma((per,))] * 2 + [dma((chunks,)), dma((per, nf - 1))]
        + [dma((chunks,))] * 2 + [dma((chunks, nchip - 1))] * 2 + [dma((chunks,)), dma((per, nf - 1))]
        + [dma((per, nchip - 1))] * 2 + [dma((per,))] * 2
        + [dma((DIRECT, nd - 1))] * 4,
        compiler_params=params(collective_id=1, has_side_effects=True),
    )(*ins, *far)


def final(nf, bins, gw, sm, fr):
    per, flocal = sm.shape[0], fr.shape[1]
    members, width = 32, gw.shape[1] // nf
    shapes = [jax.ShapeDtypeStruct(x, F32) for x in (
        (flocal, nf * 128), (flocal, 16, bins), (16, flocal), (16, flocal), (members, per * CHUNK), gw.shape, (members, width), (members, width))]
    ins = (gw, sm, fr)
    return pl.pallas_call(functools.partial(final_kernel, nf, bins), out_shape=shapes,
                          in_specs=[whole(x.shape) for x in ins], out_specs=[whole(x.shape) for x in shapes],
                          compiler_params=params())(*ins)


def shards(nd, nf, bins, fractions, missing, bin_table, bin_bias, miss_vector, scale_in, weight, scale_out, bias_out, cotangent):
    raw, packed, e, sc, *wp = exchange(nd, nf, bins.T, fractions.T, missing.T, jnp.transpose(bin_table, (0, 2, 1)), bin_bias.T,
                                       miss_vector.T, scale_in, scale_out, weight, cotangent)
    hidden, *rest = forward(nf, e, scale_in, wp, scale_out, bias_out, cotangent, sc)
    gw, sm, fr = backward(nd, nf, e, scale_in, rest[6], raw, packed, wp, rest[:3], rest[3:6], sc)
    gw = gw.reshape(-1, weight.shape[1])
    frac, table, bias, miss, sin, gw, so, bo = final(nf, bin_table.shape[1], gw, sm, fr)
    return hidden, frac.T, jnp.transpose(table, (0, 2, 1)), bias.T, miss.T, sin, gw, so, bo


def solution(mesh):
    placed = (P("dp", "feat"), P("dp", "feat"), P("dp", "feat"), P("feat", None, None), P("feat", None), P("feat", None),
              P(), P(), P(), P(), P(("dp", "feat"), None, None))
    return jax.shard_map(
        functools.partial(shards, mesh.shape["dp"], mesh.shape["feat"]),
        mesh=mesh,
        in_specs=placed,
        out_specs=(P(("dp", "feat"), None, None), P("dp", "feat"), P("feat", None, None), P("feat", None), P("feat", None),
                   P(None, "feat"), P("feat", None), P(None, "feat"), P(None, "feat")),
        check_vma=False,
    )
```

```python
import functools

import jax
import jax.numpy as jnp
from jax import lax
from jax.experimental import pallas as pl
from jax.experimental.pallas import tpu as pltpu
from jax.sharding import PartitionSpec as P

F32, BF16, F8 = jnp.float32, jnp.bfloat16, jnp.float8_e4m3fn
VMEM_LIMIT = 63 << 20
TILE = 16
DIRECT = 2
CHUNK = 256
TOP = 224.0
TOP_WEIGHT = 400.0
LO = 256.0
GELU_A = 0.7978845608028654
GELU_B = GELU_A * 0.044715


def dot(a, b):
    return jnp.dot(a, b, preferred_element_type=F32)


def dot_nt(a, b):
    return lax.dot_general(a, b, (((1,), (1,)), ((), ())), preferred_element_type=F32)


def split3(x):
    hi = x.astype(BF16)
    return hi, hi.astype(F8), ((x - hi.astype(F32)).astype(BF16) * BF16(LO)).astype(F8)


def split2(x):
    hi = x.astype(BF16)
    return hi, (x - hi.astype(F32)).astype(BF16)


def split3_weight(x):
    hi = x.astype(BF16)
    return hi, (x * (1.0 / LO)).astype(F8), (x - hi.astype(F32)).astype(F8)


def encode_pair(raw_ref, flocal, first):
    level = lax.broadcasted_iota(jnp.int32, (48, 128), 0).astype(F32)
    row = lax.broadcasted_iota(jnp.int32, (16, 128), 0)
    high, low = [], []
    for f in (first, first + 1):
        b, fr, m = [raw_ref[pl.ds(f + k * flocal, 1), :] for k in range(3)]
        here = 1.0 - m
        rest = (fr - fr.astype(BF16).astype(F32)) * here
        high.append(jnp.clip((b - level) + fr, 0.0, 1.0) * here)
        high.append(jnp.where(row == 0, here, jnp.where(row == 1, m, 0.0)))
        low.append(jnp.where(level == b, rest, 0.0))
        low.append(jnp.zeros((16, 128), F32))
    return jnp.concatenate(high, axis=0).astype(BF16), jnp.concatenate(low, axis=0).astype(BF16)


def table_pair(t_ref, p):
    blk = t_ref[pl.ds(pl.multiple_of(p * 16, 16), 16), :]
    lane = lax.broadcasted_iota(jnp.int32, (16, 128), 1)
    zero = jnp.zeros_like(blk)
    return jnp.concatenate([jnp.where(lane < 64, blk, zero), jnp.where(lane < 64, zero, blk)], axis=0)


def send(src, dst, ssem, rsem, **where):
    return pltpu.make_async_remote_copy(src_ref=src, dst_ref=dst, send_sem=ssem, recv_sem=rsem, device_id=where,
                                        device_id_type=pl.DeviceIdType.MESH)


def greet(partners):
    barrier = pltpu.get_barrier_semaphore()
    for where in partners:
        pl.semaphore_signal(barrier, inc=1, device_id=where, device_id_type=pl.DeviceIdType.MESH)
    return lambda: pl.semaphore_wait(barrier, len(partners))


def exchange_kernel(nd, nf, bins_ref, fr_ref, ms_ref, tab_ref, bias_ref, miss_ref, s_ref, so_ref, w_in, ct_in,
                    raw_ref, t_ref, e_ref, sc_ref, wh_out, w8_out, wl_out,
                    mine, et, w, ct, wh, w8, wl, load, store, r_s, r_r, x_s, x_r, y_s, y_r, z_s, z_r):
    flocal, total = bins_ref.shape
    count = total // nf
    bins, width = tab_ref.shape[2], tab_ref.shape[1]
    me, z = lax.axis_index("dp"), lax.axis_index("feat")
    nchip = nd // 2
    core, chip = lax.rem(me, 2), me // 2
    partner = me + 1 - 2 * core
    parts = ct.shape[0]
    step = ct_in.shape[0] // parts

    ready = greet([{"feat": lax.rem(z + o, nf)} for o in range(1, nf)]
                  + [{"dp": 2 * lax.rem(chip + o, nchip) + core} for o in range(1, nchip)] + [{"dp": partner}])
    loads = [pltpu.make_async_copy(w_in, w, load.at[0])] + [
        pltpu.make_async_copy(ct_in.at[pl.ds(i * step, step)], ct.at[i], load.at[i + 1]) for i in range(parts)]
    for copy in loads:
        copy.start()

    def rows(q):
        return pl.ds(pl.multiple_of(q * (3 * flocal), 3 * flocal), 3 * flocal)

    size = flocal // 2 * width // nd

    def entries(q, piece, n):
        return t_ref.at[pl.ds(pl.multiple_of(q * (nd * size) + piece * size, 8), n * size)]

    mine[0:flocal, :] = bins_ref[...].astype(F32)
    mine[flocal:2 * flocal, :] = fr_ref[...]
    mine[2 * flocal:, :] = ms_ref[...].astype(F32)
    raw_ref[rows(z), :] = mine[:, pl.ds(pl.multiple_of(z * count, count), count)]
    blank = jnp.zeros((width, 64 - bins - 2), F32)
    for p in range(flocal // 2):
        block = []
        for f in (2 * p, 2 * p + 1):
            block += [tab_ref[f], bias_ref[:, f:f + 1], miss_ref[:, f:f + 1], blank]
        t_ref[pl.ds(pl.multiple_of(z * (flocal // 2 * width) + p * width, width), width), :] = jnp.concatenate(block, axis=1)

    def send_raw(o, q):
        to = lax.rem(z + o, nf)
        return send(mine.at[:, pl.ds(pl.multiple_of(to * count, count), count)], raw_ref.at[rows(q)],
                    r_s.at[o - 1], r_r.at[o - 1], feat=to)

    def send_x(o, q):
        r = entries(q, core * nchip + chip, 1)
        return send(r, r, x_s.at[o - 1], x_r.at[o - 1], feat=lax.rem(z + o, nf))

    def send_y(o, k, c):
        r = entries(lax.rem(z - o + nf, nf), core * nchip + c, 1)
        return send(r, r, y_s.at[o - 1, k - 1], y_r.at[o - 1, k - 1], dp=2 * lax.rem(chip + k, nchip) + core)

    def send_z(o, side):
        r = entries(lax.rem(z - o + nf, nf), side * nchip, nchip)
        return send(r, r, z_s.at[o - 1], z_r.at[o - 1], dp=partner)

    others = range(1, nf)
    ready()
    for o in others:
        send_x(o, z).start()
    for o in others:
        send_raw(o, z).start()

    def top(v):
        return jnp.maximum(jnp.max(jnp.max(jnp.abs(v), axis=0, keepdims=True), axis=1, keepdims=True), 1e-30)

    pairs = flocal // 2
    at_once = min(16, pairs)
    entries_local = flocal * width

    def embed(q):
        def body(j, c):
            for k in range(at_once):
                p = q * pairs + j * at_once + k
                first = q * (3 * flocal) + 2 * (j * at_once + k)
                lh, ll = split2(table_pair(t_ref, p))
                eh, el = encode_pair(raw_ref, flocal, first)
                both = dot(jnp.concatenate([lh, ll], axis=0), eh)
                et[pl.ds(pl.multiple_of(p * 32, 32), 32), :] = both[:32] + both[32:] + dot(lh, el)
            return c

        lax.fori_loop(0, pairs // at_once, body, 0)
        for j in range(entries_local // 128):
            at = pl.ds(pl.multiple_of(q * entries_local + j * 128, 128), 128)
            e_ref[:, at] = et[at, :].T

    embed(z)
    for o in others:
        send_x(o, lax.rem(z - o + nf, nf)).wait_recv()
        for k in range(1, nchip):
            send_y(o, k, chip).start()

    loads[0].wait()
    sw = TOP_WEIGHT / top(w[...])
    for i in range(0, w.shape[0], 256):
        r = slice(i, i + 256)
        wh[r, :], w8[r, :], wl[r, :] = split3_weight(w[r, :] * sw)
    stores = [pltpu.make_async_copy(i, o, store.at[k]) for k, (i, o) in enumerate(((wh, wh_out), (w8, w8_out), (wl, wl_out)))]
    for copy in stores:
        copy.start()

    for o in others:
        for k in range(1, nchip):
            send_y(o, k, lax.rem(chip - k + nchip, nchip)).wait_recv()
        send_z(o, core).start()
    tc = jnp.full((1, 1), 1e-30, F32)
    for i in range(parts):
        loads[i + 1].wait()
        tc = jnp.maximum(tc, top(ct[i].reshape(-1, ct.shape[-1])))
    for o in others:
        q = lax.rem(z - o + nf, nf)
        send_z(o, 1 - core).wait_recv()
        send_raw(o, q).wait_recv()
        embed(q)
    sx = TOP / jnp.maximum(top(et[...]) * top(s_ref[...]), 1e-30)
    sg = TOP / (1.2 * tc * top(so_ref[...]))
    for k, v in enumerate((sx, sw, sg, 1.0 / (sx * sw), 1.0 / (sx * sw), 1.0 / (sg * sx), 1.0 / (sg * sw), 1.0 / (sg * sw))):
        sc_ref[k:k + 1, :] = jnp.broadcast_to(v, (1, 128))
    for copy in stores:
        copy.wait()
    for o in others:
        send_raw(o, z).wait_send()
        send_x(o, z).wait_send()
        for k in range(1, nchip):
            send_y(o, k, chip).wait_send()
        send_z(o, core).wait_send()


def forward_kernel(nf, e0_ref, e_ref, s_ref, wh_in, w8_in, wl_in, so_ref, bo_ref, ct_ref, sc_ref,
                   hid_ref, gh_ref, g8_ref, gl_ref, th_ref, t8_ref, tl_ref, z_ref,
                   gs_ref, gb_ref, s1, so1, so2, wh_ref, w8_ref, wl_ref, load, xh0, x80, xl0, xh1, x81, xl1, pre0, pre1):
    i = pl.program_id(0)
    tiles = pl.num_programs(0) - 1
    members, width_out = so_ref.shape
    rows = TILE * members
    x = ((xh0, x80, xl0), (xh1, x81, xl1))
    pre = (pre0, pre1)

    def prepare(e, to):
        for n in range(TILE):
            v = s1[...] * e[n:n + 1, :]
            r = slice(n * members, (n + 1) * members)
            to[0][r, :], to[1][r, :], to[2][r, :] = split3(v)

    def multiply(a, to):
        to[...] = dot(a[0][...], wh_ref[...]) + (dot(a[1][...], wl_ref[...]) + dot(a[2][...], w8_ref[...]))

    def finish(p):
        for h0 in range(0, width_out, 128):
            hs = slice(h0, h0 + 128)
            sa, sb, bo = so1[:, hs], so2[:, hs], bo_ref[:, hs]
            gs, gb = gs_ref[:, hs], gb_ref[:, hs]
            for n in range(TILE):
                r = slice(n * members, (n + 1) * members)
                q = p[r, hs]
                v = q * sa + bo
                v2 = v * v
                half = 0.5 + 0.5 * jnp.tanh(v * (GELU_B * v2 + GELU_A))
                hid = v * half
                hid_ref[n, :, hs] = hid
                g = half + hid * (1.0 - half) * ((6.0 * GELU_B) * v2 + 2.0 * GELU_A)
                ga = ct_ref[n, :, hs] * g
                gs = gs + ga * q
                gb = gb + ga
                gh_ref[r, hs], g8_ref[r, hs], gl_ref[r, hs] = split3(ga * sb)
            gs_ref[:, hs], gb_ref[:, hs] = gs, gb
        th_ref[...] = gh_ref[...].T
        t8_ref[...] = g8_ref[...].T
        tl_ref[...] = gl_ref[...].T

    @pl.when(i == 0)
    def _():
        loads = [pltpu.make_async_copy(a, b, load.at[k]) for k, (a, b) in enumerate(
            ((wh_in, wh_ref), (w8_in, w8_ref), (wl_in, wl_ref)))]
        for copy in loads:
            copy.start()
        s1[...] = s_ref[...] * sc_ref[0:0 + 1, 0:1]
        so1[...] = so_ref[...] * sc_ref[3:3 + 1, 0:1]
        so2[...] = so_ref[...] * sc_ref[2:2 + 1, 0:1]
        gs_ref[...] = jnp.zeros_like(gs_ref)
        gb_ref[...] = jnp.zeros_like(gb_ref)
        prepare(e0_ref, x[0])
        for copy in loads:
            copy.wait()
        prepare(e_ref, x[1])
        multiply(x[0], pre[0])

    for par in (0, 1):
        @pl.when((i > 0) & (i < tiles) & (i % 2 == par))
        def _():
            prepare(e_ref, x[1 - par])
            finish(pre[1 - par])
            multiply(x[par], pre[par])

    @pl.when(i == tiles)
    def _():
        finish(pre[1])
        part = width_out // nf
        for o in range(nf):
            z_ref[:, 2 * o * part:(2 * o + 1) * part] = gs_ref[:, o * part:(o + 1) * part] * sc_ref[4:4 + 1, 0:1]
            z_ref[:, (2 * o + 1) * part:(2 * o + 2) * part] = gb_ref[:, o * part:(o + 1) * part]


def backward_kernel(nd, nf, e_ref, s_ref, sc_ref, z_in, raw_in, t_in, wh_in, w8_in, wl_in, gh_in, g8_in, gl_in,
                    th_in, t8_in, tl_in, gw_far, sm_out, fr_out,
                    gw_out, z_ref, raw_ref, t_ref, wh, w8, wl, gh, g8l, th, t8, tl, wcat, s1, s2, xh0, x80, xl0, xh1, x81, xl1, g0, g1, ge, gsin, et,
                    gw, sm, gf, ra, rp, rq, rp2, rq2, rc, ru, rb, r1, r2,
                    load, a_s, a_r, p_s, p_r, q_s, q_r, p2_s, p2_r, q2_s, q2_r, c_s, c_r, d_s, d_r, e_s, e_r, f_s, f_r,
                    ua_s, ua_r, ub_s, ub_r, uc_s, uc_r, ud_s, ud_r, ue_s, ue_r, u_s, u_r, y_s, y_r):
    members, width_in = s_ref.shape
    rows = gh.shape[0]
    count = e_ref.shape[0]
    chunks = width_in // CHUNK
    direct = chunks - DIRECT
    per = chunks // nf
    nx, ny, nchip = 2, nd // 4, nd // 2
    blk, dout = gw.shape[4], gw.shape[5]
    half, sblk = sm.shape[1] // 2, sm.shape[1] // nd
    feats = CHUNK // 16
    flocal = fr_out.shape[1]
    me, z = lax.axis_index("dp"), lax.axis_index("feat")
    core, chip = lax.rem(me, 2), me // 2
    cx, cy = lax.rem(chip, nx), chip // nx
    partner = me + 1 - 2 * core

    ready = greet([{"dp": lax.rem(me + o, nd)} for o in range(1, nd)] + [{"feat": lax.rem(z + o, nf)} for o in range(1, nf)])
    loads = [pltpu.make_async_copy(i, o, load.at[k]) for k, (i, o) in enumerate(
        ((th_in, th), (t8_in, t8), (tl_in, tl), (wh_in, wh), (w8_in, w8), (wl_in, wl), (gh_in, gh), (g8_in, g8l.at[:, :dout]), (gl_in, g8l.at[:, dout:]),
         (z_in, z_ref), (raw_in, raw_ref), (t_in, t_ref)))]
    for copy in loads[:3]:
        copy.start()

    def aligned(i, n):
        return pl.ds(pl.multiple_of(i, n), n)

    def owner(i):
        return lax.rem(i + nf // 2 + 1, nf)

    def place(i):
        return owner(i) * per + i // nf

    def far(i):
        return lax.rem(owner(i) - z + nf, nf)

    def device(y, x):
        return 2 * (y * nx + x) + core

    def other_y(k):
        return lax.rem(cy + k, ny)

    def from_y(k):
        return lax.rem(cy - k + ny, ny)

    def own(i):
        return 2 * place(i) + core

    def send_a(i):
        return send(gw.at[2 * place(i) + 1 - core], ra.at[i], a_s.at[i], a_r.at[i], dp=partner)

    def send_p(i):
        return send(gw.at[own(i), :, 1 - cx, 0], rp.at[i], p_s.at[i], p_r.at[i], dp=device(cy, 1 - cx))

    def send_q(i, k):
        return send(gw.at[own(i), other_y(k), :, 1], rq.at[i, k - 1], q_s.at[i, k - 1], q_r.at[i, k - 1], dp=device(other_y(k), cx))

    def send_p2(i, k):
        return send(gw.at[own(i), other_y(k), cx, 0], rp2.at[i, k - 1], p2_s.at[i, k - 1], p2_r.at[i, k - 1], dp=device(other_y(k), cx))

    def send_q2(i):
        return send(gw.at[own(i), cy, 1 - cx, 1], rq2.at[i], q2_s.at[i], q2_r.at[i], dp=device(cy, 1 - cx))

    def send_c(i, k):
        j = i // nf
        return send(gw.at[own(i), cy, cx], rc.at[j, k - 1], c_s.at[i], c_r.at[j, k - 1], feat=owner(i))

    def send_d(i, o, q):
        j = i // nf
        return send(gw.at[own(i), cy, cx], gw_out.at[2 * j + core, q // nx, lax.rem(q, nx)], d_s.at[j, o - 1], d_r.at[j, o - 1],
                    dp=2 * lax.rem(chip + o, nchip) + core)

    def send_e(i, side):
        j = i // nf
        return send(gw_out.at[2 * j + side], gw_out.at[2 * j + side], e_s.at[j], e_r.at[j], dp=partner)

    def step_b(i):
        send_a(i).wait_recv()
        gw[own(i)] += ra[i]
        send_p(i).start()
        for k in range(1, ny):
            send_q(i, k).start()

    def step_b2(i):
        send_p(i).wait_recv()
        gw[own(i), :, cx, 0] += rp[i]
        for k in range(1, ny):
            send_q(i, k).wait_recv()
            gw[own(i), cy, :, 1] += rq[i, k - 1]
        for k in range(1, ny):
            send_p2(i, k).start()
        send_q2(i).start()

    def step_c(i):
        send_q2(i).wait_recv()
        gw[own(i), cy, cx, 1] += rq2[i]
        for k in range(1, ny):
            send_p2(i, k).wait_recv()
            gw[own(i), cy, cx, 0] += rp2[i, k - 1]

        @pl.when(owner(i) != z)
        def _():
            send_c(i, far(i)).start()

    def step_d(i):
        @pl.when(owner(i) == z)
        def _():
            total = gw[own(i), cy, cx]
            for k in range(1, nf):
                send_c(i, k).wait_recv()
                total = total + rc[i // nf, k - 1]
            gw[own(i), cy, cx] = total
            gw_out[2 * (i // nf) + core, cy, cx] = total
            for o in range(1, nchip):
                send_d(i, o, chip).start()

    def step_e(i):
        @pl.when(owner(i) == z)
        def _():
            for o in range(1, nchip):
                send_d(i, o, lax.rem(chip - o + nchip, nchip)).wait_recv()
            send_e(i, core).start()

    def step_f(i):
        @pl.when(owner(i) == z)
        def _():
            send_e(i, 1 - core).wait_recv()

    def drain(i):
        send_a(i).wait_send()
        send_p(i).wait_send()
        send_q2(i).wait_send()
        for k in range(1, ny):
            send_q(i, k).wait_send()
            send_p2(i, k).wait_send()

        @pl.when(owner(i) != z)
        def _():
            send_c(i, far(i)).wait_send()

        @pl.when(owner(i) == z)
        def _():
            for o in range(1, nchip):
                send_d(i, o, chip).wait_send()
            send_e(i, core).wait_send()

    def rows_of(q, side):
        return aligned(side * half + q * sblk, sblk)

    def whole_half(side):
        return aligned(side * half, half)

    def send_ua(i):
        return send(sm.at[i, whole_half(1 - core)], ru.at[i], ua_s.at[i], ua_r.at[i], dp=partner)

    def send_ub(i, o):
        to = lax.rem(chip + o, nchip)
        return send(sm.at[i, rows_of(to, core)], rb.at[i, o - 1], ub_s.at[i, o - 1], ub_r.at[i, o - 1], dp=2 * to + core)

    def send_uc(i, k):
        j = i // nf
        return send(sm.at[i, rows_of(chip, core)], r2.at[j, k - 1], uc_s.at[i], uc_r.at[j, k - 1], feat=owner(i))

    def send_ud(i, o, q):
        j = i // nf
        return send(sm.at[i, rows_of(chip, core)], sm_out.at[j, rows_of(q, core)], ud_s.at[j, o - 1], ud_r.at[j, o - 1],
                    dp=2 * lax.rem(chip + o, nchip) + core)

    def send_ue(i, side):
        j = i // nf
        r = sm_out.at[j, whole_half(side)]
        return send(r, r, ue_s.at[j], ue_r.at[j], dp=partner)

    def send_u(i, o):
        to = lax.rem(me + o, nd)
        return send(sm.at[i, rows_of(to // 2, lax.rem(to, 2))], r1.at[i - direct, o - 1], u_s.at[i - direct, o - 1],
                    u_r.at[i - direct, o - 1], dp=to)

    def send_y(i, o, q):
        j = i - direct
        return send(sm.at[i, rows_of(chip, core)], sm_out.at[i // nf, rows_of(q // 2, lax.rem(q, 2))], y_s.at[j, o - 1], y_r.at[j, o - 1],
                    dp=lax.rem(me + o, nd))

    def send_f(i, k, src):
        j = i // nf
        return send(gf.at[i], fr_out.at[src, aligned(j * feats, feats)], f_s.at[i], f_r.at[j, k - 1], feat=owner(i))

    def start_f(i):
        @pl.when(owner(i) != z)
        def _():
            send_f(i, far(i), z).start()

        @pl.when(owner(i) == z)
        def _():
            fr_out[z, aligned((i // nf) * feats, feats), :] = gf[i]

    def wait_f(i):
        @pl.when(owner(i) == z)
        def _():
            for k in range(1, nf):
                send_f(i, k, lax.rem(z - k + nf, nf)).wait_recv()

    def start_ua(i):
        send_ua(i).start()
        start_f(i)

    def step_ub(i):
        send_ua(i).wait_recv()
        sm[i, whole_half(core), :] += ru[i]
        for o in range(1, nchip):
            send_ub(i, o).start()

    def step_uc(i):
        r = rows_of(chip, core)
        total = sm[i, r, :]
        for o in range(1, nchip):
            send_ub(i, o).wait_recv()
            total = total + rb[i, o - 1]
        sm[i, r, :] = total

        @pl.when(owner(i) != z)
        def _():
            send_uc(i, far(i)).start()

    def gather_z(i):
        r = rows_of(chip, core)
        total = sm[i, r, :]
        for k in range(1, nf):
            send_uc(i, k).wait_recv()
            total = total + r2[i // nf, k - 1]
        sm[i, r, :] = total
        sm_out[i // nf, r, :] = total

    def step_ud(i):
        @pl.when(owner(i) == z)
        def _():
            gather_z(i)
            for o in range(1, nchip):
                send_ud(i, o, chip).start()

    def step_ue(i):
        @pl.when(owner(i) == z)
        def _():
            for o in range(1, nchip):
                send_ud(i, o, lax.rem(chip - o + nchip, nchip)).wait_recv()
            send_ue(i, core).start()

    def step_uf(i):
        @pl.when(owner(i) == z)
        def _():
            send_ue(i, 1 - core).wait_recv()

        wait_f(i)

    def drain_small(i):
        send_ua(i).wait_send()
        for o in range(1, nchip):
            send_ub(i, o).wait_send()

        @pl.when(owner(i) != z)
        def _():
            send_uc(i, far(i)).wait_send()
            send_f(i, far(i), z).wait_send()

        @pl.when(owner(i) == z)
        def _():
            for o in range(1, nchip):
                send_ud(i, o, chip).wait_send()
            send_ue(i, core).wait_send()

    def start_u(i):
        for o in range(1, nd):
            send_u(i, o).start()

    def step_v(i):
        r = rows_of(chip, core)
        total = sm[i, r, :]
        for o in range(1, nd):
            send_u(i, o).wait_recv()
            total = total + r1[i - direct, o - 1]
        sm[i, r, :] = total

        @pl.when(owner(i) != z)
        def _():
            send_uc(i, far(i)).start()

    def step_y(i):
        @pl.when(owner(i) == z)
        def _():
            gather_z(i)
            for o in range(1, nd):
                send_y(i, o, me).start()

    def step_w(i):
        @pl.when(owner(i) == z)
        def _():
            for o in range(1, nd):
                send_y(i, o, lax.rem(me - o + nd, nd)).wait_recv()

        wait_f(i)

    def drain_direct(i):
        for o in range(1, nd):
            send_u(i, o).wait_send()

        @pl.when(owner(i) != z)
        def _():
            send_uc(i, far(i)).wait_send()
            send_f(i, far(i), z).wait_send()

        @pl.when(owner(i) == z)
        def _():
            for o in range(1, nd):
                send_y(i, o, me).wait_send()

    def when_chunk(i, f, first=0, end=chunks):
        @pl.when((i >= first) & (i < end))
        def _():
            f(i)

    start_a = lambda i: send_a(i).start()
    stages = ((start_a, (0, 1, 2, 3)), (step_b, (1, 2, 3, 4)), (step_b2, (3, 4, 5, 6)), (step_c, (5, 6, 7, 8)),
              (step_d, (7, 8, 9, 10)), (step_e, (9, 10, 11)))

    def pairs(k, among):
        for step, times in stages:
            for j, at in enumerate(times):
                if at in among:
                    @pl.when(k == at)
                    def _():
                        for i in (2 * j, 2 * j + 1):
                            step(i)

    def early(j):
        @pl.when(j == 0)
        def _():
            ready()

        pairs(j, range(4))

    def late(t):
        when_chunk(t - 1, start_ua, 0, direct)
        when_chunk(t - 1, start_u, direct)
        when_chunk(t - 1, start_f, direct)
        pairs(t + 4, range(4, 12))
        when_chunk(t - 2, step_ub, 0, direct)
        when_chunk(t - 4, step_uc, 0, direct)
        when_chunk(t - 6, step_ud, 0, direct)

    x = ((xh0, x80, xl0), (xh1, x81, xl1))
    s1[...] = s_ref[...] * sc_ref[0:0 + 1, 0:1]
    s2[...] = s_ref[...] * sc_ref[6:6 + 1, 0:1]

    def cols(i):
        return aligned(place(i) * CHUNK, CHUNK)

    def prepare(i, to):
        for n in range(0, count, TILE):
            v = (e_ref[n:n + TILE, cols(i)][:, None, :] * s1[:, cols(i)][None]).reshape(TILE * members, CHUNK)
            r = slice(n * members, (n + TILE) * members)
            to[0][r, :], to[1][r, :], to[2][r, :] = split3(v)

    prepare(0, x[0])
    for copy in loads[:3]:
        copy.wait()
    for copy in loads[3:]:
        copy.start()

    def weights(j, carry):
        for par in (0, 1):
            i = 2 * j + par
            xh, x8, xl = x[par]
            r = dot(th[...], xh[...]) + (dot(t8[...], xl[...]) + dot(tl[...], x8[...])) * (1.0 / LO)
            gw[aligned(2 * place(i), 2)] = (r.T * sc_ref[5:5 + 1, 0:1]).reshape(2, ny, nx, 2, blk, dout)
            prepare(jnp.minimum(i + 1, chunks - 1), x[1 - par])
        early(j)
        return carry

    lax.fori_loop(0, chunks // 2, weights, 0)

    for copy in loads[3:]:
        copy.wait()
    gsin[...] = jnp.zeros_like(gsin)
    g1[...] = jnp.zeros_like(g1)
    step = g0.shape[0]
    objs = step // members
    parts = rows // step

    def finish(i, t, g):
        g3 = g[...].reshape(objs, members, CHUNK)
        ns = slice(t * objs, (t + 1) * objs)
        ge[ns, :] = jnp.sum(g3 * s2[:, cols(i)][None], axis=1)
        gsin[...] += jnp.sum(g3 * e_ref[ns, cols(i)][:, None, :], axis=0)

    def table(i):
        c = place(i)
        first = c * feats
        base = (first // flocal) * (3 * flocal) + lax.rem(first, flocal)
        for j in range(CHUNK // 128):
            et[j * 128:(j + 1) * 128, :] = ge[:, j * 128:(j + 1) * 128].T
        lane = lax.broadcasted_iota(jnp.int32, (16, 128), 1)
        for p in range(feats // 2):
            row = base + 2 * p
            eh, el = encode_pair(raw_ref, flocal, row)
            gh_, gl_ = split2(et[p * 32:(p + 1) * 32, :])
            both = dot_nt(jnp.concatenate([gh_, gl_], axis=0), eh)
            full = both[:32] + both[32:] + dot_nt(gh_, el)
            sm[i, p * 16:(p + 1) * 16, :] = jnp.where(lane < 64, full[:16], full[16:])
        at = feats * 8
        for j in range(CHUNK // 128):
            sm[i, at:at + members, :] = gsin[:, j * 128:(j + 1) * 128] * sc_ref[7:7 + 1, 0:1]
            at += members
        sm[i, at:at + members, :] = z_ref[:, aligned(c * 128, 128)]
        at += members
        sm[i, at:, :] = jnp.zeros_like(sm[i, at:, :])
        gsin[...] = jnp.zeros_like(gsin)

    def slopes(i):
        c = place(i)
        first = c * feats
        base = (first // flocal) * (3 * flocal) + lax.rem(first, flocal)
        level = lax.broadcasted_iota(jnp.int32, (64, 128), 0).astype(F32)
        for p in range(feats // 2):
            row = base + 2 * p
            lh, ll = split2(table_pair(t_ref, c * (feats // 2) + p))
            g = et[p * 32:(p + 1) * 32, :]
            hot = []
            for f in (row, row + 1):
                here = 1.0 - raw_ref[pl.ds(f + 2 * flocal, 1), :]
                hot.append(jnp.where(level == raw_ref[pl.ds(f, 1), :], here, 0.0))
            one = jnp.concatenate(hot, axis=0).astype(BF16)
            both = dot(jnp.concatenate([lh, ll], axis=0), one)
            picked = (both[:32] + both[32:]) * g
            gf[i, 2 * p:2 * p + 1, :] = jnp.sum(picked[:16], axis=0, keepdims=True)
            gf[i, 2 * p + 1:2 * p + 2, :] = jnp.sum(picked[16:], axis=0, keepdims=True)

    def inputs(i, carry):
        before = jnp.maximum(i - 1, 0)
        wc = wh[cols(i), :]
        wcat[:, :dout] = wl[cols(i), :]
        wcat[:, dout:] = w8[cols(i), :]
        finish(before, parts - 1, g1)
        table(before)
        slopes(before)
        for t in range(parts):
            to, fro = (g0, g1) if t % 2 == 0 else (g1, g0)
            rs = slice(t * step, (t + 1) * step)
            to[...] = dot_nt(gh[rs, :], wc) + dot_nt(g8l[rs, :], wcat[...])
            if t > 0:
                finish(i, t - 1, fro)
        late(i)
        return carry

    lax.fori_loop(0, chunks, inputs, 0)
    last = chunks - 1
    finish(last, parts - 1, g1)
    table(last)
    start_u(last)
    slopes(last)
    start_f(last)
    for i in range(direct - 4):
        step_ue(i)
    for i in range(direct - 4, direct - 2):
        step_ud(i)
    step_e(last - 1)
    step_e(last)
    for i in range(direct - 2, direct):
        step_uc(i)
    step_v(last - 1)
    step_v(last)
    for i in range(direct - 4, direct - 2):
        step_ue(i)
    for i in range(direct - 2, direct):
        step_ud(i)
    step_y(last - 1)
    step_y(last)
    for i in range(direct - 2, direct):
        step_ue(i)
    for i in range(chunks):
        step_f(i)
    leave = pltpu.make_async_copy(gw_out, gw_far, load.at[12])
    leave.start()
    for i in range(direct):
        step_uf(i)
    step_w(last - 1)

    def close(i, carry):
        drain(i)
        when_chunk(i, drain_small, 0, direct)
        when_chunk(i, drain_direct, direct)
        return carry

    lax.fori_loop(0, chunks, close, 0)
    leave.wait()
    step_w(last)


def final_kernel(nf, bins, gw_in, sm_ref, fr_ref, frac_ref, tab_ref, bias_ref, miss_ref, sin_ref, gw_out, so_ref, bo_ref):
    gw_out[...] = gw_in[...]
    flocal = fr_ref.shape[1]
    for o in range(nf):
        frac_ref[:, o * 128:(o + 1) * 128] = fr_ref[o]
    members = sin_ref.shape[0]
    feats = CHUNK // 16
    width = so_ref.shape[1]
    small = []
    for j in range(sm_ref.shape[0]):
        for p in range(feats // 2):
            block = sm_ref[j, p * 16:(p + 1) * 16, :]
            for odd in (0, 1):
                f = j * feats + 2 * p + odd
                tab_ref[f] = block[:, odd * 64:odd * 64 + bins]
                bias_ref[:, f:f + 1] = block[:, odd * 64 + bins:odd * 64 + bins + 1]
                miss_ref[:, f:f + 1] = block[:, odd * 64 + bins + 1:odd * 64 + bins + 2]
        at = feats * 8
        for q in range(CHUNK // 128):
            sin_ref[:, j * CHUNK + q * 128:j * CHUNK + (q + 1) * 128] = sm_ref[j, at:at + members, :]
            at += members
        small.append(sm_ref[j, at:at + members, :])
    small = small[0] if len(small) == 1 else jnp.concatenate(small, axis=1)
    so_ref[...] = small[:, :width]
    bo_ref[...] = small[:, width:]


def params(**kw):
    return pltpu.CompilerParams(vmem_limit_bytes=VMEM_LIMIT, **kw)


def whole(shape):
    return pl.BlockSpec(shape, lambda *_: (0,) * len(shape))


def exchange(nd, nf, bins, fr, ms, tab, bias, miss, s, so, w, ct):
    flocal, total = bins.shape
    width = tab.shape[1]
    count, (din, dout) = total // nf, w.shape
    parts = 8
    ins = (bins, fr, ms, tab, bias, miss, s, so)
    shapes = [jax.ShapeDtypeStruct(x, F32) for x in ((nf * 3 * flocal, count), (nf * flocal // 2 * width, 128), (count, din), (8, 128))]
    far = [jax.ShapeDtypeStruct(w.shape, d) for d in (BF16, F8, F8)]
    dma = pltpu.SemaphoreType.DMA
    anywhere = pl.BlockSpec(memory_space=pl.ANY)
    return pl.pallas_call(
        functools.partial(exchange_kernel, nd, nf),
        out_shape=shapes + far,
        in_specs=[whole(x.shape) for x in ins] + [anywhere] * 2,
        out_specs=[whole(x.shape) for x in shapes] + [anywhere] * 3,
        scratch_shapes=[pltpu.VMEM((3 * flocal, total), F32), pltpu.VMEM((din, count), F32), pltpu.VMEM(w.shape, F32),
                        pltpu.VMEM((parts, ct.shape[0] // parts) + ct.shape[1:], F32)]
        + [pltpu.VMEM(x.shape, x.dtype) for x in far]
        + [dma((parts + 1,)), dma((3,))] + [dma((nf - 1,))] * 4 + [dma((nf - 1, nd // 2 - 1))] * 2 + [dma((nf - 1,))] * 2,
        compiler_params=params(collective_id=0, has_side_effects=True),
    )(*ins, w, ct)


def forward(nf, e, s, wp, so, bo, ct, sc):
    count, din = e.shape
    members, dout = so.shape
    rows, tiles, block = count * members, count // TILE, TILE * members
    lag = lambda i: jnp.maximum(i - 1, 0)
    big = pl.BlockSpec((TILE, members, dout), lambda i: (lag(i), 0, 0))
    nat = pl.BlockSpec((block, dout), lambda i: (lag(i), 0))
    tra = pl.BlockSpec((dout, block), lambda i: (0, lag(i)))
    return pl.pallas_call(
        functools.partial(forward_kernel, nf),
        out_shape=[jax.ShapeDtypeStruct((count, members, dout), F32)]
        + [jax.ShapeDtypeStruct((rows, dout), d) for d in (BF16, F8, F8)]
        + [jax.ShapeDtypeStruct((dout, rows), d) for d in (BF16, F8, F8)]
        + [jax.ShapeDtypeStruct((members, 2 * dout), F32)],
        grid=(tiles + 1,),
        in_specs=[pl.BlockSpec((TILE, din), lambda i: (0, 0)), pl.BlockSpec((TILE, din), lambda i: (jnp.minimum(i + 1, tiles - 1), 0)),
                  whole(s.shape)] + [pl.BlockSpec(memory_space=pl.ANY)] * 3 + [whole(so.shape), whole(bo.shape), big, whole(sc.shape)],
        out_specs=[big, nat, nat, nat, tra, tra, tra, whole((members, 2 * dout))],
        scratch_shapes=[pltpu.VMEM(so.shape, F32)] * 2 + [pltpu.VMEM(s.shape, F32), pltpu.VMEM(so.shape, F32), pltpu.VMEM(so.shape, F32)]
        + [pltpu.VMEM(w.shape, w.dtype) for w in wp] + [pltpu.SemaphoreType.DMA((3,))]
        + [pltpu.VMEM((block, din), d) for d in (BF16, F8, F8)] * 2
        + [pltpu.VMEM((block, dout), F32)] * 2,
        compiler_params=params(),
    )(e, e, s, *wp, so, bo, ct, sc)


def backward(nd, nf, e, s, zs, raw, t, wp, gp, gt, sc):
    count, din = e.shape
    members = s.shape[0]
    rows, dout = gp[0].shape
    step = rows // 16
    chunks, nchip = din // CHUNK, nd // 2
    per = chunks // nf
    ny, blk, half, sblk = nd // 4, CHUNK // nd // 2, 256 // 2, 256 // nd
    feats, flocal = CHUNK // 16, raw.shape[0] // (3 * nf)
    layout = (ny, 2, 2, blk, dout)
    shapes = [jax.ShapeDtypeStruct(x, F32) for x in ((2 * per,) + layout, (per, 256, 128), (nf, flocal, 128))]
    ins = (e, s, sc)
    far = (zs, raw, t, *wp, *gp, *gt)
    dma = pltpu.SemaphoreType.DMA
    f32 = lambda *shape: pltpu.VMEM(shape, F32)
    return pl.pallas_call(
        functools.partial(backward_kernel, nd, nf),
        out_shape=shapes,
        in_specs=[whole(x.shape) for x in ins] + [pl.BlockSpec(memory_space=pl.ANY)] * len(far),
        out_specs=[pl.BlockSpec(memory_space=pl.ANY)] + [whole(x.shape) for x in shapes[1:]],
        scratch_shapes=[pltpu.VMEM(x.shape, x.dtype) for x in (shapes[0], zs, raw, t, *wp, gp[0])] + [pltpu.VMEM((rows, 2 * dout), F8)]
        + [pltpu.VMEM(x.shape, x.dtype) for x in gt] + [pltpu.VMEM((CHUNK, 2 * dout), F8)]
        + [f32(*s.shape)] * 2
        + [pltpu.VMEM((rows, CHUNK), d) for d in (BF16, F8, F8)] * 2
        + [f32(step, CHUNK)] * 2
        + [f32(count, CHUNK), f32(members, CHUNK), f32(CHUNK, count)]
        + [f32(2 * chunks, *layout), f32(chunks, 256, 128), f32(chunks, feats, count)]
        + [f32(chunks, *layout), f32(chunks, ny, blk, dout), f32(chunks, ny - 1, 2, blk, dout), f32(chunks, ny - 1, blk, dout),
           f32(chunks, blk, dout), f32(per, nf - 1, 2, blk, dout)]
        + [f32(chunks, half, 128), f32(chunks, nchip - 1, sblk, 128), f32(DIRECT, nd - 1, sblk, 128), f32(per, nf - 1, sblk, 128)]
        + [dma((13,))]
        + [dma((chunks,))] * 4 + [dma((chunks, ny - 1))] * 4 + [dma((chunks,))] * 2 + [dma((chunks,)), dma((per, nf - 1))]
        + [dma((per, nchip - 1))] * 2 + [dma((per,))] * 2 + [dma((chunks,)), dma((per, nf - 1))]
        + [dma((chunks,))] * 2 + [dma((chunks, nchip - 1))] * 2 + [dma((chunks,)), dma((per, nf - 1))]
        + [dma((per, nchip - 1))] * 2 + [dma((per,))] * 2
        + [dma((DIRECT, nd - 1))] * 4,
        compiler_params=params(collective_id=1, has_side_effects=True),
    )(*ins, *far)


def final(nf, bins, gw, sm, fr):
    per, flocal = sm.shape[0], fr.shape[1]
    members, width = 32, gw.shape[1] // nf
    shapes = [jax.ShapeDtypeStruct(x, F32) for x in (
        (flocal, nf * 128), (flocal, 16, bins), (16, flocal), (16, flocal), (members, per * CHUNK), gw.shape, (members, width), (members, width))]
    ins = (gw, sm, fr)
    return pl.pallas_call(functools.partial(final_kernel, nf, bins), out_shape=shapes,
                          in_specs=[whole(x.shape) for x in ins], out_specs=[whole(x.shape) for x in shapes],
                          compiler_params=params())(*ins)


def shards(nd, nf, bins, fractions, missing, bin_table, bin_bias, miss_vector, scale_in, weight, scale_out, bias_out, cotangent):
    raw, packed, e, sc, *wp = exchange(nd, nf, bins.T, fractions.T, missing.T, jnp.transpose(bin_table, (0, 2, 1)), bin_bias.T,
                                       miss_vector.T, scale_in, scale_out, weight, cotangent)
    hidden, *rest = forward(nf, e, scale_in, wp, scale_out, bias_out, cotangent, sc)
    gw, sm, fr = backward(nd, nf, e, scale_in, rest[6], raw, packed, wp, rest[:3], rest[3:6], sc)
    gw = gw.reshape(-1, weight.shape[1])
    frac, table, bias, miss, sin, gw, so, bo = final(nf, bin_table.shape[1], gw, sm, fr)
    return hidden, frac.T, jnp.transpose(table, (0, 2, 1)), bias.T, miss.T, sin, gw, so, bo


def solution(mesh):
    placed = (P("dp", "feat"), P("dp", "feat"), P("dp", "feat"), P("feat", None, None), P("feat", None), P("feat", None),
              P(), P(), P(), P(), P(("dp", "feat"), None, None))
    return jax.shard_map(
        functools.partial(shards, mesh.shape["dp"], mesh.shape["feat"]),
        mesh=mesh,
        in_specs=placed,
        out_specs=(P(("dp", "feat"), None, None), P("dp", "feat"), P("feat", None, None), P("feat", None), P("feat", None),
                   P(None, "feat"), P("feat", None), P(None, "feat"), P(None, "feat")),
        check_vma=False,
    )
```
